32 devices in a mesh: grp: 4 (over z), shard: 8 (over y, x, core).
Axes of the slice: x: 2, y: 2, z: 4, core: 2. Of those that a mesh axis runs over, the one named last changes fastest.
Arguments:
- patches: bfloat16 [8192, 16], P(('grp', 'shard')), may hold values from -6 to 6
- noise: float32 [8192, 16], P(('grp', 'shard')), may hold values from -6 to 6
- timesteps: int32 [32], P(('grp', 'shard')), may hold values from 0 to 999
- labels: int32 [32], P(('grp', 'shard')), may hold values from 0 to 999
- assign: int32 [288], replicated, may hold values from 0 to 287, each once
- tile_master: float32 [288, 256, 256], P('shard'), may hold values from -0.1875 to 0.1875
- tile_bases: float32 [288, 2, 256, 256], P('shard'), may hold values from -1 to 1, as said below
- tile_moment: float32 [288, 256, 256], P('shard'), may hold values from -0.0007324219 to 0.0007324219
- tile_second: float32 [288, 256, 256], P('shard'), may hold values from 3e-10 to 1e-08
- row_master: float32 [4379, 1024], P(None, 'shard'), may hold values from -1.5 to 1.5
- row_moment: float32 [4379, 1024], P(None, 'shard'), may hold values from -0.0007324219 to 0.0007324219
- row_second: float32 [4379, 1024], P(None, 'shard'), may hold values from 3e-10 to 1e-08
Outputs:
- loss: float32 [], replicated
- grad_norm: float32 [], replicated
- act_rms: float32 [3], replicated
- new_tile_moment: float32 [288, 256, 256], P('shard')
- new_tile_second: float32 [288, 256, 256], P('shard')
- tile_update: float32 [288, 256, 256], P('shard')
- new_row_moment: float32 [4379, 1024], P(None, 'shard')
- new_row_second: float32 [4379, 1024], P(None, 'shard')
- row_update: float32 [4379, 1024], P(None, 'shard')
The draws below stay inside these ranges and needn't reach their ends.
Inputs may be any that keep to these rules, and one draw needn't show every extreme that they name: assign is a permutation: each block stands in exactly one slot; slot s belongs to the owner s // 36. tile_bases[s, 0] and tile_bases[s, 1] are orthogonal matrices.
All inputs are finite; a program needn't handle non-finite values.
Results may differ from the reference program's by a relative error of at most 0.018.
Values may be sent and summed in bfloat16 or wider, within the bound.
A program may use at most 448 MiB of HBM per device.

```python
import math
import jax
import jax.numpy as jnp
from jax import lax

D = 1024
HEADS = 16
HD = 64
FF = 4096
NCLASS = 1000
FREQ = 256
PATCH_SIDE = 2
LAT = 32
BLK = 256
PATCH_DIM = 16
SEQ = 256
IMAGES = 32
TOKENS = 8192
TILES = 288
ROWS = 4379


def draw_tile_bases(key, part):
    normal_draw = jax.random.normal(key, (TILES * 2, BLK, BLK), jnp.float32)
    basis, upper = jnp.linalg.qr(normal_draw)
    diagonal = jnp.diagonal(upper, axis1=1, axis2=2)
    signs = jnp.where(diagonal < 0.0, -1.0, 1.0)
    return (basis * signs[:, None, :]).reshape(TILES, 2, BLK, BLK)


def draw_row_master(key, part):
    row_scale = jnp.concatenate([jnp.full((NCLASS,), 0.5, jnp.float32), jnp.full((FREQ,), FREQ ** (-0.5), jnp.float32), jnp.full((3 * D,), D ** (-0.5), jnp.float32), jnp.full((PATCH_DIM,), PATCH_DIM ** (-0.5), jnp.float32), jnp.full((PATCH_DIM,), D ** (-0.5), jnp.float32), jnp.full((15 + FF // D,), 0.2, jnp.float32)])
    normal_draw = jax.random.truncated_normal(key, -3.0, 3.0, (ROWS, D), jnp.float32)
    return normal_draw * row_scale[:, None]


def place_ends(values, stream_key, low, largest):
    extent = values.shape
    place = [jax.random.randint(jax.random.fold_in(stream_key, axis), (), 0, extent[axis]) for axis in range(len(extent))]
    values = values.at[tuple(place)].set(low)
    longest = extent.index(max(extent))
    place[longest] = (place[longest] + 1) % extent[longest]
    return values.at[tuple(place)].set(largest)


def block_levels(rng, extent, cuts, smallest, high):
    loudness = 1.0
    for axis_at, blocks in cuts:
        draws = jax.random.uniform(jax.random.fold_in(jax.random.fold_in(rng, 6), axis_at), (blocks,), jnp.float32, smallest / len(cuts), high / len(cuts))
        loudness = loudness * jnp.repeat(jnp.exp(draws), extent[axis_at] // blocks).reshape((-1,) + (1,) * (len(extent) - 1 - axis_at))
    return loudness


def normal_values(key, extent, scale, bound, cuts=(), held_as=jnp.bfloat16):
    gain = block_levels(key, extent, cuts, -0.22, 0.18) if cuts else 1.0
    values = jax.random.normal(key, extent, jnp.float32) * scale * gain
    return jnp.minimum(jnp.maximum(values, -bound), bound).astype(held_as)


def setup_inputs(seed: int = 0) -> dict:
    key_of = jax.random.split(jax.random.key(seed), 13)
    return {
        "patches": normal_values(key_of[0], (TOKENS, PATCH_DIM), 1.0, 6.0, ((0, 32),)),
        "noise": normal_values(key_of[1], (TOKENS, PATCH_DIM), 1.0, 6.0, ((0, 32),), jnp.float32),
        "timesteps": place_ends(jax.random.randint(key_of[2], (IMAGES,), 0, 1000), jax.random.fold_in(key_of[2], 1), 0, 999).astype(jnp.int32),
        "labels": place_ends(jax.random.randint(key_of[3], (IMAGES,), 0, NCLASS), jax.random.fold_in(key_of[3], 1), 0, NCLASS - 1).astype(jnp.int32),
        "assign": jax.random.permutation(key_of[4], TILES).astype(jnp.int32),
        "tile_master": normal_values(key_of[5], (TILES, BLK, BLK), D ** -0.5, 0.1875, ((0, 8),), jnp.float32),
        "tile_bases": draw_tile_bases(jax.random.fold_in(key_of[12], 71), 0),
        "tile_moment": normal_values(key_of[7], (TILES, BLK, BLK), 0.00005, 0.0007324219, ((0, 8),), jnp.float32),
        "tile_second": jnp.clip(jnp.exp(math.log(9.99999993922529e-09) - 3.506558 * jax.random.uniform(key_of[8], (TILES, BLK, BLK), jnp.float32) ** block_levels(key_of[8], (TILES, BLK, BLK), ((0, 8),), -0.2, 0.2)), 2.999999970665357e-10, 9.99999993922529e-09),
        "row_master": draw_row_master(jax.random.fold_in(key_of[12], 71), 0),
        "row_moment": normal_values(key_of[10], (ROWS, D), 0.00005, 0.0007324219, ((1, 8),), jnp.float32),
        "row_second": jnp.clip(jnp.exp(math.log(9.99999993922529e-09) - 3.506558 * jax.random.uniform(key_of[11], (ROWS, D), jnp.float32) ** block_levels(key_of[11], (ROWS, D), ((1, 8),), -0.2, 0.2)), 2.999999970665357e-10, 9.99999993922529e-09),
    }


highest = lax.Precision.HIGHEST
ln_eps = 1e-06
beta_one = 0.5
beta_two = 0.5
adam_eps = 1e-08
rate_step = 0.01
decay_rate = 0.1
clip_at = 0.25

@jax.custom_vjp
def low(v):
    return lax.optimization_barrier(v.astype(jnp.bfloat16)).astype(jnp.float32)

@jax.custom_vjp
def low_back(v):
    return v

def low_keep(v):
    return (low(v), None)

def low_pass(kept, grad):
    return (grad,)

def back_keep(v):
    return (v, None)

def back_low(kept, grad):
    return (low(grad),)
low.defvjp(low_keep, low_pass)
low_back.defvjp(back_keep, back_low)

def matmul(left_in, right_in):
    return jnp.dot(left_in, right_in, precision=highest)

def untile(block, row_count, col_count, tile_edge):
    shaped = block.reshape(row_count // tile_edge, col_count // tile_edge, tile_edge, tile_edge)
    return shaped.transpose(0, 2, 1, 3).reshape(row_count, col_count)

def matrix_shapes(model_width, hidden_width):
    return [(model_width, 6 * model_width), (model_width, 3 * model_width), (model_width, model_width), (model_width, hidden_width), (hidden_width, model_width)]

def split_matrices(tiles, model_width, hidden_width, tile_edge):
    result = []
    offset = 0
    for row_count, col_count in matrix_shapes(model_width, hidden_width):
        tile_count = row_count // tile_edge * (col_count // tile_edge)
        result.append(untile(tiles[offset:offset + tile_count], row_count, col_count, tile_edge))
        offset += tile_count
    return result

def split_rows(row_block, model_width, hidden_width, class_count, freq_width, patch_width):
    sizes_list = [class_count, freq_width, model_width, 2 * model_width, patch_width, patch_width, 1, 1, 1, 1, 1, 1, 1, 6, hidden_width // model_width, 2]
    pieces = []
    offset = 0
    for row_count in sizes_list:
        pieces.append(row_block[offset:offset + row_count])
        offset += row_count
    final_rows = pieces[3]
    w_final = jnp.concatenate([final_rows[:model_width], final_rows[model_width:]], axis=1)
    vectors = [piece.reshape(-1) for piece in pieces[6:]]
    return [pieces[0], pieces[1], pieces[2], w_final, pieces[4], pieces[5]] + vectors

def positions(grid_side, model_width):
    index = jnp.arange(grid_side * grid_side)
    row_pos = (index // grid_side).astype(jnp.float32)
    col_pos = (index % grid_side).astype(jnp.float32)
    quarter = model_width // 4
    omega = 1.0 / 10000.0 ** (jnp.arange(quarter, dtype=jnp.float32) / quarter)
    row_arg = row_pos[:, None] * omega[None, :]
    col_arg = col_pos[:, None] * omega[None, :]
    return jnp.concatenate([jnp.sin(row_arg), jnp.cos(row_arg), jnp.sin(col_arg), jnp.cos(col_arg)], axis=1)

def time_freq(step_values, freq_width):
    half_width = freq_width // 2
    freqs = jnp.exp(-math.log(10000.0) * jnp.arange(half_width, dtype=jnp.float32) / half_width)
    angle_arg = step_values.astype(jnp.float32)[:, None] * freqs[None, :]
    return jnp.concatenate([jnp.cos(angle_arg), jnp.sin(angle_arg)], axis=1)

def layer_norm(hidden_in):
    centred = hidden_in - lax.optimization_barrier(jnp.mean(hidden_in, axis=-1, keepdims=True))
    spread = lax.optimization_barrier(jnp.mean(centred * centred, axis=-1, keepdims=True))
    return centred * lax.rsqrt(spread + ln_eps)

def modulate(hidden_in, scale_row, shift_row):
    return layer_norm(hidden_in) * (1.0 + scale_row[:, None, :]) + shift_row[:, None, :]

def forward(tile_weights, row_weights, patch_block, noise_block, step_block, label_block):
    w_ada, w_qkv, w_out, w_up, w_down = split_matrices(low(tile_weights), D, FF, BLK)
    label_table, w_time1, w_time2, w_final, w_patch, w_head, b_patch, b_time1, b_time2, b_query, b_value, b_out, b_down, b_ada, b_up, b_final = split_rows(low(row_weights), D, FF, NCLASS, FREQ, PATCH_DIM)
    image_count = step_block.shape[0]
    token_count = image_count * SEQ
    head_shape = (image_count, SEQ, HEADS, HD)
    embed = low_back(matmul(patch_block, w_patch)) + b_patch
    stream = embed.reshape(image_count, SEQ, D) + positions(LAT // PATCH_SIDE, D)[None]
    freq_low = low(time_freq(step_block, FREQ))
    time_low = low(jax.nn.silu(low_back(matmul(freq_low, w_time1)) + b_time1))
    time_embed = low_back(matmul(time_low, w_time2)) + b_time2
    condition = time_embed + jnp.take(label_table, label_block, axis=0)
    cond_low = low(jax.nn.silu(condition))
    modulation = low_back(matmul(cond_low, w_ada)) + b_ada
    final_mod = low_back(matmul(cond_low, w_final)) + b_final
    shift_att, scale_att, gate_att, shift_mlp, scale_mlp, gate_mlp = jnp.split(modulation, 6, axis=1)
    shift_fin, scale_fin = jnp.split(final_mod, 2, axis=1)
    att_in = low(modulate(stream, scale_att, shift_att)).reshape(token_count, D)
    qkv_all = low_back(matmul(att_in, w_qkv))
    queries = low(qkv_all[:, :D] + b_query).reshape(head_shape)
    keys_all = low(qkv_all[:, D:2 * D]).reshape(head_shape)
    values_all = low(qkv_all[:, 2 * D:] + b_value).reshape(head_shape)
    scores = low_back(jnp.einsum('ilhd,imhd->ihlm', queries, keys_all, precision=highest) * HD ** (-0.5))
    probs_low = low(jax.nn.softmax(scores, axis=-1))
    attended = jnp.einsum('ihlm,imhd->ilhd', probs_low, values_all, precision=highest).reshape(token_count, D)
    attended = low(low_back(attended))
    out_att = (low_back(matmul(attended, w_out)) + b_out).reshape(image_count, SEQ, D)
    branch_att = gate_att[:, None, :] * out_att
    stream_mid = stream + branch_att
    mlp_in = low(modulate(stream_mid, scale_mlp, shift_mlp)).reshape(token_count, D)
    hidden_low = low(jax.nn.gelu(low_back(matmul(mlp_in, w_up)) + b_up, approximate=True))
    out_mlp = (low_back(matmul(hidden_low, w_down)) + b_down).reshape(image_count, SEQ, D)
    branch_mlp = gate_mlp[:, None, :] * out_mlp
    stream_end = stream_mid + branch_mlp
    end_in = low(modulate(stream_end, scale_fin, shift_fin)).reshape(token_count, D)
    predicted = low_back(matmul(end_in, w_head.T))
    mismatch = predicted - noise_block
    total_square = jnp.sum(mismatch * mismatch)
    statistics = jnp.stack([total_square, jnp.sum(stream_end * stream_end), jnp.sum(branch_att * branch_att), jnp.sum(branch_mlp * branch_mlp)])
    return (total_square / (TOKENS * PATCH_DIM), statistics)

def reference(patches, noise, timesteps, labels, assign, tile_master, tile_bases, tile_moment, tile_second, row_master, row_moment, row_second):
    tile_order = jnp.zeros_like(tile_master).at[assign].set(tile_master)
    block_images = 16
    block_count = IMAGES // block_images
    patch_blocks = patches.astype(jnp.float32).reshape(block_count, block_images * SEQ, PATCH_DIM)
    noise_blocks = noise.reshape(block_count, block_images * SEQ, PATCH_DIM)
    step_blocks = timesteps.reshape(block_count, block_images)
    label_blocks = labels.reshape(block_count, block_images)

    def one_block(carry, inputs):
        grad_tiles, grad_rows, totals = carry
        patch_block, noise_block, step_block, label_block = inputs

        def loss_of(tile_weights, row_weights):
            return forward(tile_weights, row_weights, patch_block, noise_block, step_block, label_block)
        loss_value, backward, block_stats = jax.vjp(loss_of, tile_order, row_master, has_aux=True)
        tile_grad, row_grad = backward(jnp.ones_like(loss_value))
        return ((grad_tiles + tile_grad, grad_rows + row_grad, totals + block_stats), None)
    start = (jnp.zeros_like(tile_master), jnp.zeros_like(row_master), jnp.zeros((4,), jnp.float32))
    (grad_tiles, grad_rows, totals), unused = lax.scan(one_block, start, (patch_blocks, noise_blocks, step_blocks, label_blocks))
    grad_slots = grad_tiles[assign]
    square_sum = jnp.sum(grad_slots * grad_slots) + jnp.sum(grad_rows * grad_rows)
    grad_norm = jnp.sqrt(square_sum)
    factor = clip_at / jnp.maximum(grad_norm, clip_at)
    tile_grad = factor * grad_slots
    left_basis = tile_bases[:, 0]
    right_basis = tile_bases[:, 1]
    rotated = jnp.einsum('sji,sjk->sik', left_basis, jnp.einsum('sij,sjk->sik', tile_grad, right_basis, precision=highest), precision=highest)
    new_tile_moment = beta_one * tile_moment + (1.0 - beta_one) * rotated
    new_tile_second = beta_two * tile_second + (1.0 - beta_two) * rotated * rotated
    direction = new_tile_moment / (jnp.sqrt(new_tile_second) + adam_eps)
    restored = jnp.einsum('sij,skj->sik', jnp.einsum('sij,sjk->sik', left_basis, direction, precision=highest), right_basis, precision=highest)
    tile_update = -rate_step * restored
    row_grad = factor * grad_rows
    new_row_moment = beta_one * row_moment + (1.0 - beta_one) * row_grad
    new_row_second = beta_two * row_second + (1.0 - beta_two) * row_grad * row_grad
    row_update = -rate_step * (new_row_moment / (jnp.sqrt(new_row_second) + adam_eps) + decay_rate * row_master)
    loss = totals[0] / (TOKENS * PATCH_DIM)
    act_rms = jnp.sqrt(totals[1:] / (TOKENS * D))
    return (loss, grad_norm, act_rms, new_tile_moment, new_tile_second, tile_update, new_row_moment, new_row_second, row_update)
```

```python
import functools
import math

import jax
import jax.numpy as jnp
from jax import lax
from jax.experimental import pallas as pl
from jax.experimental.pallas import tpu as pltpu
from jax.sharding import PartitionSpec as P

D = 1024
HEADS = 16
HD = 64
FF = 4096
NCLASS = 1000
FREQ = 256
PATCH_SIDE = 2
LAT = 32
BLK = 256
PATCH_DIM = 16
SEQ = 256

NB = D // BLK
HB = FF // BLK
QB = 3 * NB
ADA = NB * 6 * NB
BIG = NB * QB + NB * NB + 2 * NB * HB
AT_QKV, AT_OUT, AT_UP, AT_DOWN = 0, NB * QB, NB * QB + NB * NB, NB * QB + NB * NB + NB * HB
L_ATT, L_OUT, L_MLP, L_HID = 0, NB, 2 * NB, 3 * NB
R_QKV = 3 * NB + HB
R_OUT = R_QKV + QB
R_UP = R_OUT + NB
R_DOWN = R_UP + HB
ACTS = R_DOWN + NB
B_OUT, B_UP, B_DOWN = QB, QB + NB, QB + NB + HB
ROW_STEP = 16
LANES = D // 128
NEAR = 64
NEAR_START = NCLASS + FREQ + 3 * D
N_PATCH, N_TIME1, N_TIME2, N_QUERY, N_VALUE, N_OUT, N_DOWN, N_ADA = range(2 * PATCH_DIM, 2 * PATCH_DIM + 8)
N_UP = N_ADA + 6
N_FINAL = N_UP + FF // D
NEAR_REAL = N_FINAL + 2
T_PATCH, T_OUT, T_DOWN, T_QUERY, T_VALUE, T_UP = range(2 * PATCH_DIM, 2 * PATCH_DIM + 6)
T_END = T_UP + FF // D
TOKEN_ROWS = 48

GROUPS, SHARDS = 4, 8
MESH_ID = pl.DeviceIdType.MESH

ln_eps = 1e-06
beta_one = 0.5
beta_two = 0.5
adam_eps = 1e-08
rate_step = 0.01
decay_rate = 0.1
clip_at = 0.25

f32 = jnp.float32
bf16 = jnp.bfloat16


def nn(left, right):
    return lax.dot_general(left, right, (((1,), (0,)), ((), ())), preferred_element_type=f32)


def nt(left, right):
    return lax.dot_general(left, right, (((1,), (1,)), ((), ())), preferred_element_type=f32)


def tn(left, right):
    return lax.dot_general(left, right, (((0,), (0,)), ((), ())), preferred_element_type=f32)


def wide(ref, at, count=ROW_STEP):
    return jnp.concatenate([ref[r, pl.ds(at, count), :] for r in range(NB)], axis=1)


def put(ref, base, at, value, count=ROW_STEP):
    for r in range(NB):
        ref[base + r, pl.ds(at, count), :] = value[:, r * BLK : (r + 1) * BLK].astype(ref.dtype)


def fold(value):
    return jnp.sum(value.reshape(-1, 8, value.shape[-1]), axis=0)


def normed(value):
    centred = value - jnp.mean(value, axis=-1, keepdims=True)
    spread = jnp.mean(centred * centred, axis=-1, keepdims=True)
    back = lax.rsqrt(spread + ln_eps)
    return centred * back, back


def over_rows(body):
    def step(i, unused):
        body(pl.multiple_of(i * ROW_STEP, ROW_STEP))
        return unused

    lax.fori_loop(0, SEQ // ROW_STEP, step, 0)


def over(count, body):
    def step(i, unused):
        body(i)
        return unused

    lax.fori_loop(0, count, step, 0)


def norm_back(grad, value, scale):
    norm, back = normed(value)
    inner = grad * (1.0 + scale)
    mean_one = jnp.mean(inner, axis=-1, keepdims=True)
    mean_two = jnp.mean(inner * norm, axis=-1, keepdims=True)
    return norm, (inner - mean_one - norm * mean_two) * back


def gelu_pair(value):
    root = math.sqrt(2.0 / math.pi)
    square = value * value
    bend = jnp.tanh(root * (value + 0.044715 * value * square))
    half = 0.5 * (1.0 + bend)
    slope = half + 0.5 * value * (1.0 - bend * bend) * root * (1.0 + 3 * 0.044715 * square)
    return value * half, slope


def block_body(
    loss_factor, place_ref, tiles_ref, patches_ref, noise_ref, spot_ref, near_ref, mods_ref,
    acts_ref, dmod_ref, ends_ref, stats_ref,
    w_ref, stream, middle, last, out_att, out_mlp, low_in, low_att, qkv, hid, slope, probs, flow, sums,
    near_wide, bias_ref, mod_ref, dbias_ref, w_sem,
):
    att_scale = HD ** (-0.5)
    cuts = (AT_QKV, AT_OUT, AT_UP, AT_DOWN, BIG)

    def fetch(b, sem):
        pltpu.make_async_copy(tiles_ref.at[place_ref[b]], w_ref.at[b], w_sem.at[sem]).start()

    for m in range(4):
        over(cuts[m + 1] - cuts[m], lambda b, m=m: fetch(cuts[m] + b, m))

    def arrived(m):
        span = pl.ds(cuts[m], cuts[m + 1] - cuts[m])
        pltpu.make_async_copy(tiles_ref.at[pl.ds(0, cuts[m + 1] - cuts[m])], w_ref.at[span], w_sem.at[m]).wait()

    def mod(i):
        return mod_ref[i : i + 1, :]

    near_wide[...] = near_ref[...].astype(f32)

    def row_block(row, r):
        return jnp.concatenate([near_wide[2 * r, row : row + 1, :], near_wide[2 * r + 1, row : row + 1, :]], axis=1)

    def near_block(row, r):
        span = slice(row, row + PATCH_DIM)
        return jnp.concatenate([near_ref[2 * r, span, :], near_ref[2 * r + 1, span, :]], axis=1)

    for r in range(NB):
        bias_ref[r] = row_block(N_QUERY, r)
        bias_ref[NB + r] = jnp.zeros((1, BLK), f32)
        bias_ref[2 * NB + r] = row_block(N_VALUE, r)
        bias_ref[B_OUT + r] = row_block(N_OUT, r)
        bias_ref[B_DOWN + r] = row_block(N_DOWN, r)
        for i in range(FF // D):
            bias_ref[B_UP + i * NB + r] = row_block(N_UP + i, r)
    for i in range(8):
        mod_ref[i : i + 1, :] = jnp.concatenate([mods_ref[i * LANES + o : i * LANES + o + 1, :] for o in range(LANES)], axis=1)

    lane = lax.broadcasted_iota(jnp.int32, (SEQ, 128), 1)
    lower = lane < HD
    halves = (lower, jnp.logical_not(lower))

    def masked(value, side):
        return jnp.where(halves[side], value, jnp.zeros_like(value))

    sums[...] = jnp.zeros_like(sums)
    S_SQ_END, S_SQ_ATT, S_SQ_MLP = 0, 1, 2
    S_DSH_A, S_DSC_A, S_DG_A, S_DSH_M, S_DSC_M, S_DG_M, S_DSH_F, S_DSC_F = range(3, 11)
    S_PATCH, S_OUT, S_DOWN = 11, 12, 13

    def collect(which, value):
        sums[which] = sums[which] + fold(value)

    patches = patches_ref[...]
    for r in range(NB):
        span = slice(r * BLK, (r + 1) * BLK)
        stream[r] = nn(patches, near_block(0, r)) + row_block(N_PATCH, r) + spot_ref[:, span]

    def modulate(source, scale, shift):
        def body(at):
            norm, _ = normed(wide(source, at))
            put(low_in, 0, at, norm * (1.0 + scale) + shift)

        over_rows(body)

    def transposed(base, ref, count):
        over(count, lambda r: acts_ref.__setitem__(base + r, ref[r].T))

    modulate(stream, mod(1), mod(0))
    transposed(L_ATT, low_in, NB)
    arrived(0)

    def qkv_step(c):
        total = nn(low_in[0], w_ref[AT_QKV + c])
        for r in range(1, NB):
            total += nn(low_in[r], w_ref[AT_QKV + r * QB + c])
        qkv[c] = (total + bias_ref[c]).astype(bf16)

    over(QB, qkv_step)

    def attend(c):
        for half in range(2):
            span = slice(half * 128, (half + 1) * 128)
            q, k, v = qkv[c, :, span], qkv[NB + c, :, span], qkv[2 * NB + c, :, span]
            parts = []
            for side in range(2):
                scores = nt(masked(q, side), k) * att_scale
                top = jnp.max(scores, axis=-1, keepdims=True)
                power = jnp.exp(scores - top)
                prob = power / jnp.sum(power, axis=-1, keepdims=True)
                probs[c * 4 + half * 2 + side] = prob
                parts.append(nn(prob.astype(bf16), v))
            low_att[c, :, span] = jnp.where(lower, parts[0], parts[1]).astype(bf16)

    over(NB, attend)
    transposed(L_OUT, low_att, NB)
    arrived(1)

    def out_step(c):
        total = nn(low_att[0], w_ref[AT_OUT + c])
        for r in range(1, NB):
            total += nn(low_att[r], w_ref[AT_OUT + r * NB + c])
        out_att[c] = total + bias_ref[B_OUT + c]

    over(NB, out_step)

    def mid_step(at):
        branch = mod(2) * wide(out_att, at)
        collect(S_SQ_ATT, branch * branch)
        value = wide(stream, at) + branch
        put(middle, 0, at, value)
        norm, _ = normed(value)
        put(low_in, 0, at, norm * (1.0 + mod(4)) + mod(3))

    over_rows(mid_step)
    transposed(L_MLP, low_in, NB)
    arrived(2)

    def up_step(c):
        total = nn(low_in[0], w_ref[AT_UP + c])
        for r in range(1, NB):
            total += nn(low_in[r], w_ref[AT_UP + r * HB + c])
        value, back = gelu_pair(total + bias_ref[B_UP + c])
        slope[c] = back
        low = value.astype(bf16)
        hid[c] = low
        acts_ref[L_HID + c] = low.T

    over(HB, up_step)
    arrived(3)

    def down_step(c):
        total = nn(hid[0], w_ref[AT_DOWN + c])
        for r in range(1, HB):
            total += nn(hid[r], w_ref[AT_DOWN + r * NB + c])
        out_mlp[c] = total + bias_ref[B_DOWN + c]

    over(NB, down_step)

    def end_step(at):
        branch = mod(5) * wide(out_mlp, at)
        collect(S_SQ_MLP, branch * branch)
        value = wide(middle, at) + branch
        collect(S_SQ_END, value * value)
        put(last, 0, at, value)
        norm, _ = normed(value)
        put(low_in, 0, at, norm * (1.0 + mod(7)) + mod(6))

    over_rows(end_step)
    predicted = nt(low_in[0], near_block(PATCH_DIM, 0))
    for r in range(1, NB):
        predicted += nt(low_in[r], near_block(PATCH_DIM, r))
    mismatch = predicted - noise_ref[...]
    loss_sum = jnp.sum(mismatch * mismatch)
    pred_low = (loss_factor * mismatch).astype(bf16)
    def put_rows(row, count, r, value):
        for i in range(2):
            ends_ref[2 * r + i, row : row + count, :] = value[:, i * 128 : (i + 1) * 128]

    for r in range(NB):
        put_rows(PATCH_DIM, PATCH_DIM, r, tn(pred_low, low_in[r]))
        flow[r] = nn(pred_low, near_block(PATCH_DIM, r))

    def end_back(at):
        grad = wide(flow, at)
        norm, value = norm_back(grad, wide(last, at), mod(7))
        collect(S_DSC_F, grad * norm)
        collect(S_DSH_F, grad)
        put(last, 0, at, value)
        collect(S_DG_M, value * wide(out_mlp, at))
        down = value * mod(5)
        collect(S_DOWN, down)
        put(acts_ref, R_DOWN, at, down)

    over_rows(end_back)

    def up_back(c):
        total = nt(acts_ref[R_DOWN], w_ref[AT_DOWN + c * NB])
        for j in range(1, NB):
            total += nt(acts_ref[R_DOWN + j], w_ref[AT_DOWN + c * NB + j])
        value = total * slope[c]
        dbias_ref[2 * NB + c] = jnp.sum(value, axis=0, keepdims=True)
        acts_ref[R_UP + c] = value.astype(bf16)

    over(HB, up_back)

    def mlp_back(r):
        total = nt(acts_ref[R_UP], w_ref[AT_UP + r * HB])
        for c in range(1, HB):
            total += nt(acts_ref[R_UP + c], w_ref[AT_UP + r * HB + c])
        flow[r] = total

    over(NB, mlp_back)

    def mid_back(at):
        grad = wide(flow, at)
        norm, value = norm_back(grad, wide(middle, at), mod(4))
        collect(S_DSC_M, grad * norm)
        collect(S_DSH_M, grad)
        value = value + wide(last, at)
        put(middle, 0, at, value)
        collect(S_DG_A, value * wide(out_att, at))
        proj = value * mod(2)
        collect(S_OUT, proj)
        put(acts_ref, R_OUT, at, proj)

    over_rows(mid_back)

    def att_back(r):
        total = nt(acts_ref[R_OUT], w_ref[AT_OUT + r * NB])
        for c in range(1, NB):
            total += nt(acts_ref[R_OUT + c], w_ref[AT_OUT + r * NB + c])
        low_att[r] = total.astype(bf16)

    over(NB, att_back)

    def attend_back(c):
        for half in range(2):
            span = slice(half * 128, (half + 1) * 128)
            q, k, v = qkv[c, :, span], qkv[NB + c, :, span], qkv[2 * NB + c, :, span]
            grad = low_att[c, :, span]
            found = []
            for side in range(2):
                prob = probs[c * 4 + half * 2 + side]
                dprob = nt(masked(grad, side), v)
                dvalue = tn(prob.astype(bf16), grad)
                dscore = prob * (dprob - jnp.sum(dprob * prob, axis=-1, keepdims=True))
                low = dscore.astype(bf16)
                found.append((nn(low, k) * att_scale, tn(low, q) * att_scale, dvalue))
            merged = [jnp.where(lower, one, two) for one, two in zip(*found)]
            for i in range(3):
                acts_ref[R_QKV + i * NB + c, :, span] = merged[i].astype(bf16)
            dbias_ref[c, :, span] = jnp.sum(merged[0], axis=0, keepdims=True)
            dbias_ref[NB + c, :, span] = jnp.sum(merged[2], axis=0, keepdims=True)

    over(NB, attend_back)

    def in_back(r):
        total = nt(acts_ref[R_QKV], w_ref[AT_QKV + r * QB])
        for c in range(1, QB):
            total += nt(acts_ref[R_QKV + c], w_ref[AT_QKV + r * QB + c])
        flow[r] = total

    over(NB, in_back)

    def first_back(at):
        grad = wide(flow, at)
        norm, value = norm_back(grad, wide(stream, at), mod(1))
        collect(S_DSC_A, grad * norm)
        collect(S_DSH_A, grad)
        value = value + wide(middle, at)
        collect(S_PATCH, value)
        put(low_in, 0, at, value)

    over_rows(first_back)
    for r in range(NB):
        put_rows(0, PATCH_DIM, r, tn(patches, low_in[r]))

    def total_of(which):
        return jnp.sum(sums[which], axis=0, keepdims=True)

    for i in range(8):
        value = total_of(S_DSH_A + i)
        for o in range(LANES):
            dmod_ref[i * LANES + o : i * LANES + o + 1, :] = value[:, o * 128 : (o + 1) * 128]
    for row, which in ((T_PATCH, S_PATCH), (T_OUT, S_OUT), (T_DOWN, S_DOWN)):
        value = total_of(which)
        for r in range(NB):
            put_rows(row, 1, r, value[:, r * BLK : (r + 1) * BLK])
    for r in range(NB):
        put_rows(T_QUERY, 1, r, dbias_ref[r])
        put_rows(T_VALUE, 1, r, dbias_ref[NB + r])
        for i in range(FF // D):
            put_rows(T_UP + i, 1, r, dbias_ref[2 * NB + i * NB + r])
    ends_ref[:, T_END:, :] = jnp.zeros((LANES, TOKEN_ROWS - T_END, 128), f32)
    row = lax.broadcasted_iota(jnp.int32, (8, 128), 0)
    found = jnp.where(row == 0, loss_sum, 0.0)
    for i in range(3):
        found = jnp.where(row == i + 1, jnp.sum(sums[i]), found)
    stats_ref[...] = found


def block_step(place, tiles, patches, noise, spots, near, mods, loss_factor):
    vmem = pl.BlockSpec(memory_space=pltpu.VMEM)
    macs = 3 * SEQ * BIG * BLK * BLK
    return pl.pallas_call(
        functools.partial(block_body, loss_factor),
        out_shape=[
            jax.ShapeDtypeStruct((ACTS, BLK, BLK), bf16),
            jax.ShapeDtypeStruct((8 * LANES, 128), f32),
            jax.ShapeDtypeStruct((LANES, TOKEN_ROWS, 128), f32),
            jax.ShapeDtypeStruct((8, 128), f32),
        ],
        in_specs=[pl.BlockSpec(memory_space=pltpu.SMEM), pl.BlockSpec(memory_space=pl.ANY)] + [vmem] * 5,
        out_specs=[vmem] * 4,
        scratch_shapes=[
            pltpu.VMEM((BIG, BLK, BLK), bf16),
            pltpu.VMEM((NB, SEQ, BLK), f32),
            pltpu.VMEM((NB, SEQ, BLK), f32),
            pltpu.VMEM((NB, SEQ, BLK), f32),
            pltpu.VMEM((NB, SEQ, BLK), f32),
            pltpu.VMEM((NB, SEQ, BLK), f32),
            pltpu.VMEM((NB, SEQ, BLK), bf16),
            pltpu.VMEM((NB, SEQ, BLK), bf16),
            pltpu.VMEM((QB, SEQ, BLK), bf16),
            pltpu.VMEM((HB, SEQ, BLK), bf16),
            pltpu.VMEM((HB, SEQ, BLK), f32),
            pltpu.VMEM((HEADS, SEQ, SEQ), f32),
            pltpu.VMEM((NB, SEQ, BLK), f32),
            pltpu.VMEM((14, 8, D), f32),
            pltpu.VMEM((LANES, NEAR, 128), f32),
            pltpu.VMEM((B_DOWN + NB, 1, BLK), f32),
            pltpu.VMEM((8, D), f32),
            pltpu.VMEM((2 * NB + HB, 1, BLK), f32),
            pltpu.SemaphoreType.DMA((4,)),
        ],
        compiler_params=pltpu.CompilerParams(vmem_limit_bytes=61 << 20),
        cost_estimate=pl.CostEstimate(flops=2 * macs, bytes_accessed=BIG * BLK * BLK * 4, transcendentals=0),
        name="block_step",
    )(place, tiles, patches, noise, spots, near, mods)


def ada_front_body(row_ref, col_ref, cond_ref, tile_ref, out_ref):
    s = pl.program_id(0)

    @pl.when(s == 0)
    def _():
        out_ref[...] = jnp.zeros_like(out_ref)

    @pl.when(col_ref[s] >= 0)
    def _():
        c = col_ref[s]
        out_ref[c] = out_ref[c] + nn(cond_ref[row_ref[s]], tile_ref[0].astype(bf16))


def ada_front(row_of, col_of, cond_blocks, tile_master):
    per, images = tile_master.shape[0], cond_blocks.shape[1]
    return pl.pallas_call(
        ada_front_body,
        grid_spec=pltpu.PrefetchScalarGridSpec(
            num_scalar_prefetch=2,
            grid=(per,),
            in_specs=[
                pl.BlockSpec(cond_blocks.shape, lambda s, r, c: (0, 0, 0)),
                pl.BlockSpec((1, BLK, BLK), lambda s, r, c: (s, 0, 0)),
            ],
            out_specs=pl.BlockSpec((6 * NB, images, BLK), lambda s, r, c: (0, 0, 0)),
        ),
        out_shape=jax.ShapeDtypeStruct((6 * NB, images, BLK), f32),
        name="ada_front",
    )(row_of, col_of, cond_blocks, tile_master)


def ada_back_body(row_ref, col_ref, dmod_ref, tile_ref, out_ref):
    s = pl.program_id(0)

    @pl.when(s == 0)
    def _():
        out_ref[...] = jnp.zeros_like(out_ref)

    @pl.when(col_ref[s] >= 0)
    def _():
        r = row_ref[s]
        out_ref[r] = out_ref[r] + nt(dmod_ref[col_ref[s]], tile_ref[0].astype(bf16))


def ada_back(row_of, col_of, dmod_blocks, tile_master):
    per, images = tile_master.shape[0], dmod_blocks.shape[1]
    return pl.pallas_call(
        ada_back_body,
        grid_spec=pltpu.PrefetchScalarGridSpec(
            num_scalar_prefetch=2,
            grid=(per,),
            in_specs=[
                pl.BlockSpec(dmod_blocks.shape, lambda s, r, c: (0, 0, 0)),
                pl.BlockSpec((1, BLK, BLK), lambda s, r, c: (s, 0, 0)),
            ],
            out_specs=pl.BlockSpec((NB, images, BLK), lambda s, r, c: (0, 0, 0)),
        ),
        out_shape=jax.ShapeDtypeStruct((NB, images, BLK), f32),
        name="ada_back",
    )(row_of, col_of, dmod_blocks, tile_master)


def tile_grad_body(left_ref, right_ref, acts_ref, out_ref):
    s = pl.program_id(0)
    out_ref[0] = nn(acts_ref[left_ref[s]], acts_ref[right_ref[s]]).astype(bf16)


def tile_grads(left_of, right_of, acts):
    count = left_of.shape[0]
    return pl.pallas_call(
        tile_grad_body,
        grid_spec=pltpu.PrefetchScalarGridSpec(
            num_scalar_prefetch=2,
            grid=(count,),
            in_specs=[pl.BlockSpec(acts.shape, lambda s, a, b: (0, 0, 0))],
            out_specs=pl.BlockSpec((1, BLK, BLK), lambda s, a, b: (s, 0, 0)),
        ),
        out_shape=jax.ShapeDtypeStruct((count, BLK, BLK), bf16),
        compiler_params=pltpu.CompilerParams(vmem_limit_bytes=40 << 20),
        name="tile_grads",
    )(left_of, right_of, acts)


def adam_body(group, where_ref, row_ref, col_ref, factor_ref, grads_ref, cond_ref, dmod_ref, bases_ref, moment_ref, second_ref,
              new_moment_ref, new_second_ref, update_ref, grad):
    step = pl.program_id(0)
    factor = factor_ref[0]
    for j in range(group):
        s = step * group + j

        @pl.when(col_ref[s] >= 0)
        def _():
            grad[...] = nn(cond_ref[row_ref[s]], dmod_ref[jnp.maximum(col_ref[s], 0)]).astype(bf16)

        @pl.when(col_ref[s] < 0)
        def _():
            grad[...] = grads_ref[where_ref[s]]

        left, right = bases_ref[j, 0].astype(bf16), bases_ref[j, 1].astype(bf16)
        turned = factor * nn(left.T, nn(grad[...], right).astype(bf16))
        moment = beta_one * moment_ref[j] + (1.0 - beta_one) * turned
        second = beta_two * second_ref[j] + (1.0 - beta_two) * turned * turned
        new_moment_ref[j] = moment
        new_second_ref[j] = second
        direction = (moment / (jnp.sqrt(second) + adam_eps)).astype(bf16)
        update_ref[j] = -rate_step * nt(nn(left, direction).astype(bf16), right)


def adam(where, row_of, col_of, factor, grads, cond_blocks, dmod_blocks, bases, moment, second):
    per = moment.shape[0]
    group = next(g for g in (3, 2, 1) if per % g == 0)
    tile = pl.BlockSpec((group, BLK, BLK), lambda s, *_: (s, 0, 0))

    def whole(array):
        return pl.BlockSpec(array.shape, lambda s, *_: (0,) * array.ndim)

    shape = jax.ShapeDtypeStruct(moment.shape, f32)
    return pl.pallas_call(
        functools.partial(adam_body, group),
        grid_spec=pltpu.PrefetchScalarGridSpec(
            num_scalar_prefetch=4,
            grid=(per // group,),
            in_specs=[
                whole(grads),
                whole(cond_blocks),
                whole(dmod_blocks),
                pl.BlockSpec((group, 2, BLK, BLK), lambda s, *_: (s, 0, 0, 0)),
                tile,
                tile,
            ],
            out_specs=[tile] * 3,
            scratch_shapes=[pltpu.VMEM((BLK, BLK), bf16)],
        ),
        out_shape=[shape] * 3,
        compiler_params=pltpu.CompilerParams(vmem_limit_bytes=56 << 20),
        name="adam_tiles",
    )(where, row_of, col_of, factor, grads, cond_blocks, dmod_blocks, bases, moment, second)

def spread_body(
    cap, n_third,
    slot_ref, row_ref, col_ref, tiles_ref, rows_ref, ids_ref,
    out_ref, near_ref, mods_ref, freq_ref, label_ref, time_ref, cond_ref, pre_ref, own_cond_ref,
    tile, pack, ids, near, times, conds, near_wide, cond_group, product, part, part_out, part_in,
    load_sem, keep_sem, send_sem, recv_sem, small_send, small_recv,
):
    z, s = lax.axis_index("grp"), lax.axis_index("shard")
    per = tile.shape[0]
    images = GROUPS * SHARDS
    third = cap // 3
    step = third // n_third
    x_at, y_at, c_at, z_at = (z, s ^ 2), (z, s ^ 4), (z, s ^ 1), (z ^ 1, s)
    far_z = [(lax.rem(z + i, GROUPS), s) for i in range(1, GROUPS)]
    near_s = [(z, s ^ i) for i in range(1, SHARDS)]

    barrier = pltpu.get_barrier_semaphore()
    for peer in far_z + near_s:
        pl.semaphore_signal(barrier, inc=1, device_id=peer, device_id_type=MESH_ID)
    load = pltpu.make_async_copy(tiles_ref, tile, load_sem)
    load.start()

    def block_rows(index, count):
        return pl.ds(pl.multiple_of(index * count, count), count)

    ids[block_rows(s * GROUPS + z, 8), :] = ids_ref[...]
    near_wide[...] = jnp.zeros_like(near_wide)
    near_wide[: NEAR_REAL - 3, :] = rows_ref[NEAR_START : NEAR_START + NEAR_REAL - 3, :]
    near_wide[NEAR_REAL - 3 : NEAR_REAL, :] = rows_ref[NEAR_START + NEAR_REAL - 3 : NEAR_START + NEAR_REAL, :]
    near[s] = near_wide[...].astype(bf16)
    near_wide[...] = near_wide[...].astype(bf16).astype(f32)
    pl.semaphore_wait(barrier, len(far_z) + len(near_s))

    sent = []

    def push(src, dst, peer, index):
        copy = pltpu.make_async_remote_copy(
            src_ref=src, dst_ref=dst, send_sem=small_send.at[index], recv_sem=small_recv.at[index],
            device_id=peer, device_id_type=MESH_ID,
        )
        copy.start()
        sent.append(copy)
        return copy

    def to_group(stage, pairs):
        first = len(far_z) + stage * len(near_s)
        return [push(*pairs(peer[1]), peer, first + i) for i, peer in enumerate(near_s)]

    def got(copies):
        for copy in copies:
            copy.wait_recv()

    own_ids = ids.at[block_rows(s * GROUPS + z, 8)]
    id_far = [push(own_ids, own_ids, peer, i) for i, peer in enumerate(far_z)]
    near_copies = to_group(0, lambda p: (near.at[s], near.at[s]))

    parity = lax.rem(z, 2)
    starts = (third + parity * third, 0, 2 * third - parity * third)

    def chunk(index):
        kind, at = divmod(index, n_third)
        return pl.ds(starts[kind] + at * step, step)

    load.wait()
    big = []

    def send(kind, stream, index, peer, src, owner, arrives):
        copy = pltpu.make_async_remote_copy(
            src_ref=src, dst_ref=out_ref.at[owner, chunk(index)],
            send_sem=send_sem.at[kind, index], recv_sem=recv_sem.at[stream, arrives],
            device_id=peer, device_id_type=MESH_ID,
        )
        copy.start()
        big.append(copy)

    def wait_for(stream, index, owner):
        place = out_ref.at[owner, chunk(index)]
        pltpu.make_async_remote_copy(
            src_ref=place, dst_ref=place, send_sem=send_sem.at[0, index], recv_sem=recv_sem.at[stream, index],
            device_id=x_at, device_id_type=MESH_ID,
        ).wait_recv()

    def pack_chunk(index):
        kind, at = divmod(index, n_third)

        def one(i, unused):
            p = starts[kind] + at * step + i
            pack[p] = tile[slot_ref[p]].astype(bf16)
            return unused

        lax.fori_loop(0, step, one, 0)

    def send_mine(index):
        src = pack.at[chunk(index)]
        if index < 2 * n_third:
            send(0, 0, index, x_at, src, s, index)
            send(1, 1, index, y_at, src, s, index)
        send(2, 3, index, c_at, src, s, index)

    owners = (s ^ 2, s ^ 4, s ^ 6)

    def pass_on(which, index):
        owner = owners[which]
        wait_for(which, index, owner)
        here = out_ref.at[owner, chunk(index)]
        if index < 2 * n_third:
            if which == 0 and index % 2 == 0:
                send(6, 2, index, y_at, here, owner, index)
            if which == 1 and index % 2 == 1:
                send(7, 2, index, x_at, here, owner, index)
        if index < n_third:
            send(8 + which, which, index, z_at, here, owner, 2 * n_third + index)
        send(3 + which, 4 + which, index, c_at, here, owner, index)

    for j in range(n_third):
        pack_chunk(j)
        send_mine(j)
    got(id_far)
    span = block_rows(s, 8 * GROUPS)
    id_near = to_group(1, lambda p: (ids.at[span], ids.at[span]))
    for j in range(n_third, 3 * n_third):
        pack_chunk(j)
    keep = pltpu.make_async_copy(pack, out_ref.at[s, pl.ds(0, cap)], keep_sem)
    keep.start()
    stages = {}

    def silu_low(value):
        return (value * jax.nn.sigmoid(value)).astype(bf16)

    def row_slice(start, count):
        return rows_ref[start : start + count, :].astype(bf16)

    def time_stage():
        got(id_near)
        freq = jnp.concatenate([ids[pl.ds(i, images, stride=8), :] for i in range(2)], axis=1).astype(bf16)
        freq_ref[...] = freq
        label_ref[...] = ids[pl.ds(2, images, stride=8), :]
        pre = nn(freq, row_slice(NCLASS, FREQ)) + near_wide[N_TIME1 : N_TIME1 + 1, :]
        pre_ref[...] = pre
        times[s] = silu_low(pre)
        stages["time"] = to_group(2, lambda p: (times.at[s], times.at[s]))

    def cond_stage():
        got(stages["time"])
        total = jnp.zeros((images, 128), f32) + near_wide[N_TIME2 : N_TIME2 + 1, :]
        for o in range(SHARDS):
            total += nn(times[o], row_slice(NCLASS + FREQ + o * 128, 128))
        hot = label_ref[...].astype(jnp.int32)[:, :1] == lax.broadcasted_iota(jnp.int32, (images, D), 1)
        total += nn(hot.astype(bf16), row_slice(0, D))
        own_cond_ref[...] = total
        conds[s] = silu_low(total)
        stages["cond"] = to_group(3, lambda p: (conds.at[s], conds.at[s]))

    def group_stage():
        got(stages["cond"])
        at = lax.broadcasted_iota(jnp.int32, (SHARDS, images), 1)
        row = lax.broadcasted_iota(jnp.int32, (SHARDS, images), 0)
        pick = (at == row * GROUPS + z).astype(bf16)
        for o in range(SHARDS):
            half = o % 2
            cond_group[o // 2, :, half * 128 : (half + 1) * 128] = nn(pick, conds[o])

    def ada_stage(start, count):
        def one(j, unused):
            product[start + j] = nn(cond_group[row_ref[start + j]].astype(bf16), tile[start + j].astype(bf16))
            return unused

        lax.fori_loop(0, count, one, 0)

    def part_stage():
        part[...] = jnp.zeros_like(part)

        def column(c, unused):
            total = jnp.zeros((SHARDS, BLK), f32)
            for j in range(per):
                total += jnp.where(col_ref[j] == c, 1.0, 0.0) * product[j]
            for half in range(2):
                part[block_rows(2 * c + half, 8), :] = total[:, half * 128 : (half + 1) * 128]
            return unused

        lax.fori_loop(0, 6 * NB, column, 0)
        for i in range(6):
            place = block_rows(i * LANES + s, 8)
            part[place, :] = part[place, :] + near_wide[N_ADA + i : N_ADA + i + 1, :]
        for i in range(2):
            total = jnp.zeros((SHARDS, 128), f32) + near_wide[N_FINAL + i : N_FINAL + i + 1, :]
            for r in range(NB):
                weight = row_slice(NCLASS + FREQ + D + i * D + r * BLK, BLK)
                total += nn(cond_group[r].astype(bf16), weight)
            part[block_rows((6 + i) * LANES + s, 8), :] = total
        for o in range(SHARDS):
            part_out[o] = part[pl.ds(o, 8 * LANES, stride=8), :]
        part_in[s] = part_out[s]
        stages["part"] = to_group(4, lambda p: (part_out.at[p], part_in.at[s]))

    def mod_stage():
        got(stages["part"])
        total = part_in[0]
        for o in range(1, SHARDS):
            total += part_in[o]
        mods_ref[...] = total
        got(near_copies)
        near_ref[...] = near[...]
        time_ref[...] = times[...]
        cond_ref[...] = conds[...]

    cut = per // 3
    hooks = [
        time_stage, cond_stage, group_stage, lambda: ada_stage(0, cut), lambda: ada_stage(cut, cut),
        lambda: ada_stage(2 * cut, per - 2 * cut), part_stage, mod_stage,
    ]
    seen = [0]

    def hook():
        if hooks:
            hooks.pop(0)()

    def z_next():
        order = [(w, 2 * n_third + j) for j in range(n_third) for w in (0, 1)]
        order += [(2, 2 * n_third + j) for j in range(n_third)]
        if seen[0] < len(order):
            pass_on(*order[seen[0]])
            seen[0] += 1

    for j in range(n_third):
        pass_on(0, j)
        pass_on(1, j)
        hook()
        if j:
            z_next()
    for j in range(n_third, 3 * n_third):
        send_mine(j)
    for j in range(n_third):
        pass_on(2, j)
        if j % 2:
            z_next()
            hook()
    for j in range(n_third, 2 * n_third):
        pass_on(0, j)
        pass_on(1, j)
        hook()
        z_next()
    for j in range(n_third, 2 * n_third):
        pass_on(2, j)
        if j % 2:
            z_next()
            hook()
    while hooks:
        hook()
    while seen[0] < 3 * n_third:
        z_next()
    for index in range(3 * n_third):
        wait_for(3, index, s ^ 1)
        for which in range(3):
            wait_for(4 + which, index, owners[which] ^ 1)
    keep.wait()
    for copy in big + sent:
        copy.wait_send()


def spread(cap, slot_of, row_of, col_of, tile_master, row_master, ids):
    per = tile_master.shape[0]
    n_third = 4 if cap // 3 % 4 == 0 else next(n for n in (5, 3, 2, 1) if cap // 3 % n == 0)
    images = GROUPS * SHARDS
    vmem = pl.BlockSpec(memory_space=pltpu.VMEM)
    smem = pl.BlockSpec(memory_space=pltpu.SMEM)
    anywhere = pl.BlockSpec(memory_space=pl.ANY)
    small = (GROUPS - 1) + 5 * (SHARDS - 1)
    return pl.pallas_call(
        functools.partial(spread_body, cap, n_third),
        out_shape=[
            jax.ShapeDtypeStruct((SHARDS, per, BLK, BLK), bf16),
            jax.ShapeDtypeStruct((LANES, NEAR, 128), bf16),
            jax.ShapeDtypeStruct((8 * LANES, 128), f32),
            jax.ShapeDtypeStruct((images, FREQ), bf16),
            jax.ShapeDtypeStruct((images, 128), f32),
            jax.ShapeDtypeStruct((SHARDS, images, 128), bf16),
            jax.ShapeDtypeStruct((SHARDS, images, 128), bf16),
            jax.ShapeDtypeStruct((images, 128), f32),
            jax.ShapeDtypeStruct((images, 128), f32),
        ],
        in_specs=[smem] * 3 + [anywhere] + [vmem] * 2,
        out_specs=[anywhere] + [vmem] * 8,
        scratch_shapes=[
            pltpu.VMEM((per, BLK, BLK), f32),
            pltpu.VMEM((cap, BLK, BLK), bf16),
            pltpu.VMEM((images * 8, 128), f32),
            pltpu.VMEM((LANES, NEAR, 128), bf16),
            pltpu.VMEM((SHARDS, images, 128), bf16),
            pltpu.VMEM((SHARDS, images, 128), bf16),
            pltpu.VMEM((NEAR, 128), f32),
            pltpu.VMEM((NB, SHARDS, BLK), f32),
            pltpu.VMEM((per, SHARDS, BLK), f32),
            pltpu.VMEM((8 * LANES * 8, 128), f32),
            pltpu.VMEM((SHARDS, 8 * LANES, 128), f32),
            pltpu.VMEM((SHARDS, 8 * LANES, 128), f32),
            pltpu.SemaphoreType.DMA,
            pltpu.SemaphoreType.DMA,
            pltpu.SemaphoreType.DMA((11, 3 * n_third)),
            pltpu.SemaphoreType.DMA((7, 3 * n_third)),
            pltpu.SemaphoreType.DMA((small,)),
            pltpu.SemaphoreType.DMA((small,)),
        ],
        compiler_params=pltpu.CompilerParams(collective_id=cap, has_side_effects=True, vmem_limit_bytes=40 << 20),
        name="spread",
    )(slot_of, row_of, col_of, tile_master, row_master, ids)

RING = 4
Z_LAG = 5


def collect_body(
    cap, ch,
    left_ref, right_ref, row_ref, col_ref, count_ref,
    acts_ref, dmod_ref, ends_ref, stats_ref, time_ref, cond_ref, freq_ref, label_ref, pre_ref, own_cond_ref, rows_ref, tiles_ref,
    grads_ref, d_blocks_ref, own_rows_ref, norm_ref, stat_ref,
    out_c, in_c, out_d, out_x, out_y, in_dx, in_dy, in_x, in_y, total, low_in, high_in, final,
    tile, product, all_d, wide_d, all_stats, tok_in, tok_z, tokens, part_out, part_in, pre_out, pre_in, own_dcond, own_dpre,
    vectors, squares, square_in,
    c_send, c_recv, d_send, dx_recv, dy_recv, x_send, x_recv, y_send, y_recv, up_send, low_recv, high_recv, final_recv, down_send,
    keep_sem, load_sem, small_send, small_recv,
):
    z, s = lax.axis_index("grp"), lax.axis_index("shard")
    per = product.shape[0]
    images = GROUPS * SHARDS
    chunks = cap // ch
    x_at, y_at, c_at = (z, s ^ 2), (z, s ^ 4), (z, s ^ 1)
    far_z = [(lax.rem(z + i, GROUPS), s) for i in range(1, GROUPS)]
    near_s = [(z, s ^ i) for i in range(1, SHARDS)]
    half = BLK // 2
    upper, lower = pl.ds(0, half), pl.ds(half, half)

    barrier = pltpu.get_barrier_semaphore()
    for peer in far_z + near_s:
        pl.semaphore_signal(barrier, inc=1, device_id=peer, device_id_type=MESH_ID)

    def remote(src, dst, sent, received, peer):
        return pltpu.make_async_remote_copy(
            src_ref=src, dst_ref=dst, send_sem=sent, recv_sem=received, device_id=peer, device_id_type=MESH_ID
        )

    def block_rows(index, count):
        return pl.ds(pl.multiple_of(index * count, count), count)

    def far(stage, src, dst):
        return [
            remote(src, dst, small_send.at[stage * 3 + i], small_recv.at[stage * 3 + i], peer) for i, peer in enumerate(far_z)
        ]

    def group(stage, src_of, dst):
        first = 9 + stage * 7
        return [
            remote(src_of(peer[1]), dst, small_send.at[first + i], small_recv.at[first + i], peer)
            for i, peer in enumerate(near_s)
        ]

    own_d = all_d.at[block_rows(s * GROUPS + z, 8 * LANES)]
    own_stat = all_stats.at[block_rows(s * GROUPS + z, 8)]
    group_d = all_d.at[block_rows(s, 8 * LANES * GROUPS)]
    group_stat = all_stats.at[block_rows(s, 8 * GROUPS)]

    def small_copies(name):
        if name == "d_far":
            return far(0, own_d, own_d)
        if name == "stat_far":
            return far(1, own_stat, own_stat)
        if name == "tok_far":
            return far(2, tok_z.at[z], tok_z.at[z])
        if name == "tok":
            return group(0, lambda p: ends_ref.at[p], tok_in.at[s])
        if name == "d":
            return group(1, lambda p: group_d, group_d)
        if name == "stat":
            return group(2, lambda p: group_stat, group_stat)
        if name == "part":
            return group(3, lambda p: part_out.at[p], part_in.at[s])
        if name == "pre":
            return group(4, lambda p: pre_out.at[p], pre_in.at[s])
        return group(5, lambda p: square_in.at[s], square_in.at[s])

    def begin(*names):
        for name in names:
            for copy in small_copies(name):
                copy.start()

    def got(*names):
        for name in names:
            for copy in small_copies(name):
                copy.wait_recv()

    def load(part):
        count = tile.shape[0]
        return pltpu.make_async_copy(tiles_ref.at[pl.ds(part * count, count)], tile, load_sem)

    load(0).start()
    own_d[...] = dmod_ref[...].astype(bf16)
    own_stat[...] = stats_ref[...]
    tok_in[s] = ends_ref[s]
    squares[...] = jnp.zeros_like(squares)
    pl.semaphore_wait(barrier, len(far_z) + len(near_s))
    begin("d_far", "stat_far", "tok")

    def spread_stage():
        got("d_far", "stat_far")
        begin("d", "stat")
        got("tok")
        value = tok_in[0]
        for o in range(1, SHARDS):
            value += tok_in[o]
        tok_z[z] = value
        begin("tok_far")

    def order_stage():
        got("d", "stat", "tok_far")
        value = tok_z[0]
        for i in range(1, GROUPS):
            value += tok_z[i]
        tokens[...] = value
        value = all_stats[pl.ds(0, 8), :]
        for i in range(1, images):
            value += all_stats[pl.ds(8 * i, 8), :]
        stat_ref[...] = value

        def widen(i, unused):
            place = block_rows(i, 8 * LANES)
            wide_d[place, :] = all_d[place, :].astype(f32)
            return unused

        lax.fori_loop(0, images, widen, 0)
        for q in range(6 * LANES):
            d_blocks_ref[q // 2, :, (q % 2) * 128 : (q % 2 + 1) * 128] = wide_d[
                pl.ds(q, images, stride=8 * LANES), :
            ].astype(bf16)

    def own_columns(i):
        return wide_d[pl.ds(i * LANES + s, images, stride=8 * LANES), :]

    def ada_stage(part):
        count = tile.shape[0]
        load(part).wait()

        def one(j, unused):
            at = part * count + j
            product[at] = nt(d_blocks_ref[jnp.maximum(col_ref[at], 0)], tile[j].astype(bf16))
            return unused

        lax.fori_loop(0, count, one, 0)
        if (part + 1) * count < per:
            load(part + 1).start()

    def row_slice(start, count):
        return rows_ref[start : start + count, :].astype(bf16)

    final_at = NCLASS + FREQ + D

    def part_stage():
        for r in range(NB):
            value = jnp.zeros((images, BLK), f32)
            for i in range(2):
                value += nt(own_columns(6 + i).astype(bf16), row_slice(final_at + i * D + r * BLK, BLK))

            def add(j, value, r=r):
                chosen = jnp.logical_and(col_ref[j] >= 0, row_ref[j] == r)
                return value + jnp.where(chosen, 1.0, 0.0) * product[j]

            value = lax.fori_loop(0, per, add, value)
            for i in range(2):
                part_out[2 * r + i] = value[:, i * 128 : (i + 1) * 128]
        part_in[s] = part_out[s]
        begin("part")

    def slope(value):
        gate = jax.nn.sigmoid(value)
        return gate * (1.0 + value * (1.0 - gate))

    def cond_stage():
        got("part")
        value = part_in[0]
        for o in range(1, SHARDS):
            value += part_in[o]
        value = value * slope(own_cond_ref[...])
        own_dcond[...] = value
        for o in range(SHARDS):
            pre_out[o] = nt(value.astype(bf16), row_slice(NCLASS + FREQ + o * 128, 128))
        pre_in[s] = pre_out[s]
        begin("pre")

    def row_stage():
        got("pre")
        value = pre_in[0]
        for o in range(1, SHARDS):
            value += pre_in[o]
        value = value * slope(pre_ref[...])
        own_dpre[...] = value
        dpre_low, dcond = value.astype(bf16), own_dcond[...]
        dcond_low = dcond.astype(bf16)
        gathered = []

        def keep(start, value):
            own_rows_ref[start : start + value.shape[0], :] = value
            gathered.append(fold(value * value))

        hot = label_ref[...].astype(jnp.int32)[:, :1] == lax.broadcasted_iota(jnp.int32, (images, NCLASS), 1)
        keep(
            0,
            lax.dot_general(
                hot.astype(f32), dcond, (((0,), (0,)), ((), ())), preferred_element_type=f32, precision=lax.Precision.HIGHEST
            ),
        )
        keep(NCLASS, tn(freq_ref[...], dpre_low))
        for o in range(SHARDS):
            keep(NCLASS + FREQ + o * 128, tn(time_ref[o], dcond_low))
            for i in range(2):
                keep(final_at + i * D + o * 128, tn(cond_ref[o], own_columns(6 + i).astype(bf16)))
        keep(NEAR_START, tokens[: 2 * PATCH_DIM, :])

        vectors[...] = jnp.zeros_like(vectors)

        def vector(row, value):
            vectors[row : row + 1, :] = value

        vector(0, tokens[T_PATCH : T_PATCH + 1, :])
        vector(1, jnp.sum(value, axis=0, keepdims=True))
        vector(2, jnp.sum(dcond, axis=0, keepdims=True))
        vector(3, tokens[T_QUERY : T_QUERY + 1, :])
        vector(4, tokens[T_VALUE : T_VALUE + 1, :])
        vector(5, tokens[T_OUT : T_OUT + 1, :])
        vector(6, tokens[T_DOWN : T_DOWN + 1, :])
        for i in range(8):
            vector(7 + i if i < 6 else 7 + i + FF // D, jnp.sum(own_columns(i), axis=0, keepdims=True))
        for i in range(FF // D):
            vector(13 + i, tokens[T_UP + i : T_UP + i + 1, :])
        start = NEAR_START + 2 * PATCH_DIM
        rest = own_rows_ref.shape[0] - start
        whole = rest // 8 * 8
        own_rows_ref[start : start + whole, :] = vectors[:whole, :]
        own_rows_ref[start + whole : start + rest, :] = vectors[whole:rest, :]
        value = fold(vectors[...] * vectors[...])
        for piece in gathered:
            value += piece
        squares[:, :128] = squares[:, :128] + value

    def slot_of(i):
        return lax.rem(i + RING, RING)

    def block(owner, p):
        at = owner * per + p
        return nn(acts_ref[left_ref[at]], acts_ref[right_ref[at]])

    targets = (s ^ 6, s ^ 2, s ^ 4, s)

    def c_copy(slot, item):
        return remote(out_c.at[slot, item], in_c.at[slot, item], c_send.at[slot, item], c_recv.at[slot, item], c_at)

    def dx_copy(slot):
        return remote(out_d.at[slot, :, upper], in_dx.at[slot], d_send.at[slot, 0], dx_recv.at[slot], x_at)

    def dy_copy(slot):
        return remote(out_d.at[slot, :, lower], in_dy.at[slot], d_send.at[slot, 1], dy_recv.at[slot], y_at)

    def x_copy(slot):
        return remote(out_x.at[slot], in_x.at[slot], x_send.at[slot], x_recv.at[slot], x_at)

    def y_copy(slot):
        return remote(out_y.at[slot], in_y.at[slot], y_send.at[slot], y_recv.at[slot], y_at)

    def inside(i):
        return jnp.logical_and(i >= 0, i < chunks)

    def each(body):
        def one(c, unused):
            body(c)
            return unused

        lax.fori_loop(0, ch, one, 0)

    def for_sibling(n):
        slot = slot_of(n)
        for item in range(4):
            at = n + 1 if item == 0 else n

            @pl.when(inside(at))
            def _():
                def one(c):
                    out_c[slot, item, c] = block(targets[item] ^ 1, at * ch + c).astype(bf16)

                each(one)
                c_copy(slot, item).start()

    def for_owners(i):
        slot, before = slot_of(i), slot_of(i - 1)

        @pl.when(inside(i + 1))
        def _():
            c_copy(slot, 0).wait_recv()

            def one(c):
                value = block(targets[0], (i + 1) * ch + c) + in_c[slot, 0, c].astype(f32)
                out_d[slot, c] = value.astype(bf16)

            each(one)
            dx_copy(slot).start()
            dy_copy(slot).start()

        @pl.when(inside(i))
        def _():
            c_copy(slot, 1).wait_recv()
            dy_copy(before).wait_recv()

            def one(c):
                value = block(targets[1], i * ch + c) + in_c[slot, 1, c].astype(f32)
                out_x[slot, c, upper] = value[:half].astype(bf16)
                out_x[slot, c, lower] = (value[half:] + in_dy[before, c].astype(f32)).astype(bf16)

            each(one)
            x_copy(slot).start()
            c_copy(slot, 2).wait_recv()
            dx_copy(before).wait_recv()

            def two(c):
                value = block(targets[2], i * ch + c) + in_c[slot, 2, c].astype(f32)
                out_y[slot, c, upper] = (value[:half] + in_dx[before, c].astype(f32)).astype(bf16)
                out_y[slot, c, lower] = value[half:].astype(bf16)

            each(two)
            y_copy(slot).start()
            c_copy(slot, 3).wait_recv()

            def three(c):
                value = block(targets[3], i * ch + c) + in_c[slot, 3, c].astype(f32)
                total[i * ch + c] = value.astype(bf16)

            each(three)

        @pl.when(inside(i - 1))
        def _():
            x_copy(before).wait_recv()
            y_copy(before).wait_recv()

            def one(c):
                at = (i - 1) * ch + c
                value = total[at].astype(f32) + in_x[before, c].astype(f32) + in_y[before, c].astype(f32)
                total[at] = value.astype(bf16)

            each(one)

    def along(j):
        even = lax.rem(j, 2) == 0
        rank = jnp.where(even, z, GROUPS - 1 - z)
        down = jnp.where(even, lax.rem(z + GROUPS - 1, GROUPS), lax.rem(z + 1, GROUPS))
        up = jnp.where(even, lax.rem(z + 1, GROUPS), lax.rem(z + GROUPS - 1, GROUPS))
        return rank, (down, s), (up, s)

    def z_copy(name, j):
        _, down, up = along(j)
        span = pl.ds(j * ch, ch)
        if name == "rise":
            return remote(total.at[span], low_in.at[span], up_send.at[j], low_recv.at[j], up)
        if name == "sink":
            return remote(total.at[span], high_in.at[span], up_send.at[j], high_recv.at[j], down)
        if name == "final_down":
            return remote(final.at[span], final.at[span], down_send.at[0, j], final_recv.at[j], down)
        return remote(final.at[span], final.at[span], down_send.at[1, j], final_recv.at[j], up)

    def over_z(i):
        j = i - 1

        @pl.when(inside(j))
        def _():
            rank, _, _ = along(j)

            @pl.when(rank == 0)
            def _():
                z_copy("rise", j).start()

            @pl.when(rank == 3)
            def _():
                z_copy("sink", j).start()

        j2 = i - 2

        @pl.when(jnp.logical_and(inside(j2), along(j2)[0] == 2))
        def _():
            z_copy("sink", j2).wait_recv()

            def one(c):
                at = j2 * ch + c
                total[at] = (total[at].astype(f32) + high_in[at].astype(f32)).astype(bf16)

            each(one)
            z_copy("sink", j2).start()

        j3 = i - 3

        @pl.when(jnp.logical_and(inside(j3), along(j3)[0] == 1))
        def _():
            z_copy("rise", j3).wait_recv()
            z_copy("sink", j3).wait_recv()

            def one(c):
                at = j3 * ch + c
                value = total[at].astype(f32) + low_in[at].astype(f32) + high_in[at].astype(f32)
                final[at] = value.astype(bf16)

            each(one)
            z_copy("final_down", j3).start()
            z_copy("final_up", j3).start()

        j4 = i - 4

        @pl.when(jnp.logical_and(inside(j4), along(j4)[0] == 2))
        def _():
            z_copy("final_up", j4).wait_recv()
            z_copy("final_up", j4).start()

        j5 = i - Z_LAG

        @pl.when(inside(j5))
        def _():
            rank = along(j5)[0]

            @pl.when(jnp.logical_or(rank == 0, rank == 3))
            def _():
                z_copy("final_up", j5).wait_recv()

            span = pl.ds(j5 * ch, ch)
            pltpu.make_async_copy(final.at[span], grads_ref.at[span], keep_sem.at[j5]).start()

            def one(c):
                at = j5 * ch + c
                value = final[at].astype(f32) * jnp.where(at < count_ref[0], 1.0, 0.0)
                squares[...] = squares[...] + fold(value * value)

            each(one)

    def settle(i):
        n = i - 1
        slot = slot_of(n)
        for item in range(4):

            @pl.when(inside(n + 1 if item == 0 else n))
            def _():
                c_copy(slot, item).wait_send()

        n2 = i - 2
        slot2 = slot_of(n2)

        @pl.when(inside(n2 + 1))
        def _():
            dx_copy(slot2).wait_send()
            dy_copy(slot2).wait_send()

        @pl.when(inside(n2))
        def _():
            x_copy(slot2).wait_send()
            y_copy(slot2).wait_send()

    hooks = {
        0: spread_stage, 2: order_stage, 3: lambda: ada_stage(0), 4: lambda: ada_stage(1), 5: lambda: ada_stage(2),
        6: part_stage, 8: cond_stage, 10: row_stage,
    }

    for_sibling(-1)

    def iteration(step, unused):
        i = step - 1
        for_sibling(i + 1)
        for_owners(i)
        over_z(i)
        settle(i)
        for at, stage in hooks.items():
            pl.when(i == at)(stage)
        return unused

    lax.fori_loop(0, chunks + 1 + Z_LAG, iteration, 0)

    square_in[s] = jnp.zeros((8, 128), f32) + jnp.sum(squares[...])
    begin("square")

    cond_gram = jnp.zeros((images, images), f32)
    for o in range(SHARDS):
        cond_gram += nt(cond_ref[o], cond_ref[o])

    def gram(c, value):
        return value + nt(d_blocks_ref[c], d_blocks_ref[c])

    d_gram = lax.fori_loop(0, 6 * NB, gram, jnp.zeros((images, images), f32))
    got("square")
    value = square_in[0]
    for o in range(1, SHARDS):
        value += square_in[o]
    norm_ref[...] = value + jnp.sum(cond_gram * d_gram)

    def finish(j, unused):
        span = pl.ds(j * ch, ch)
        pltpu.make_async_copy(final.at[span], grads_ref.at[span], keep_sem.at[j]).wait()
        rank = along(j)[0]

        @pl.when(rank == 0)
        def _():
            z_copy("rise", j).wait_send()

        @pl.when(rank >= 2)
        def _():
            z_copy("sink", j).wait_send()

        @pl.when(rank == 1)
        def _():
            z_copy("final_down", j).wait_send()

        @pl.when(jnp.logical_or(rank == 1, rank == 2))
        def _():
            z_copy("final_up", j).wait_send()

        return unused

    lax.fori_loop(0, chunks, finish, 0)
    for name in ("d_far", "stat_far", "tok_far", "tok", "d", "stat", "part", "pre", "square"):
        for copy in small_copies(name):
            copy.wait_send()


def collect(cap, left_of, right_of, row_of, col_of, count, acts, dmod, ends, stats, times, conds, freq_low, label, own_pre, own_cond,
            row_master, tile_master):
    per = tile_master.shape[0]
    ch = next(n for n in (2, 1) if cap % n == 0)
    chunks = cap // ch
    images = GROUPS * SHARDS
    vmem = pl.BlockSpec(memory_space=pltpu.VMEM)
    smem = pl.BlockSpec(memory_space=pltpu.SMEM)
    anywhere = pl.BlockSpec(memory_space=pl.ANY)
    small = 9 + 6 * (SHARDS - 1)
    dma = pltpu.SemaphoreType.DMA

    def blocks(*lead):
        return pltpu.VMEM(lead + (BLK, BLK), bf16)

    return pl.pallas_call(
        functools.partial(collect_body, cap, ch),
        out_shape=[
            jax.ShapeDtypeStruct((per, BLK, BLK), bf16),
            jax.ShapeDtypeStruct((6 * NB, images, BLK), bf16),
            jax.ShapeDtypeStruct(row_master.shape, f32),
            jax.ShapeDtypeStruct((8, 128), f32),
            jax.ShapeDtypeStruct((8, 128), f32),
        ],
        in_specs=[smem] * 5 + [vmem] * 11 + [anywhere],
        out_specs=[anywhere] + [vmem] * 4,
        scratch_shapes=[
            blocks(RING, 4, ch),
            blocks(RING, 4, ch),
            blocks(RING, ch),
            blocks(RING, ch),
            blocks(RING, ch),
            pltpu.VMEM((RING, ch, BLK // 2, BLK), bf16),
            pltpu.VMEM((RING, ch, BLK // 2, BLK), bf16),
            blocks(RING, ch),
            blocks(RING, ch),
            blocks(cap),
            blocks(cap),
            blocks(cap),
            blocks(cap),
            pltpu.VMEM((per // 3, BLK, BLK), f32),
            pltpu.VMEM((per, images, BLK), f32),
            pltpu.VMEM((images * 8 * LANES, 128), bf16),
            pltpu.VMEM((images * 8 * LANES, 128), f32),
            pltpu.VMEM((images * 8, 128), f32),
            pltpu.VMEM((SHARDS, TOKEN_ROWS, 128), f32),
            pltpu.VMEM((GROUPS, TOKEN_ROWS, 128), f32),
            pltpu.VMEM((TOKEN_ROWS, 128), f32),
            pltpu.VMEM((SHARDS, images, 128), f32),
            pltpu.VMEM((SHARDS, images, 128), f32),
            pltpu.VMEM((SHARDS, images, 128), f32),
            pltpu.VMEM((SHARDS, images, 128), f32),
            pltpu.VMEM((images, 128), f32),
            pltpu.VMEM((images, 128), f32),
            pltpu.VMEM((24, 128), f32),
            pltpu.VMEM((8, BLK), f32),
            pltpu.VMEM((SHARDS, 8, 128), f32),
            dma((RING, 4)),
            dma((RING, 4)),
            dma((RING, 2)),
            dma((RING,)),
            dma((RING,)),
            dma((RING,)),
            dma((RING,)),
            dma((RING,)),
            dma((RING,)),
            dma((chunks,)),
            dma((chunks,)),
            dma((chunks,)),
            dma((chunks,)),
            dma((2, chunks)),
            dma((chunks,)),
            dma,
            dma((small,)),
            dma((small,)),
        ],
        compiler_params=pltpu.CompilerParams(
            collective_id=100 + cap, has_side_effects=True, vmem_limit_bytes=61 << 20
        ),
        name="collect",
    )(left_of, right_of, row_of, col_of, count, acts, dmod, ends, stats, times, conds, freq_low, label, own_pre, own_cond,
      row_master, tile_master)


def positions(grid_side, model_width):
    index = jnp.arange(grid_side * grid_side)
    row_pos = (index // grid_side).astype(f32)
    col_pos = (index % grid_side).astype(f32)
    quarter = model_width // 4
    omega = 1.0 / 10000.0 ** (jnp.arange(quarter, dtype=f32) / quarter)
    row_arg = row_pos[:, None] * omega[None, :]
    col_arg = col_pos[:, None] * omega[None, :]
    return jnp.concatenate([jnp.sin(row_arg), jnp.cos(row_arg), jnp.sin(col_arg), jnp.cos(col_arg)], axis=1)


def time_freq(step_values, freq_width):
    half_width = freq_width // 2
    freqs = jnp.exp(-math.log(10000.0) * jnp.arange(half_width, dtype=f32) / half_width)
    angle_arg = step_values.astype(f32)[:, None] * freqs[None, :]
    return jnp.concatenate([jnp.cos(angle_arg), jnp.sin(angle_arg)], axis=1)


def silu_slope(value):
    gate = jax.nn.sigmoid(value)
    return gate * (1.0 + value * (1.0 - gate))


def blocked(array):
    count = array.shape[0]
    return array.reshape(count, -1, BLK).transpose(1, 0, 2)


def factors_of(assign):
    n = jnp.maximum(assign - ADA, 0)
    out, up, down = n - AT_OUT, n - AT_UP, n - AT_DOWN
    left = jnp.where(
        n < AT_OUT,
        L_ATT + n // QB,
        jnp.where(n < AT_UP, L_OUT + out // NB, jnp.where(n < AT_DOWN, L_MLP + up // HB, L_HID + down // NB)),
    )
    right = jnp.where(
        n < AT_OUT,
        R_QKV + n % QB,
        jnp.where(n < AT_UP, R_OUT + out % NB, jnp.where(n < AT_DOWN, R_UP + up % HB, R_DOWN + down % NB)),
    )
    return left.astype(jnp.int32), right.astype(jnp.int32)


def spread_plain(slot_of, row_of, col_of, tile_master, row_master, timesteps, labels):
    shard_count = lax.axis_size("shard")
    everyone = ("grp", "shard")
    me = lax.axis_index("shard")
    per, columns = tile_master.shape[0], row_master.shape[1]
    low_rows = row_master.astype(bf16)
    at = [0]

    def take(count):
        at[0] += count
        return low_rows[at[0] - count : at[0]]

    table, w_time1, w_time2 = take(NCLASS), take(FREQ), take(D)
    w_final = (take(D), take(D))
    take(2 * PATCH_DIM)
    take(1)
    b_time1, b_time2 = take(1), take(1)
    take(4)
    b_ada = take(6)
    take(FF // D)
    b_final = take(2)
    b_mod = jnp.concatenate([b_ada, b_final], axis=0)

    packed = pack_tiles(slot_of, tile_master)
    gathered = lax.all_gather(packed, "shard", axis=0, tiled=True)
    near = lax.all_gather(low_rows[NEAR_START:], "shard", axis=1, tiled=True)
    near = jnp.pad(near, ((0, NEAR - NEAR_REAL), (0, 0))).reshape(NEAR, LANES, 128).transpose(1, 0, 2)

    ids = lax.all_gather(jnp.concatenate([timesteps, labels]), everyone, axis=0)
    all_steps, all_labels = ids[:, 0], ids[:, 1]
    freq_low = time_freq(all_steps, FREQ).astype(bf16)
    own_pre = nn(freq_low, w_time1) + b_time1
    time_low = lax.all_gather(jax.nn.silu(own_pre).astype(bf16), "shard", axis=1, tiled=True)
    one_hot = (all_labels[:, None] == jnp.arange(NCLASS, dtype=jnp.int32)[None, :]).astype(bf16)
    own_cond = nn(time_low, w_time2) + b_time2 + nn(one_hot, table)
    cond_low = lax.all_gather(jax.nn.silu(own_cond).astype(bf16), "shard", axis=1, tiled=True)
    group_cond = lax.dynamic_slice(cond_low, (lax.axis_index("grp") * shard_count, 0), (shard_count, D))
    part_mod = ada_front(row_of, col_of, blocked(group_cond), tile_master)
    part_mod = part_mod.transpose(1, 0, 2).reshape(shard_count, 6, D)
    part_final = jnp.stack([nn(group_cond, w_final[0]), nn(group_cond, w_final[1])], axis=1)
    spread = jnp.zeros((shard_count, 8, D), f32)
    spread = lax.dynamic_update_slice(
        spread,
        jnp.concatenate([jnp.zeros((shard_count, 6, columns), f32), part_final], axis=1) + b_mod[None].astype(f32),
        (0, 0, me * columns),
    )
    spread = spread + jnp.concatenate([part_mod, jnp.zeros((shard_count, 2, D), f32)], axis=1)
    mods = lax.psum_scatter(spread, "shard", scatter_dimension=0, tiled=True)[0]
    label = jnp.broadcast_to(all_labels.astype(f32)[:, None], (all_labels.shape[0], 128))

    def lanes(array):
        return array.reshape(-1, LANES, 128).transpose(1, 0, 2)

    return (
        gathered, near, mods.reshape(8 * LANES, 128), freq_low, label, lanes(time_low), lanes(cond_low), own_pre, own_cond,
    )


def collect_plain(left_of, right_of, row_of, col_of, count, acts, dmod, ends, stats, times, conds, freq_low, label, own_pre, own_cond,
                  row_master, tile_master):
    everyone = ("grp", "shard")
    me = lax.axis_index("shard")
    columns = row_master.shape[1]
    low_rows = row_master.astype(bf16)
    w_time2 = low_rows[NCLASS + FREQ : NCLASS + FREQ + D]
    w_final = [low_rows[NCLASS + FREQ + (1 + i) * D : NCLASS + FREQ + (2 + i) * D] for i in range(2)]
    one_hot = (label[:, :1].astype(jnp.int32) == jnp.arange(NCLASS, dtype=jnp.int32)[None, :]).astype(bf16)
    time_low, cond_low = (array.transpose(1, 0, 2).reshape(-1, D) for array in (times, conds))
    partial = tile_grads(left_of, right_of, acts)
    own_tiles = lax.psum_scatter(partial, "shard", scatter_dimension=0, tiled=True)
    own_tiles = lax.psum(own_tiles, "grp")

    all_dmod = lax.all_gather(dmod.reshape(1, -1).astype(bf16), everyone, axis=0, tiled=True)
    dmod_blocks = blocked(all_dmod[:, : 6 * D])
    own_dmod = lax.dynamic_slice(all_dmod.reshape(-1, 8, D), (0, 0, me * columns), (all_dmod.shape[0], 8, columns))
    part_cond = ada_back(row_of, col_of, dmod_blocks, tile_master).transpose(1, 0, 2).reshape(-1, D)
    part_cond = part_cond + nt(own_dmod[:, 6], w_final[0]) + nt(own_dmod[:, 7], w_final[1])
    own_dcond = lax.psum_scatter(part_cond, "shard", scatter_dimension=1, tiled=True) * silu_slope(own_cond)
    dcond_low = own_dcond.astype(bf16)
    own_dpre = lax.psum_scatter(nt(dcond_low, w_time2), "shard", scatter_dimension=1, tiled=True)
    own_dpre = own_dpre * silu_slope(own_pre)
    wide_dmod = own_dmod.astype(f32)

    token_rows = ends.transpose(1, 0, 2).reshape(TOKEN_ROWS, D)
    token_rows = lax.psum_scatter(token_rows, "shard", scatter_dimension=1, tiled=True)
    token_rows = lax.psum(token_rows, "grp")
    own_rows = jnp.concatenate(
        [
            tn(one_hot.astype(f32), own_dcond),
            tn(freq_low, own_dpre.astype(bf16)),
            tn(time_low, dcond_low),
            tn(cond_low, own_dmod[:, 6]),
            tn(cond_low, own_dmod[:, 7]),
            token_rows[: T_PATCH + 1],
            jnp.sum(own_dpre, axis=0)[None],
            jnp.sum(own_dcond, axis=0)[None],
            token_rows[T_QUERY : T_VALUE + 1],
            token_rows[T_OUT : T_DOWN + 1],
            jnp.sum(wide_dmod[:, :6], axis=0),
            token_rows[T_UP:T_END],
            jnp.sum(wide_dmod[:, 6:], axis=0),
        ],
        axis=0,
    )
    whole_stats = lax.psum(stats[:4, 0], everyone)
    cond_gram = nt(cond_low, cond_low)
    dmod_gram = nt(all_dmod[:, : 6 * D], all_dmod[:, : 6 * D])
    counted = jnp.arange(own_tiles.shape[0], dtype=jnp.int32) < count
    wide_tiles = jnp.where(counted[:, None, None], own_tiles.astype(f32), 0.0)
    square_part = jnp.sum(wide_tiles * wide_tiles) + jnp.sum(own_rows * own_rows)
    square_sum = lax.psum(square_part, "shard") + jnp.sum(cond_gram * dmod_gram)
    return own_tiles, dmod_blocks, own_rows, square_sum, whole_stats


def pack_body(slot_ref, tile_ref, out_ref):
    out_ref[...] = tile_ref[...].astype(bf16)


def pack_tiles(slot_of, tile_master):
    per = tile_master.shape[0]
    return pl.pallas_call(
        pack_body,
        grid_spec=pltpu.PrefetchScalarGridSpec(
            num_scalar_prefetch=1,
            grid=(per,),
            in_specs=[pl.BlockSpec((1, BLK, BLK), lambda p, slots: (slots[p], 0, 0))],
            out_specs=pl.BlockSpec((1, BLK, BLK), lambda p, slots: (p, 0, 0)),
        ),
        out_shape=jax.ShapeDtypeStruct(tile_master.shape, bf16),
        name="pack_tiles",
    )(slot_of, tile_master)


def shards(
    patches, noise, timesteps, labels, assign, tile_master, tile_bases, tile_moment, tile_second,
    row_master, row_moment, row_second,
):
    group_count, shard_count = lax.axis_size("grp"), lax.axis_size("shard")
    everyone = ("grp", "shard")
    me = lax.axis_index("shard")
    per = tile_master.shape[0]
    columns = row_master.shape[1]
    token_total = patches.shape[0] * group_count * shard_count
    tile_total = assign.shape[0]

    slot_ids = jnp.arange(tile_total, dtype=jnp.int32)
    mine = lax.dynamic_slice(assign, (me * per,), (per,))
    row_of = jnp.where(mine < ADA, mine // (6 * NB), 0).astype(jnp.int32)
    col_of = jnp.where(mine < ADA, mine % (6 * NB), -1).astype(jnp.int32)
    owned = assign.reshape(-1, per)
    local = jnp.arange(per, dtype=jnp.int32)
    ahead = (owned[:, None, :] % tile_total < ADA).astype(jnp.int32) * per + local[None, None, :]
    behind = (owned[:, :, None] < ADA).astype(jnp.int32) * per + local[None, :, None]
    rank = jnp.sum((ahead < behind).astype(jnp.int32), axis=2)
    place = (rank + jnp.arange(owned.shape[0], dtype=jnp.int32)[:, None] * per).reshape(-1)
    ordered = jnp.sum(jnp.where(place[None, :] == slot_ids[:, None], assign[None, :], 0), axis=1)
    inverse = jnp.sum(jnp.where(assign[None, :] == slot_ids[:, None], place[None, :], 0), axis=1)
    rank = lax.dynamic_slice(rank, (me, 0), (1, per))[0]
    slot_of = jnp.sum(jnp.where(rank[None, :] == local[:, None], local[None, :], 0), axis=1)

    fast = group_count == GROUPS and shard_count == SHARDS
    if fast:
        freq = time_freq(timesteps, FREQ).reshape(2, 128)
        ids = jnp.concatenate([freq, jnp.broadcast_to(labels.astype(f32)[:, None], (1, 128)), jnp.zeros((5, 128), f32)], axis=0)
        gathered, near, mods, freq_low, label, times, conds, own_pre, own_cond = spread(
            per, slot_of, row_of, col_of, tile_master, row_master, ids
        )
        gathered = gathered.reshape(tile_total, BLK, BLK)
    else:
        gathered, near, mods, freq_low, label, times, conds, own_pre, own_cond = spread_plain(
            slot_of, row_of, col_of, tile_master, row_master, timesteps, labels
        )

    loss_scale = 1.0 / (token_total * PATCH_DIM)
    acts, dmod, ends, stats = block_step(
        inverse[ADA:], gathered, patches, noise, positions(LAT // PATCH_SIDE, D), near, mods.reshape(8 * LANES, 128),
        2.0 * loss_scale,
    )

    left_of, right_of = factors_of(ordered)
    count = jnp.sum((col_of < 0).astype(jnp.int32)).reshape(1)
    if fast:
        own_tiles, dmod_blocks, own_rows, squares, totals = collect(
            per, left_of, right_of, row_of, col_of, count, acts, dmod, ends, stats, times, conds, freq_low, label, own_pre,
            own_cond, row_master, tile_master,
        )
        square_sum, whole_stats = squares[0, 0], totals[:4, 0]
    else:
        own_tiles, dmod_blocks, own_rows, square_sum, whole_stats = collect_plain(
            left_of, right_of, row_of, col_of, count, acts, dmod, ends, stats, times, conds, freq_low, label, own_pre,
            own_cond, row_master, tile_master,
        )
    grad_norm = jnp.sqrt(square_sum)
    factor = clip_at / jnp.maximum(grad_norm, clip_at)

    images = conds.shape[1]
    cond_columns = conds.reshape(NB, 2, images, 128).transpose(0, 1, 3, 2).reshape(NB, BLK, images)
    new_tile_moment, new_tile_second, tile_update = adam(
        rank, row_of, col_of, factor.reshape(1), own_tiles, cond_columns, dmod_blocks,
        tile_bases, tile_moment, tile_second,
    )
    row_grad = factor * own_rows
    new_row_moment = beta_one * row_moment + (1.0 - beta_one) * row_grad
    new_row_second = beta_two * row_second + (1.0 - beta_two) * row_grad * row_grad
    row_update = -rate_step * (new_row_moment / (jnp.sqrt(new_row_second) + adam_eps) + decay_rate * row_master)
    loss = whole_stats[0] / (token_total * PATCH_DIM)
    act_rms = jnp.sqrt(whole_stats[1:] / (token_total * D))
    return (
        loss, grad_norm, act_rms, new_tile_moment, new_tile_second, tile_update, new_row_moment, new_row_second, row_update,
    )


def solution(mesh):
    placed = (
        P(("grp", "shard"), None),
        P(("grp", "shard"), None),
        P(("grp", "shard")),
        P(("grp", "shard")),
        P(),
        P("shard", None, None),
        P("shard", None, None, None),
        P("shard", None, None),
        P("shard", None, None),
        P(None, "shard"),
        P(None, "shard"),
        P(None, "shard"),
    )
    return jax.shard_map(
        shards,
        mesh=mesh,
        in_specs=placed,
        out_specs=(
            P(), P(), P(),
            P("shard", None, None), P("shard", None, None), P("shard", None, None),
            P(None, "shard"), P(None, "shard"), P(None, "shard"),
        ),
        check_vma=False,
    )
```

```python
import functools
import math

import jax
import jax.numpy as jnp
from jax import lax
from jax.experimental import pallas as pl
from jax.experimental.pallas import tpu as pltpu
from jax.sharding import PartitionSpec as P

D = 1024
HEADS = 16
HD = 64
FF = 4096
NCLASS = 1000
FREQ = 256
PATCH_SIDE = 2
LAT = 32
BLK = 256
PATCH_DIM = 16
SEQ = 256

NB = D // BLK
HB = FF // BLK
QB = 3 * NB
ADA = NB * 6 * NB
BIG = NB * QB + NB * NB + 2 * NB * HB
AT_QKV, AT_OUT, AT_UP, AT_DOWN = 0, NB * QB, NB * QB + NB * NB, NB * QB + NB * NB + NB * HB
L_ATT, L_OUT, L_MLP, L_HID = 0, NB, 2 * NB, 3 * NB
R_QKV = 3 * NB + HB
R_OUT = R_QKV + QB
R_UP = R_OUT + NB
R_DOWN = R_UP + HB
ACTS = R_DOWN + NB
B_OUT, B_UP, B_DOWN = QB, QB + NB, QB + NB + HB
ROW_STEP = 16
ADAM_GROUP = 3
LANES = D // 128
NEAR = 64
NEAR_START = NCLASS + FREQ + 3 * D
N_PATCH, N_TIME1, N_TIME2, N_QUERY, N_VALUE, N_OUT, N_DOWN, N_ADA = range(2 * PATCH_DIM, 2 * PATCH_DIM + 8)
N_UP = N_ADA + 6
N_FINAL = N_UP + FF // D
NEAR_REAL = N_FINAL + 2
T_PATCH, T_OUT, T_DOWN, T_QUERY, T_VALUE, T_UP = range(2 * PATCH_DIM, 2 * PATCH_DIM + 6)
T_END = T_UP + FF // D
TOKEN_ROWS = 48

CAPS = (28, 30)
GROUPS, SHARDS = 4, 8
MESH_ID = pl.DeviceIdType.MESH

ln_eps = 1e-06
beta_one = 0.5
beta_two = 0.5
adam_eps = 1e-08
rate_step = 0.01
decay_rate = 0.1
clip_at = 0.25

f32 = jnp.float32
bf16 = jnp.bfloat16


def nn(left, right):
    return lax.dot_general(left, right, (((1,), (0,)), ((), ())), preferred_element_type=f32)


def nt(left, right):
    return lax.dot_general(left, right, (((1,), (1,)), ((), ())), preferred_element_type=f32)


def tn(left, right):
    return lax.dot_general(left, right, (((0,), (0,)), ((), ())), preferred_element_type=f32)


def wide(ref, at, count=ROW_STEP):
    return jnp.concatenate([ref[r, pl.ds(at, count), :] for r in range(NB)], axis=1)


def put(ref, base, at, value, count=ROW_STEP):
    for r in range(NB):
        ref[base + r, pl.ds(at, count), :] = value[:, r * BLK : (r + 1) * BLK].astype(ref.dtype)


def fold(value):
    return jnp.sum(value.reshape(-1, 8, value.shape[-1]), axis=0)


def normed(value):
    centred = value - jnp.mean(value, axis=-1, keepdims=True)
    spread = jnp.mean(centred * centred, axis=-1, keepdims=True)
    back = lax.rsqrt(spread + ln_eps)
    return centred * back, back


def over_rows(body):
    def step(i, unused):
        body(pl.multiple_of(i * ROW_STEP, ROW_STEP))
        return unused

    lax.fori_loop(0, SEQ // ROW_STEP, step, 0)


def over(count, body):
    def step(i, unused):
        body(i)
        return unused

    lax.fori_loop(0, count, step, 0)


def norm_back(grad, value, scale):
    norm, back = normed(value)
    inner = grad * (1.0 + scale)
    mean_one = jnp.mean(inner, axis=-1, keepdims=True)
    mean_two = jnp.mean(inner * norm, axis=-1, keepdims=True)
    return norm, (inner - mean_one - norm * mean_two) * back


def gelu_pair(value):
    root = math.sqrt(2.0 / math.pi)
    square = value * value
    bend = jnp.tanh(root * (value + 0.044715 * value * square))
    half = 0.5 * (1.0 + bend)
    slope = half + 0.5 * value * (1.0 - bend * bend) * root * (1.0 + 3 * 0.044715 * square)
    return value * half, slope


def block_body(
    loss_factor, place_ref, tiles_ref, patches_ref, noise_ref, spot_ref, near_ref, mods_ref,
    acts_ref, dmod_ref, ends_ref, stats_ref,
    w_ref, stream, middle, last, out_att, out_mlp, low_in, low_att, qkv, hid, slope, probs, flow, sums,
    near_wide, bias_ref, mod_ref, dbias_ref, w_sem,
):
    att_scale = HD ** (-0.5)
    cuts = (AT_QKV, AT_OUT, AT_UP, AT_DOWN, BIG)

    def fetch(b, sem):
        pltpu.make_async_copy(tiles_ref.at[place_ref[b]], w_ref.at[b], w_sem.at[sem]).start()

    for m in range(4):
        over(cuts[m + 1] - cuts[m], lambda b, m=m: fetch(cuts[m] + b, m))

    def arrived(m):
        span = pl.ds(cuts[m], cuts[m + 1] - cuts[m])
        pltpu.make_async_copy(tiles_ref.at[pl.ds(0, cuts[m + 1] - cuts[m])], w_ref.at[span], w_sem.at[m]).wait()

    def mod(i):
        return mod_ref[i : i + 1, :]

    near_wide[...] = near_ref[...].astype(f32)

    def row_block(row, r):
        return jnp.concatenate([near_wide[2 * r, row : row + 1, :], near_wide[2 * r + 1, row : row + 1, :]], axis=1)

    def near_block(row, r):
        span = slice(row, row + PATCH_DIM)
        return jnp.concatenate([near_ref[2 * r, span, :], near_ref[2 * r + 1, span, :]], axis=1)

    for r in range(NB):
        bias_ref[r] = row_block(N_QUERY, r)
        bias_ref[NB + r] = jnp.zeros((1, BLK), f32)
        bias_ref[2 * NB + r] = row_block(N_VALUE, r)
        bias_ref[B_OUT + r] = row_block(N_OUT, r)
        bias_ref[B_DOWN + r] = row_block(N_DOWN, r)
        for i in range(FF // D):
            bias_ref[B_UP + i * NB + r] = row_block(N_UP + i, r)
    for i in range(8):
        mod_ref[i : i + 1, :] = jnp.concatenate([mods_ref[i * LANES + o : i * LANES + o + 1, :] for o in range(LANES)], axis=1)

    lane = lax.broadcasted_iota(jnp.int32, (SEQ, 128), 1)
    lower = lane < HD
    halves = (lower, jnp.logical_not(lower))

    def masked(value, side):
        return jnp.where(halves[side], value, jnp.zeros_like(value))

    sums[...] = jnp.zeros_like(sums)
    S_SQ_END, S_SQ_ATT, S_SQ_MLP = 0, 1, 2
    S_DSH_A, S_DSC_A, S_DG_A, S_DSH_M, S_DSC_M, S_DG_M, S_DSH_F, S_DSC_F = range(3, 11)
    S_PATCH, S_OUT, S_DOWN = 11, 12, 13

    def collect(which, value):
        sums[which] = sums[which] + fold(value)

    patches = patches_ref[...]
    side = LAT // PATCH_SIDE
    for r in range(NB):
        stream[r] = tn(patches, near_block(0, r)) + row_block(N_PATCH, r)
    for i in range(side):
        span = slice(i * side, (i + 1) * side)
        for r in range(2):
            stream[r, span, :] = stream[r, span, :] + spot_ref[r, i : i + 1, :]
            stream[2 + r, span, :] = stream[2 + r, span, :] + spot_ref[r]

    def modulate(source, scale, shift):
        def body(at):
            norm, _ = normed(wide(source, at))
            put(low_in, 0, at, norm * (1.0 + scale) + shift)

        over_rows(body)

    def transposed(base, ref, count):
        over(count, lambda r: acts_ref.__setitem__(base + r, ref[r].T))

    modulate(stream, mod(1), mod(0))
    transposed(L_ATT, low_in, NB)
    arrived(0)

    def qkv_step(c):
        total = nn(low_in[0], w_ref[AT_QKV + c])
        for r in range(1, NB):
            total += nn(low_in[r], w_ref[AT_QKV + r * QB + c])
        qkv[c] = (total + bias_ref[c]).astype(bf16)

    over(QB, qkv_step)

    def attend(c):
        for half in range(2):
            span = slice(half * 128, (half + 1) * 128)
            q, k, v = qkv[c, :, span], qkv[NB + c, :, span], qkv[2 * NB + c, :, span]
            parts = []
            for side in range(2):
                scores = nt(masked(q, side), k) * att_scale
                top = jnp.max(scores, axis=-1, keepdims=True)
                power = jnp.exp(scores - top)
                prob = power / jnp.sum(power, axis=-1, keepdims=True)
                probs[c * 4 + half * 2 + side] = prob
                parts.append(nn(prob.astype(bf16), v))
            low_att[c, :, span] = jnp.where(lower, parts[0], parts[1]).astype(bf16)

    over(NB, attend)
    transposed(L_OUT, low_att, NB)
    arrived(1)

    def out_step(c):
        total = nn(low_att[0], w_ref[AT_OUT + c])
        for r in range(1, NB):
            total += nn(low_att[r], w_ref[AT_OUT + r * NB + c])
        out_att[c] = total + bias_ref[B_OUT + c]

    over(NB, out_step)

    def mid_step(at):
        branch = mod(2) * wide(out_att, at)
        collect(S_SQ_ATT, branch * branch)
        value = wide(stream, at) + branch
        put(middle, 0, at, value)
        norm, _ = normed(value)
        put(low_in, 0, at, norm * (1.0 + mod(4)) + mod(3))

    over_rows(mid_step)
    transposed(L_MLP, low_in, NB)
    arrived(2)

    def up_step(c):
        total = nn(low_in[0], w_ref[AT_UP + c])
        for r in range(1, NB):
            total += nn(low_in[r], w_ref[AT_UP + r * HB + c])
        value, back = gelu_pair(total + bias_ref[B_UP + c])
        slope[c] = back
        low = value.astype(bf16)
        hid[c] = low
        acts_ref[L_HID + c] = low.T

    over(HB, up_step)
    arrived(3)

    def down_step(c):
        total = nn(hid[0], w_ref[AT_DOWN + c])
        for r in range(1, HB):
            total += nn(hid[r], w_ref[AT_DOWN + r * NB + c])
        out_mlp[c] = total + bias_ref[B_DOWN + c]

    over(NB, down_step)

    def end_step(at):
        branch = mod(5) * wide(out_mlp, at)
        collect(S_SQ_MLP, branch * branch)
        value = wide(middle, at) + branch
        collect(S_SQ_END, value * value)
        put(last, 0, at, value)
        norm, _ = normed(value)
        put(low_in, 0, at, norm * (1.0 + mod(7)) + mod(6))

    over_rows(end_step)
    predicted = nt(near_block(PATCH_DIM, 0), low_in[0])
    for r in range(1, NB):
        predicted += nt(near_block(PATCH_DIM, r), low_in[r])
    mismatch = predicted - noise_ref[...]
    loss_sum = jnp.sum(mismatch * mismatch)
    pred_low = (loss_factor * mismatch).astype(bf16)
    def put_rows(row, count, r, value):
        for i in range(2):
            ends_ref[2 * r + i, row : row + count, :] = value[:, i * 128 : (i + 1) * 128]

    for r in range(NB):
        put_rows(PATCH_DIM, PATCH_DIM, r, nn(pred_low, low_in[r]))
        flow[r] = tn(pred_low, near_block(PATCH_DIM, r))

    def end_back(at):
        grad = wide(flow, at)
        norm, value = norm_back(grad, wide(last, at), mod(7))
        collect(S_DSC_F, grad * norm)
        collect(S_DSH_F, grad)
        put(last, 0, at, value)
        collect(S_DG_M, value * wide(out_mlp, at))
        down = value * mod(5)
        collect(S_DOWN, down)
        put(acts_ref, R_DOWN, at, down)

    over_rows(end_back)

    def up_back(c):
        total = nt(acts_ref[R_DOWN], w_ref[AT_DOWN + c * NB])
        for j in range(1, NB):
            total += nt(acts_ref[R_DOWN + j], w_ref[AT_DOWN + c * NB + j])
        value = total * slope[c]
        dbias_ref[2 * NB + c] = jnp.sum(value, axis=0, keepdims=True)
        acts_ref[R_UP + c] = value.astype(bf16)

    over(HB, up_back)

    def mlp_back(r):
        total = nt(acts_ref[R_UP], w_ref[AT_UP + r * HB])
        for c in range(1, HB):
            total += nt(acts_ref[R_UP + c], w_ref[AT_UP + r * HB + c])
        flow[r] = total

    over(NB, mlp_back)

    def mid_back(at):
        grad = wide(flow, at)
        norm, value = norm_back(grad, wide(middle, at), mod(4))
        collect(S_DSC_M, grad * norm)
        collect(S_DSH_M, grad)
        value = value + wide(last, at)
        put(middle, 0, at, value)
        collect(S_DG_A, value * wide(out_att, at))
        proj = value * mod(2)
        collect(S_OUT, proj)
        put(acts_ref, R_OUT, at, proj)

    over_rows(mid_back)

    def att_back(r):
        total = nt(acts_ref[R_OUT], w_ref[AT_OUT + r * NB])
        for c in range(1, NB):
            total += nt(acts_ref[R_OUT + c], w_ref[AT_OUT + r * NB + c])
        low_att[r] = total.astype(bf16)

    over(NB, att_back)

    def attend_back(c):
        for half in range(2):
            span = slice(half * 128, (half + 1) * 128)
            q, k, v = qkv[c, :, span], qkv[NB + c, :, span], qkv[2 * NB + c, :, span]
            grad = low_att[c, :, span]
            found = []
            for side in range(2):
                prob = probs[c * 4 + half * 2 + side]
                dprob = nt(masked(grad, side), v)
                dvalue = tn(prob.astype(bf16), grad)
                dscore = prob * (dprob - jnp.sum(dprob * prob, axis=-1, keepdims=True))
                low = dscore.astype(bf16)
                found.append((nn(low, k) * att_scale, tn(low, q) * att_scale, dvalue))
            merged = [jnp.where(lower, one, two) for one, two in zip(*found)]
            for i in range(3):
                acts_ref[R_QKV + i * NB + c, :, span] = merged[i].astype(bf16)
            dbias_ref[c, :, span] = jnp.sum(merged[0], axis=0, keepdims=True)
            dbias_ref[NB + c, :, span] = jnp.sum(merged[2], axis=0, keepdims=True)

    over(NB, attend_back)

    def in_back(r):
        total = nt(acts_ref[R_QKV], w_ref[AT_QKV + r * QB])
        for c in range(1, QB):
            total += nt(acts_ref[R_QKV + c], w_ref[AT_QKV + r * QB + c])
        flow[r] = total

    over(NB, in_back)

    def first_back(at):
        grad = wide(flow, at)
        norm, value = norm_back(grad, wide(stream, at), mod(1))
        collect(S_DSC_A, grad * norm)
        collect(S_DSH_A, grad)
        value = value + wide(middle, at)
        collect(S_PATCH, value)
        put(low_in, 0, at, value)

    over_rows(first_back)
    for r in range(NB):
        put_rows(0, PATCH_DIM, r, nn(patches, low_in[r]))

    def total_of(which):
        return jnp.sum(sums[which], axis=0, keepdims=True)

    for i in range(8):
        value = total_of(S_DSH_A + i)
        for o in range(LANES):
            dmod_ref[i * LANES + o : i * LANES + o + 1, :] = value[:, o * 128 : (o + 1) * 128]
    for row, which in ((T_PATCH, S_PATCH), (T_OUT, S_OUT), (T_DOWN, S_DOWN)):
        value = total_of(which)
        for r in range(NB):
            put_rows(row, 1, r, value[:, r * BLK : (r + 1) * BLK])
    for r in range(NB):
        put_rows(T_QUERY, 1, r, dbias_ref[r])
        put_rows(T_VALUE, 1, r, dbias_ref[NB + r])
        for i in range(FF // D):
            put_rows(T_UP + i, 1, r, dbias_ref[2 * NB + i * NB + r])
    ends_ref[:, T_END:, :] = jnp.zeros((LANES, TOKEN_ROWS - T_END, 128), f32)
    row = lax.broadcasted_iota(jnp.int32, (8, 128), 0)
    found = jnp.where(row == 0, loss_sum, 0.0)
    for i in range(3):
        found = jnp.where(row == i + 1, jnp.sum(sums[i]), found)
    stats_ref[...] = found


def block_step(place, tiles, patches, noise, spots, near, mods, loss_factor):
    vmem = pl.BlockSpec(memory_space=pltpu.VMEM)
    macs = 3 * SEQ * BIG * BLK * BLK
    return pl.pallas_call(
        functools.partial(block_body, loss_factor),
        out_shape=[
            jax.ShapeDtypeStruct((ACTS, BLK, BLK), bf16),
            jax.ShapeDtypeStruct((8 * LANES, 128), f32),
            jax.ShapeDtypeStruct((LANES, TOKEN_ROWS, 128), f32),
            jax.ShapeDtypeStruct((8, 128), f32),
        ],
        in_specs=[pl.BlockSpec(memory_space=pltpu.SMEM), pl.BlockSpec(memory_space=pl.ANY)] + [vmem] * 5,
        out_specs=[vmem] * 4,
        scratch_shapes=[
            pltpu.VMEM((BIG, BLK, BLK), bf16),
            pltpu.VMEM((NB, SEQ, BLK), f32),
            pltpu.VMEM((NB, SEQ, BLK), f32),
            pltpu.VMEM((NB, SEQ, BLK), f32),
            pltpu.VMEM((NB, SEQ, BLK), f32),
            pltpu.VMEM((NB, SEQ, BLK), f32),
            pltpu.VMEM((NB, SEQ, BLK), bf16),
            pltpu.VMEM((NB, SEQ, BLK), bf16),
            pltpu.VMEM((QB, SEQ, BLK), bf16),
            pltpu.VMEM((HB, SEQ, BLK), bf16),
            pltpu.VMEM((HB, SEQ, BLK), f32),
            pltpu.VMEM((HEADS, SEQ, SEQ), f32),
            pltpu.VMEM((NB, SEQ, BLK), f32),
            pltpu.VMEM((14, 8, D), f32),
            pltpu.VMEM((LANES, NEAR, 128), f32),
            pltpu.VMEM((B_DOWN + NB, 1, BLK), f32),
            pltpu.VMEM((8, D), f32),
            pltpu.VMEM((2 * NB + HB, 1, BLK), f32),
            pltpu.SemaphoreType.DMA((4,)),
        ],
        compiler_params=pltpu.CompilerParams(vmem_limit_bytes=61 << 20),
        cost_estimate=pl.CostEstimate(flops=2 * macs, bytes_accessed=BIG * BLK * BLK * 4, transcendentals=0),
        name="block_step",
    )(place, tiles, patches, noise, spots, near, mods)


def ada_front_body(row_ref, col_ref, cond_ref, tile_ref, out_ref):
    s = pl.program_id(0)

    @pl.when(s == 0)
    def _():
        out_ref[...] = jnp.zeros_like(out_ref)

    @pl.when(col_ref[s] >= 0)
    def _():
        c = col_ref[s]
        out_ref[c] = out_ref[c] + nn(cond_ref[row_ref[s]], tile_ref[0].astype(bf16))


def ada_front(row_of, col_of, cond_blocks, tile_master):
    per, images = tile_master.shape[0], cond_blocks.shape[1]
    return pl.pallas_call(
        ada_front_body,
        grid_spec=pltpu.PrefetchScalarGridSpec(
            num_scalar_prefetch=2,
            grid=(per,),
            in_specs=[
                pl.BlockSpec(cond_blocks.shape, lambda s, r, c: (0, 0, 0)),
                pl.BlockSpec((1, BLK, BLK), lambda s, r, c: (s, 0, 0)),
            ],
            out_specs=pl.BlockSpec((6 * NB, images, BLK), lambda s, r, c: (0, 0, 0)),
        ),
        out_shape=jax.ShapeDtypeStruct((6 * NB, images, BLK), f32),
        name="ada_front",
    )(row_of, col_of, cond_blocks, tile_master)


def ada_back_body(row_ref, col_ref, dmod_ref, tile_ref, out_ref):
    s = pl.program_id(0)

    @pl.when(s == 0)
    def _():
        out_ref[...] = jnp.zeros_like(out_ref)

    @pl.when(col_ref[s] >= 0)
    def _():
        r = row_ref[s]
        out_ref[r] = out_ref[r] + nt(dmod_ref[col_ref[s]], tile_ref[0].astype(bf16))


def ada_back(row_of, col_of, dmod_blocks, tile_master):
    per, images = tile_master.shape[0], dmod_blocks.shape[1]
    return pl.pallas_call(
        ada_back_body,
        grid_spec=pltpu.PrefetchScalarGridSpec(
            num_scalar_prefetch=2,
            grid=(per,),
            in_specs=[
                pl.BlockSpec(dmod_blocks.shape, lambda s, r, c: (0, 0, 0)),
                pl.BlockSpec((1, BLK, BLK), lambda s, r, c: (s, 0, 0)),
            ],
            out_specs=pl.BlockSpec((NB, images, BLK), lambda s, r, c: (0, 0, 0)),
        ),
        out_shape=jax.ShapeDtypeStruct((NB, images, BLK), f32),
        name="ada_back",
    )(row_of, col_of, dmod_blocks, tile_master)


def tile_grad_body(left_ref, right_ref, acts_ref, out_ref):
    s = pl.program_id(0)
    out_ref[0] = nn(acts_ref[left_ref[s]], acts_ref[right_ref[s]]).astype(bf16)


def tile_grads(left_of, right_of, acts):
    count = left_of.shape[0]
    return pl.pallas_call(
        tile_grad_body,
        grid_spec=pltpu.PrefetchScalarGridSpec(
            num_scalar_prefetch=2,
            grid=(count,),
            in_specs=[pl.BlockSpec(acts.shape, lambda s, a, b: (0, 0, 0))],
            out_specs=pl.BlockSpec((1, BLK, BLK), lambda s, a, b: (s, 0, 0)),
        ),
        out_shape=jax.ShapeDtypeStruct((count, BLK, BLK), bf16),
        compiler_params=pltpu.CompilerParams(vmem_limit_bytes=40 << 20),
        name="tile_grads",
    )(left_of, right_of, acts)


def adam_body(
    group, where_ref, row_ref, col_ref,
    norm_ref, grads_ref, cond_ref, dmod_ref, bases_ref, moment_ref, second_ref, row_grad_ref, row_master_ref, row_moment_ref, row_second_ref,
    new_moment_ref, new_second_ref, update_ref, new_row_moment_ref, new_row_second_ref, row_update_ref,
):
    step = pl.program_id(0)
    factor = clip_at / jnp.maximum(jnp.sqrt(norm_ref[0:1, 0:1]), clip_at)

    def moved(moment, second, grad):
        new_moment = beta_one * moment + (1.0 - beta_one) * grad
        new_second = beta_two * second + (1.0 - beta_two) * grad * grad
        return new_moment, new_second, new_moment / (jnp.sqrt(new_second) + adam_eps)

    for j in range(group):
        s = step * group + j
        r, c = row_ref[s], col_ref[s]
        cond = jnp.concatenate([cond_ref[2 * r], cond_ref[2 * r + 1]], axis=1)
        thin = tn(cond, dmod_ref[jnp.maximum(c, 0)]).astype(bf16)
        grad = jnp.where(c >= 0, thin, grads_ref[where_ref[s]])
        left, right = bases_ref[j, 0].astype(bf16), bases_ref[j, 1].astype(bf16)
        turned = factor * tn(left, nn(grad, right).astype(bf16))
        moment, second, direction = moved(moment_ref[j], second_ref[j], turned)
        new_moment_ref[j] = moment
        new_second_ref[j] = second
        update_ref[j] = -rate_step * nt(nn(left, direction.astype(bf16)).astype(bf16), right)

    moment, second, direction = moved(row_moment_ref[...], row_second_ref[...], factor * row_grad_ref[...])
    new_row_moment_ref[...] = moment
    new_row_second_ref[...] = second
    row_update_ref[...] = -rate_step * (direction + decay_rate * row_master_ref[...])


def adam(where, row_of, col_of, norm, grads, conds, dmod_blocks, bases, moment, second, row_grad, row_master, row_moment, row_second):
    per = moment.shape[0]
    group = next(g for g in (ADAM_GROUP, 3, 2, 1) if per % g == 0)
    steps = per // group
    tile = pl.BlockSpec((group, BLK, BLK), lambda s, *_: (s, 0, 0))
    row_count, columns = row_master.shape
    row = pl.BlockSpec((-(-row_count // (8 * steps)) * 8, columns), lambda s, *_: (s, 0))

    def whole(array):
        return pl.BlockSpec(array.shape, lambda s, *_: (0,) * array.ndim)

    shape = jax.ShapeDtypeStruct(moment.shape, f32)
    row_shape = jax.ShapeDtypeStruct(row_master.shape, f32)
    return pl.pallas_call(
        functools.partial(adam_body, group),
        grid_spec=pltpu.PrefetchScalarGridSpec(
            num_scalar_prefetch=3,
            grid=(steps,),
            in_specs=[
                whole(norm),
                whole(grads),
                whole(conds),
                whole(dmod_blocks),
                pl.BlockSpec((group, 2, BLK, BLK), lambda s, *_: (s, 0, 0, 0)),
                tile,
                tile,
                row,
                row,
                row,
                row,
            ],
            out_specs=[tile] * 3 + [row] * 3,
        ),
        out_shape=[shape] * 3 + [row_shape] * 3,
        compiler_params=pltpu.CompilerParams(vmem_limit_bytes=61 << 20),
        name="adam",
    )(where, row_of, col_of, norm, grads, conds, dmod_blocks, bases, moment, second, row_grad, row_master, row_moment, row_second)


def spread_body(
    cap, n_third,
    slot_ref, row_ref, col_ref, tiles_ref, rows_ref, ids_ref,
    out_ref, near_ref, mods_ref, freq_ref, label_ref, time_ref, cond_ref, pre_ref, own_cond_ref,
    tile, pack, ids, near, times, conds, near_wide, cond_group, product, part, part_out, part_in,
    load_sem, keep_sem, send_sem, recv_sem, small_send, small_recv,
):
    z, s = lax.axis_index("grp"), lax.axis_index("shard")
    per = tile.shape[0]
    images = GROUPS * SHARDS
    third = cap // 3
    both = cap - 2 * third
    x_at, y_at, c_at, z_at = (z, s ^ 2), (z, s ^ 4), (z, s ^ 1), (z ^ 1, s)
    far_z = [(lax.rem(z + i, GROUPS), s) for i in range(1, GROUPS)]
    near_s = [(z, s ^ i) for i in range(1, SHARDS)]

    barrier = pltpu.get_barrier_semaphore()
    for peer in far_z + near_s:
        pl.semaphore_signal(barrier, inc=1, device_id=peer, device_id_type=MESH_ID)
    load = pltpu.make_async_copy(tiles_ref, tile, load_sem)
    load.start()

    def block_rows(index, count):
        return pl.ds(pl.multiple_of(index * count, count), count)

    ids[block_rows(s * GROUPS + z, 8), :] = ids_ref[...]
    near_wide[...] = jnp.zeros_like(near_wide)
    near_wide[: NEAR_REAL - 3, :] = rows_ref[NEAR_START : NEAR_START + NEAR_REAL - 3, :]
    near_wide[NEAR_REAL - 3 : NEAR_REAL, :] = rows_ref[NEAR_START + NEAR_REAL - 3 : NEAR_START + NEAR_REAL, :]
    near[s] = near_wide[...].astype(bf16)
    near_wide[...] = near_wide[...].astype(bf16).astype(f32)
    pl.semaphore_wait(barrier, len(far_z) + len(near_s))

    sent = []

    def push(src, dst, peer, index):
        copy = pltpu.make_async_remote_copy(
            src_ref=src, dst_ref=dst, send_sem=small_send.at[index], recv_sem=small_recv.at[index],
            device_id=peer, device_id_type=MESH_ID,
        )
        copy.start()
        sent.append(copy)
        return copy

    def to_group(stage, pairs):
        first = len(far_z) + stage * len(near_s)
        return [push(*pairs(peer[1]), peer, first + i) for i, peer in enumerate(near_s)]

    def got(copies):
        for copy in copies:
            copy.wait_recv()

    own_ids = ids.at[block_rows(s * GROUPS + z, 8)]
    id_far = [push(own_ids, own_ids, peer, i) for i, peer in enumerate(far_z)]
    near_copies = to_group(0, lambda p: (near.at[s], near.at[s]))

    parity = lax.rem(z, 2)
    starts = (both + parity * third, 0, both + third - parity * third)

    def chunk_of(index):
        kind, at = divmod(index, n_third)
        size = both if kind == 1 else third
        first, last = at * size // n_third, (at + 1) * size // n_third
        return starts[kind] + first, last - first

    def chunk(index):
        return pl.ds(*chunk_of(index))

    load.wait()
    big = []

    def send(kind, stream, index, peer, src, owner, arrives):
        copy = pltpu.make_async_remote_copy(
            src_ref=src, dst_ref=out_ref.at[owner, chunk(index)],
            send_sem=send_sem.at[kind, index], recv_sem=recv_sem.at[stream, arrives],
            device_id=peer, device_id_type=MESH_ID,
        )
        copy.start()
        big.append(copy)

    def wait_for(stream, index, owner):
        place = out_ref.at[owner, chunk(index)]
        pltpu.make_async_remote_copy(
            src_ref=place, dst_ref=place, send_sem=send_sem.at[0, index], recv_sem=recv_sem.at[stream, index],
            device_id=x_at, device_id_type=MESH_ID,
        ).wait_recv()

    def pack_chunk(index):
        start, count = chunk_of(index)

        def one(i, unused):
            p = start + i
            pack[p] = tile[slot_ref[p]].astype(bf16)
            return unused

        lax.fori_loop(0, count, one, 0)

    def send_mine(index):
        src = pack.at[chunk(index)]
        if index < 2 * n_third:
            send(0, 0, index, x_at, src, s, index)
            send(1, 1, index, y_at, src, s, index)
        send(2, 3, index, c_at, src, s, index)

    owners = (s ^ 2, s ^ 4, s ^ 6)

    def pass_on(which, index):
        owner = owners[which]
        wait_for(which, index, owner)
        here = out_ref.at[owner, chunk(index)]
        if index < 2 * n_third:
            if which == 0 and index % 2 == 0:
                send(6, 2, index, y_at, here, owner, index)
            if which == 1 and index % 2 == 1:
                send(7, 2, index, x_at, here, owner, index)
        if index < n_third:
            send(8 + which, which, index, z_at, here, owner, 2 * n_third + index)
        send(3 + which, 4 + which, index, c_at, here, owner, index)

    for j in range(n_third):
        pack_chunk(j)
        send_mine(j)
    got(id_far)
    span = block_rows(s, 8 * GROUPS)
    id_near = to_group(1, lambda p: (ids.at[span], ids.at[span]))
    for j in range(n_third, 3 * n_third):
        pack_chunk(j)
    keep = pltpu.make_async_copy(pack, out_ref.at[s, pl.ds(0, cap)], keep_sem)
    keep.start()
    stages = {}

    def silu_low(value):
        return (value * jax.nn.sigmoid(value)).astype(bf16)

    def row_slice(start, count):
        return rows_ref[start : start + count, :].astype(bf16)

    def time_stage():
        got(id_near)
        freq = jnp.concatenate([ids[pl.ds(i, images, stride=8), :] for i in range(2)], axis=1).astype(bf16)
        freq_ref[...] = freq
        label_ref[...] = ids[pl.ds(2, images, stride=8), :]
        pre = nn(freq, row_slice(NCLASS, FREQ)) + near_wide[N_TIME1 : N_TIME1 + 1, :]
        pre_ref[...] = pre
        times[s] = silu_low(pre)
        stages["time"] = to_group(2, lambda p: (times.at[s], times.at[s]))

    def cond_stage():
        got(stages["time"])
        total = jnp.zeros((images, 128), f32) + near_wide[N_TIME2 : N_TIME2 + 1, :]
        for o in range(SHARDS):
            total += nn(times[o], row_slice(NCLASS + FREQ + o * 128, 128))
        hot = label_ref[...].astype(jnp.int32)[:, :1] == lax.broadcasted_iota(jnp.int32, (images, D), 1)
        total += nn(hot.astype(bf16), row_slice(0, D))
        own_cond_ref[...] = total
        conds[s] = silu_low(total)
        stages["cond"] = to_group(3, lambda p: (conds.at[s], conds.at[s]))

    def group_stage():
        got(stages["cond"])
        at = lax.broadcasted_iota(jnp.int32, (SHARDS, images), 1)
        row = lax.broadcasted_iota(jnp.int32, (SHARDS, images), 0)
        pick = (at == row * GROUPS + z).astype(bf16)
        for o in range(SHARDS):
            half = o % 2
            cond_group[o // 2, :, half * 128 : (half + 1) * 128] = nn(pick, conds[o])

    def ada_stage(start, count):
        def one(j, unused):
            product[start + j] = nn(cond_group[row_ref[start + j]].astype(bf16), tile[start + j].astype(bf16))
            return unused

        lax.fori_loop(0, count, one, 0)

    def part_stage():
        part[...] = jnp.zeros_like(part)

        def column(c, unused):
            total = jnp.zeros((SHARDS, BLK), f32)
            for j in range(per):
                total += jnp.where(col_ref[j] == c, 1.0, 0.0) * product[j]
            for half in range(2):
                part[block_rows(2 * c + half, 8), :] = total[:, half * 128 : (half + 1) * 128]
            return unused

        lax.fori_loop(0, 6 * NB, column, 0)
        for i in range(6):
            place = block_rows(i * LANES + s, 8)
            part[place, :] = part[place, :] + near_wide[N_ADA + i : N_ADA + i + 1, :]
        for i in range(2):
            total = jnp.zeros((SHARDS, 128), f32) + near_wide[N_FINAL + i : N_FINAL + i + 1, :]
            for r in range(NB):
                weight = row_slice(NCLASS + FREQ + D + i * D + r * BLK, BLK)
                total += nn(cond_group[r].astype(bf16), weight)
            part[block_rows((6 + i) * LANES + s, 8), :] = total
        for o in range(SHARDS):
            part_out[o] = part[pl.ds(o, 8 * LANES, stride=8), :]
        part_in[s] = part_out[s]
        stages["part"] = to_group(4, lambda p: (part_out.at[p], part_in.at[s]))

    def mod_stage():
        got(stages["part"])
        total = part_in[0]
        for o in range(1, SHARDS):
            total += part_in[o]
        mods_ref[...] = total
        got(near_copies)
        near_ref[...] = near[...]
        time_ref[...] = times[...]
        cond_ref[...] = conds[...]

    cut = per // 3
    hooks = [
        (0.10, time_stage), (0.30, cond_stage), (0.50, group_stage), (0.55, lambda: ada_stage(0, cut)),
        (0.60, lambda: ada_stage(cut, cut)), (0.65, lambda: ada_stage(2 * cut, per - 2 * cut)), (0.70, part_stage), (2.0, mod_stage),
    ]
    seen = [0]
    steps = [0]

    def hook(last=False):
        steps[0] += 1
        while hooks and (last or steps[0] >= hooks[0][0] * 3 * n_third):
            hooks.pop(0)[1]()

    def z_next():
        order = [(w, 2 * n_third + j) for j in range(n_third) for w in (0, 1)]
        order += [(2, 2 * n_third + j) for j in range(n_third)]
        if seen[0] < len(order):
            pass_on(*order[seen[0]])
            seen[0] += 1

    for j in range(n_third):
        pass_on(0, j)
        pass_on(1, j)
        hook()
        if j:
            z_next()
    for j in range(n_third, 3 * n_third):
        send_mine(j)
    for j in range(n_third):
        pass_on(2, j)
        if j % 2:
            z_next()
            hook()
    for j in range(n_third, 2 * n_third):
        pass_on(0, j)
        pass_on(1, j)
        hook()
        z_next()
    for j in range(n_third, 2 * n_third):
        pass_on(2, j)
        if j % 2:
            z_next()
            hook()
    while seen[0] < 3 * n_third:
        z_next()
    hook(last=True)
    for index in range(3 * n_third):
        wait_for(3, index, s ^ 1)
        for which in range(3):
            wait_for(4 + which, index, owners[which] ^ 1)
    keep.wait()
    for copy in big + sent:
        copy.wait_send()


def spread(cap, slot_of, row_of, col_of, tile_master, row_master, ids):
    per = tile_master.shape[0]
    n_third = 5
    images = GROUPS * SHARDS
    vmem = pl.BlockSpec(memory_space=pltpu.VMEM)
    smem = pl.BlockSpec(memory_space=pltpu.SMEM)
    anywhere = pl.BlockSpec(memory_space=pl.ANY)
    small = (GROUPS - 1) + 5 * (SHARDS - 1)
    return pl.pallas_call(
        functools.partial(spread_body, cap, n_third),
        out_shape=[
            jax.ShapeDtypeStruct((SHARDS, per, BLK, BLK), bf16),
            jax.ShapeDtypeStruct((LANES, NEAR, 128), bf16),
            jax.ShapeDtypeStruct((8 * LANES, 128), f32),
            jax.ShapeDtypeStruct((images, FREQ), bf16),
            jax.ShapeDtypeStruct((images, 128), f32),
            jax.ShapeDtypeStruct((SHARDS, images, 128), bf16),
            jax.ShapeDtypeStruct((SHARDS, images, 128), bf16),
            jax.ShapeDtypeStruct((images, 128), f32),
            jax.ShapeDtypeStruct((images, 128), f32),
        ],
        in_specs=[smem] * 3 + [anywhere] + [vmem] * 2,
        out_specs=[anywhere] + [vmem] * 8,
        scratch_shapes=[
            pltpu.VMEM((per, BLK, BLK), f32),
            pltpu.VMEM((cap, BLK, BLK), bf16),
            pltpu.VMEM((images * 8, 128), f32),
            pltpu.VMEM((LANES, NEAR, 128), bf16),
            pltpu.VMEM((SHARDS, images, 128), bf16),
            pltpu.VMEM((SHARDS, images, 128), bf16),
            pltpu.VMEM((NEAR, 128), f32),
            pltpu.VMEM((NB, SHARDS, BLK), f32),
            pltpu.VMEM((per, SHARDS, BLK), f32),
            pltpu.VMEM((8 * LANES * 8, 128), f32),
            pltpu.VMEM((SHARDS, 8 * LANES, 128), f32),
            pltpu.VMEM((SHARDS, 8 * LANES, 128), f32),
            pltpu.SemaphoreType.DMA,
            pltpu.SemaphoreType.DMA,
            pltpu.SemaphoreType.DMA((11, 3 * n_third)),
            pltpu.SemaphoreType.DMA((7, 3 * n_third)),
            pltpu.SemaphoreType.DMA((small,)),
            pltpu.SemaphoreType.DMA((small,)),
        ],
        compiler_params=pltpu.CompilerParams(collective_id=cap, has_side_effects=True, vmem_limit_bytes=61 << 20),
        name="spread",
    )(slot_of, row_of, col_of, tile_master, row_master, ids)

RING = 4
Z_LAG = 5


def collect_body(
    cap, ch,
    left_ref, right_ref, row_ref, col_ref, count_ref,
    acts_ref, dmod_ref, ends_ref, stats_ref, time_ref, cond_ref, freq_ref, label_ref, pre_ref, own_cond_ref, rows_ref, tiles_ref,
    grads_ref, d_blocks_ref, own_rows_ref, norm_ref, stat_ref,
    out_c, in_c, out_d, out_x, out_y, in_dx, in_dy, in_x, in_y, total, low_in, high_in, final,
    tile, product, all_d, wide_d, all_stats, tok_in, tok_z, tokens, part_out, part_in, pre_out, pre_in, own_dcond, own_dpre,
    vectors, squares, square_in,
    c_send, c_recv, d_send, dx_recv, dy_recv, x_send, x_recv, y_send, y_recv, up_send, low_recv, high_recv, final_recv, down_send,
    keep_sem, load_sem, small_send, small_recv,
):
    z, s = lax.axis_index("grp"), lax.axis_index("shard")
    per = product.shape[0]
    images = GROUPS * SHARDS
    chunks = cap // ch
    x_at, y_at, c_at = (z, s ^ 2), (z, s ^ 4), (z, s ^ 1)
    far_z = [(lax.rem(z + i, GROUPS), s) for i in range(1, GROUPS)]
    near_s = [(z, s ^ i) for i in range(1, SHARDS)]
    half = BLK // 2
    upper, lower = pl.ds(0, half), pl.ds(half, half)

    barrier = pltpu.get_barrier_semaphore()
    for peer in far_z + near_s:
        pl.semaphore_signal(barrier, inc=1, device_id=peer, device_id_type=MESH_ID)

    def remote(src, dst, sent, received, peer):
        return pltpu.make_async_remote_copy(
            src_ref=src, dst_ref=dst, send_sem=sent, recv_sem=received, device_id=peer, device_id_type=MESH_ID
        )

    def block_rows(index, count):
        return pl.ds(pl.multiple_of(index * count, count), count)

    def far(stage, src, dst):
        return [
            remote(src, dst, small_send.at[stage * 3 + i], small_recv.at[stage * 3 + i], peer) for i, peer in enumerate(far_z)
        ]

    def group(stage, src_of, dst):
        first = 9 + stage * 7
        return [
            remote(src_of(peer[1]), dst, small_send.at[first + i], small_recv.at[first + i], peer)
            for i, peer in enumerate(near_s)
        ]

    own_d = all_d.at[block_rows(s * GROUPS + z, 8 * LANES)]
    own_stat = all_stats.at[block_rows(s * GROUPS + z, 8)]
    group_d = all_d.at[block_rows(s, 8 * LANES * GROUPS)]
    group_stat = all_stats.at[block_rows(s, 8 * GROUPS)]

    def small_copies(name):
        if name == "d_far":
            return far(0, own_d, own_d)
        if name == "stat_far":
            return far(1, own_stat, own_stat)
        if name == "tok_far":
            return far(2, tok_z.at[z], tok_z.at[z])
        if name == "tok":
            return group(0, lambda p: ends_ref.at[p], tok_in.at[s])
        if name == "d":
            return group(1, lambda p: group_d, group_d)
        if name == "stat":
            return group(2, lambda p: group_stat, group_stat)
        if name == "part":
            return group(3, lambda p: part_out.at[p], part_in.at[s])
        if name == "pre":
            return group(4, lambda p: pre_out.at[p], pre_in.at[s])
        return group(5, lambda p: square_in.at[s], square_in.at[s])

    def begin(*names):
        for name in names:
            for copy in small_copies(name):
                copy.start()

    def got(*names):
        for name in names:
            for copy in small_copies(name):
                copy.wait_recv()

    def load(part):
        count = tile.shape[0]
        return pltpu.make_async_copy(tiles_ref.at[pl.ds(part * count, count)], tile, load_sem)

    load(0).start()
    own_d[...] = dmod_ref[...].astype(bf16)
    own_stat[...] = stats_ref[...]
    tok_in[s] = ends_ref[s]
    squares[...] = jnp.zeros_like(squares)
    pl.semaphore_wait(barrier, len(far_z) + len(near_s))
    begin("d_far", "stat_far", "tok")

    def spread_stage():
        got("d_far", "stat_far")
        begin("d", "stat")
        got("tok")
        value = tok_in[0]
        for o in range(1, SHARDS):
            value += tok_in[o]
        tok_z[z] = value
        begin("tok_far")

    def order_stage():
        got("d", "stat", "tok_far")
        value = tok_z[0]
        for i in range(1, GROUPS):
            value += tok_z[i]
        tokens[...] = value
        value = all_stats[pl.ds(0, 8), :]
        for i in range(1, images):
            value += all_stats[pl.ds(8 * i, 8), :]
        stat_ref[...] = value

        def widen(i, unused):
            place = block_rows(i, 8 * LANES)
            wide_d[place, :] = all_d[place, :].astype(f32)
            return unused

        lax.fori_loop(0, images, widen, 0)
        for q in range(6 * LANES):
            d_blocks_ref[q // 2, :, (q % 2) * 128 : (q % 2 + 1) * 128] = wide_d[
                pl.ds(q, images, stride=8 * LANES), :
            ].astype(bf16)

    def own_columns(i):
        return wide_d[pl.ds(i * LANES + s, images, stride=8 * LANES), :]

    def ada_stage(part):
        count = tile.shape[0]
        load(part).wait()

        def one(j, unused):
            at = part * count + j
            product[at] = nt(d_blocks_ref[jnp.maximum(col_ref[at], 0)], tile[j].astype(bf16))
            return unused

        lax.fori_loop(0, count, one, 0)
        if (part + 1) * count < per:
            load(part + 1).start()

    def row_slice(start, count):
        return rows_ref[start : start + count, :].astype(bf16)

    final_at = NCLASS + FREQ + D

    def part_stage():
        for r in range(NB):
            value = jnp.zeros((images, BLK), f32)
            for i in range(2):
                value += nt(own_columns(6 + i).astype(bf16), row_slice(final_at + i * D + r * BLK, BLK))

            def add(j, value, r=r):
                chosen = jnp.logical_and(col_ref[j] >= 0, row_ref[j] == r)
                return value + jnp.where(chosen, 1.0, 0.0) * product[j]

            value = lax.fori_loop(0, per, add, value)
            for i in range(2):
                part_out[2 * r + i] = value[:, i * 128 : (i + 1) * 128]
        part_in[s] = part_out[s]
        begin("part")

    def slope(value):
        gate = jax.nn.sigmoid(value)
        return gate * (1.0 + value * (1.0 - gate))

    def cond_stage():
        got("part")
        value = part_in[0]
        for o in range(1, SHARDS):
            value += part_in[o]
        value = value * slope(own_cond_ref[...])
        own_dcond[...] = value
        for o in range(SHARDS):
            pre_out[o] = nt(value.astype(bf16), row_slice(NCLASS + FREQ + o * 128, 128))
        pre_in[s] = pre_out[s]
        begin("pre")

    def row_stage():
        got("pre")
        value = pre_in[0]
        for o in range(1, SHARDS):
            value += pre_in[o]
        value = value * slope(pre_ref[...])
        own_dpre[...] = value
        dpre_low, dcond = value.astype(bf16), own_dcond[...]
        dcond_low = dcond.astype(bf16)
        gathered = []

        def keep(start, value):
            own_rows_ref[start : start + value.shape[0], :] = value
            gathered.append(fold(value * value))

        hot = label_ref[...].astype(jnp.int32)[:, :1] == lax.broadcasted_iota(jnp.int32, (images, NCLASS), 1)
        keep(
            0,
            lax.dot_general(
                hot.astype(f32), dcond, (((0,), (0,)), ((), ())), preferred_element_type=f32, precision=lax.Precision.HIGHEST
            ),
        )
        keep(NCLASS, tn(freq_ref[...], dpre_low))
        for o in range(SHARDS):
            keep(NCLASS + FREQ + o * 128, tn(time_ref[o], dcond_low))
            for i in range(2):
                keep(final_at + i * D + o * 128, tn(cond_ref[o], own_columns(6 + i).astype(bf16)))
        keep(NEAR_START, tokens[: 2 * PATCH_DIM, :])

        vectors[...] = jnp.zeros_like(vectors)

        def vector(row, value):
            vectors[row : row + 1, :] = value

        vector(0, tokens[T_PATCH : T_PATCH + 1, :])
        vector(1, jnp.sum(value, axis=0, keepdims=True))
        vector(2, jnp.sum(dcond, axis=0, keepdims=True))
        vector(3, tokens[T_QUERY : T_QUERY + 1, :])
        vector(4, tokens[T_VALUE : T_VALUE + 1, :])
        vector(5, tokens[T_OUT : T_OUT + 1, :])
        vector(6, tokens[T_DOWN : T_DOWN + 1, :])
        for i in range(8):
            vector(7 + i if i < 6 else 7 + i + FF // D, jnp.sum(own_columns(i), axis=0, keepdims=True))
        for i in range(FF // D):
            vector(13 + i, tokens[T_UP + i : T_UP + i + 1, :])
        start = NEAR_START + 2 * PATCH_DIM
        rest = own_rows_ref.shape[0] - start
        whole = rest // 8 * 8
        own_rows_ref[start : start + whole, :] = vectors[:whole, :]
        own_rows_ref[start + whole : start + rest, :] = vectors[whole:rest, :]
        value = fold(vectors[...] * vectors[...])
        for piece in gathered:
            value += piece
        squares[:, :128] = squares[:, :128] + value

    def slot_of(i):
        return lax.rem(i + RING, RING)

    def block(owner, p):
        at = owner * per + p
        return nn(acts_ref[left_ref[at]], acts_ref[right_ref[at]])

    targets = (s ^ 6, s ^ 2, s ^ 4, s)

    def c_copy(slot, item):
        return remote(out_c.at[slot, item], in_c.at[slot, item], c_send.at[slot, item], c_recv.at[slot, item], c_at)

    def dx_copy(slot):
        return remote(out_d.at[slot, :, upper], in_dx.at[slot], d_send.at[slot, 0], dx_recv.at[slot], x_at)

    def dy_copy(slot):
        return remote(out_d.at[slot, :, lower], in_dy.at[slot], d_send.at[slot, 1], dy_recv.at[slot], y_at)

    def x_copy(slot):
        return remote(out_x.at[slot], in_x.at[slot], x_send.at[slot], x_recv.at[slot], x_at)

    def y_copy(slot):
        return remote(out_y.at[slot], in_y.at[slot], y_send.at[slot], y_recv.at[slot], y_at)

    def inside(i):
        return jnp.logical_and(i >= 0, i < chunks)

    def each(body):
        def one(c, unused):
            body(c)
            return unused

        lax.fori_loop(0, ch, one, 0)

    def for_sibling(n):
        slot = slot_of(n)
        for item in range(4):
            at = n + 1 if item == 0 else n

            @pl.when(inside(at))
            def _():
                def one(c):
                    out_c[slot, item, c] = block(targets[item] ^ 1, at * ch + c).astype(bf16)

                each(one)
                c_copy(slot, item).start()

    def for_owners(i):
        slot, before = slot_of(i), slot_of(i - 1)

        @pl.when(inside(i + 1))
        def _():
            c_copy(slot, 0).wait_recv()

            def one(c):
                value = block(targets[0], (i + 1) * ch + c) + in_c[slot, 0, c].astype(f32)
                out_d[slot, c] = value.astype(bf16)

            each(one)
            dx_copy(slot).start()
            dy_copy(slot).start()

        @pl.when(inside(i))
        def _():
            c_copy(slot, 1).wait_recv()
            dy_copy(before).wait_recv()

            def one(c):
                value = block(targets[1], i * ch + c) + in_c[slot, 1, c].astype(f32)
                out_x[slot, c, upper] = value[:half].astype(bf16)
                out_x[slot, c, lower] = (value[half:] + in_dy[before, c].astype(f32)).astype(bf16)

            each(one)
            x_copy(slot).start()
            c_copy(slot, 2).wait_recv()
            dx_copy(before).wait_recv()

            def two(c):
                value = block(targets[2], i * ch + c) + in_c[slot, 2, c].astype(f32)
                out_y[slot, c, upper] = (value[:half] + in_dx[before, c].astype(f32)).astype(bf16)
                out_y[slot, c, lower] = value[half:].astype(bf16)

            each(two)
            y_copy(slot).start()
            c_copy(slot, 3).wait_recv()

            def three(c):
                value = block(targets[3], i * ch + c) + in_c[slot, 3, c].astype(f32)
                total[i * ch + c] = value.astype(bf16)

            each(three)

        @pl.when(inside(i - 1))
        def _():
            x_copy(before).wait_recv()
            y_copy(before).wait_recv()

            def one(c):
                at = (i - 1) * ch + c
                value = total[at].astype(f32) + in_x[before, c].astype(f32) + in_y[before, c].astype(f32)
                total[at] = value.astype(bf16)

            each(one)

    def along(j):
        even = lax.rem(j, 2) == 0
        rank = jnp.where(even, z, GROUPS - 1 - z)
        down = jnp.where(even, lax.rem(z + GROUPS - 1, GROUPS), lax.rem(z + 1, GROUPS))
        up = jnp.where(even, lax.rem(z + 1, GROUPS), lax.rem(z + GROUPS - 1, GROUPS))
        return rank, (down, s), (up, s)

    def z_copy(name, j):
        _, down, up = along(j)
        span = pl.ds(j * ch, ch)
        if name == "rise":
            return remote(total.at[span], low_in.at[span], up_send.at[j], low_recv.at[j], up)
        if name == "sink":
            return remote(total.at[span], high_in.at[span], up_send.at[j], high_recv.at[j], down)
        if name == "final_down":
            return remote(final.at[span], final.at[span], down_send.at[0, j], final_recv.at[j], down)
        return remote(final.at[span], final.at[span], down_send.at[1, j], final_recv.at[j], up)

    def over_z(i):
        j = i - 1

        @pl.when(inside(j))
        def _():
            rank, _, _ = along(j)

            @pl.when(rank == 0)
            def _():
                z_copy("rise", j).start()

            @pl.when(rank == 3)
            def _():
                z_copy("sink", j).start()

        j2 = i - 2

        @pl.when(jnp.logical_and(inside(j2), along(j2)[0] == 2))
        def _():
            z_copy("sink", j2).wait_recv()

            def one(c):
                at = j2 * ch + c
                total[at] = (total[at].astype(f32) + high_in[at].astype(f32)).astype(bf16)

            each(one)
            z_copy("sink", j2).start()

        j3 = i - 3

        @pl.when(jnp.logical_and(inside(j3), along(j3)[0] == 1))
        def _():
            z_copy("rise", j3).wait_recv()
            z_copy("sink", j3).wait_recv()

            def one(c):
                at = j3 * ch + c
                value = total[at].astype(f32) + low_in[at].astype(f32) + high_in[at].astype(f32)
                final[at] = value.astype(bf16)

            each(one)
            z_copy("final_down", j3).start()
            z_copy("final_up", j3).start()

        j4 = i - 4

        @pl.when(jnp.logical_and(inside(j4), along(j4)[0] == 2))
        def _():
            z_copy("final_up", j4).wait_recv()
            z_copy("final_up", j4).start()

        j5 = i - Z_LAG

        @pl.when(inside(j5))
        def _():
            rank = along(j5)[0]

            @pl.when(jnp.logical_or(rank == 0, rank == 3))
            def _():
                z_copy("final_up", j5).wait_recv()

            span = pl.ds(j5 * ch, ch)
            pltpu.make_async_copy(final.at[span], grads_ref.at[span], keep_sem.at[j5]).start()

            def one(c):
                at = j5 * ch + c
                value = final[at].astype(f32) * jnp.where(at < count_ref[0], 1.0, 0.0)
                squares[...] = squares[...] + fold(value * value)

            each(one)

    def settle(i):
        n = i - 1
        slot = slot_of(n)
        for item in range(4):

            @pl.when(inside(n + 1 if item == 0 else n))
            def _():
                c_copy(slot, item).wait_send()

        n2 = i - 2
        slot2 = slot_of(n2)

        @pl.when(inside(n2 + 1))
        def _():
            dx_copy(slot2).wait_send()
            dy_copy(slot2).wait_send()

        @pl.when(inside(n2))
        def _():
            x_copy(slot2).wait_send()
            y_copy(slot2).wait_send()

    hooks = {
        0: spread_stage, 3: order_stage, 4: lambda: ada_stage(0), 5: lambda: ada_stage(1), 6: lambda: ada_stage(2),
        7: part_stage, 10: cond_stage, 13: row_stage,
    }

    for_sibling(-1)

    def iteration(step, unused):
        i = step - 1
        for_sibling(i + 1)
        for_owners(i)
        over_z(i)
        settle(i)
        for at, stage in hooks.items():
            pl.when(i == at)(stage)
        return unused

    lax.fori_loop(0, chunks + 1 + Z_LAG, iteration, 0)

    square_in[s] = jnp.zeros((8, 128), f32) + jnp.sum(squares[...])
    begin("square")

    cond_gram = jnp.zeros((images, images), f32)
    for o in range(SHARDS):
        cond_gram += nt(cond_ref[o], cond_ref[o])

    def gram(c, value):
        return value + nt(d_blocks_ref[c], d_blocks_ref[c])

    d_gram = lax.fori_loop(0, 6 * NB, gram, jnp.zeros((images, images), f32))
    got("square")
    value = square_in[0]
    for o in range(1, SHARDS):
        value += square_in[o]
    norm_ref[...] = value + jnp.sum(cond_gram * d_gram)

    def finish(j, unused):
        span = pl.ds(j * ch, ch)
        pltpu.make_async_copy(final.at[span], grads_ref.at[span], keep_sem.at[j]).wait()
        rank = along(j)[0]

        @pl.when(rank == 0)
        def _():
            z_copy("rise", j).wait_send()

        @pl.when(rank >= 2)
        def _():
            z_copy("sink", j).wait_send()

        @pl.when(rank == 1)
        def _():
            z_copy("final_down", j).wait_send()

        @pl.when(jnp.logical_or(rank == 1, rank == 2))
        def _():
            z_copy("final_up", j).wait_send()

        return unused

    lax.fori_loop(0, chunks, finish, 0)
    for name in ("d_far", "stat_far", "tok_far", "tok", "d", "stat", "part", "pre", "square"):
        for copy in small_copies(name):
            copy.wait_send()


def collect(cap, left_of, right_of, row_of, col_of, count, acts, dmod, ends, stats, times, conds, freq_low, label, own_pre, own_cond,
            row_master, tile_master):
    per = tile_master.shape[0]
    ch = next(n for n in (2, 1) if cap % n == 0)
    chunks = cap // ch
    images = GROUPS * SHARDS
    vmem = pl.BlockSpec(memory_space=pltpu.VMEM)
    smem = pl.BlockSpec(memory_space=pltpu.SMEM)
    anywhere = pl.BlockSpec(memory_space=pl.ANY)
    small = 9 + 6 * (SHARDS - 1)
    dma = pltpu.SemaphoreType.DMA

    def blocks(*lead):
        return pltpu.VMEM(lead + (BLK, BLK), bf16)

    return pl.pallas_call(
        functools.partial(collect_body, cap, ch),
        out_shape=[
            jax.ShapeDtypeStruct((per, BLK, BLK), bf16),
            jax.ShapeDtypeStruct((6 * NB, images, BLK), bf16),
            jax.ShapeDtypeStruct(row_master.shape, f32),
            jax.ShapeDtypeStruct((8, 128), f32),
            jax.ShapeDtypeStruct((8, 128), f32),
        ],
        in_specs=[smem] * 5 + [vmem] * 11 + [anywhere],
        out_specs=[anywhere] + [vmem] * 4,
        scratch_shapes=[
            blocks(RING, 4, ch),
            blocks(RING, 4, ch),
            blocks(RING, ch),
            blocks(RING, ch),
            blocks(RING, ch),
            pltpu.VMEM((RING, ch, BLK // 2, BLK), bf16),
            pltpu.VMEM((RING, ch, BLK // 2, BLK), bf16),
            blocks(RING, ch),
            blocks(RING, ch),
            blocks(cap),
            blocks(cap),
            blocks(cap),
            blocks(cap),
            pltpu.VMEM((per // 3, BLK, BLK), f32),
            pltpu.VMEM((per, images, BLK), f32),
            pltpu.VMEM((images * 8 * LANES, 128), bf16),
            pltpu.VMEM((images * 8 * LANES, 128), f32),
            pltpu.VMEM((images * 8, 128), f32),
            pltpu.VMEM((SHARDS, TOKEN_ROWS, 128), f32),
            pltpu.VMEM((GROUPS, TOKEN_ROWS, 128), f32),
            pltpu.VMEM((TOKEN_ROWS, 128), f32),
            pltpu.VMEM((SHARDS, images, 128), f32),
            pltpu.VMEM((SHARDS, images, 128), f32),
            pltpu.VMEM((SHARDS, images, 128), f32),
            pltpu.VMEM((SHARDS, images, 128), f32),
            pltpu.VMEM((images, 128), f32),
            pltpu.VMEM((images, 128), f32),
            pltpu.VMEM((24, 128), f32),
            pltpu.VMEM((8, BLK), f32),
            pltpu.VMEM((SHARDS, 8, 128), f32),
            dma((RING, 4)),
            dma((RING, 4)),
            dma((RING, 2)),
            dma((RING,)),
            dma((RING,)),
            dma((RING,)),
            dma((RING,)),
            dma((RING,)),
            dma((RING,)),
            dma((chunks,)),
            dma((chunks,)),
            dma((chunks,)),
            dma((chunks,)),
            dma((2, chunks)),
            dma((chunks,)),
            dma,
            dma((small,)),
            dma((small,)),
        ],
        compiler_params=pltpu.CompilerParams(
            collective_id=100 + cap, has_side_effects=True, vmem_limit_bytes=61 << 20
        ),
        name="collect",
    )(left_of, right_of, row_of, col_of, count, acts, dmod, ends, stats, times, conds, freq_low, label, own_pre, own_cond,
      row_master, tile_master)


def position_table(grid_side, model_width):
    quarter = model_width // 4
    omega = 1.0 / 10000.0 ** (jnp.arange(quarter, dtype=f32) / quarter)
    angle = jnp.arange(grid_side).astype(f32)[:, None] * omega[None, :]
    return jnp.stack([jnp.sin(angle), jnp.cos(angle)])


def time_freq(step_values, freq_width):
    half_width = freq_width // 2
    freqs = jnp.exp(-math.log(10000.0) * jnp.arange(half_width, dtype=f32) / half_width)
    angle_arg = step_values.astype(f32)[:, None] * freqs[None, :]
    return jnp.concatenate([jnp.cos(angle_arg), jnp.sin(angle_arg)], axis=1)


def silu_slope(value):
    gate = jax.nn.sigmoid(value)
    return gate * (1.0 + value * (1.0 - gate))


def blocked(array):
    count = array.shape[0]
    return array.reshape(count, -1, BLK).transpose(1, 0, 2)


def factors_of(assign):
    n = jnp.maximum(assign - ADA, 0)
    out, up, down = n - AT_OUT, n - AT_UP, n - AT_DOWN
    left = jnp.where(
        n < AT_OUT,
        L_ATT + n // QB,
        jnp.where(n < AT_UP, L_OUT + out // NB, jnp.where(n < AT_DOWN, L_MLP + up // HB, L_HID + down // NB)),
    )
    right = jnp.where(
        n < AT_OUT,
        R_QKV + n % QB,
        jnp.where(n < AT_UP, R_OUT + out % NB, jnp.where(n < AT_DOWN, R_UP + up % HB, R_DOWN + down % NB)),
    )
    return left.astype(jnp.int32), right.astype(jnp.int32)


def spread_plain(slot_of, row_of, col_of, tile_master, row_master, timesteps, labels):
    shard_count = lax.axis_size("shard")
    everyone = ("grp", "shard")
    me = lax.axis_index("shard")
    per, columns = tile_master.shape[0], row_master.shape[1]
    low_rows = row_master.astype(bf16)
    at = [0]

    def take(count):
        at[0] += count
        return low_rows[at[0] - count : at[0]]

    table, w_time1, w_time2 = take(NCLASS), take(FREQ), take(D)
    w_final = (take(D), take(D))
    take(2 * PATCH_DIM)
    take(1)
    b_time1, b_time2 = take(1), take(1)
    take(4)
    b_ada = take(6)
    take(FF // D)
    b_final = take(2)
    b_mod = jnp.concatenate([b_ada, b_final], axis=0)

    packed = pack_tiles(slot_of, tile_master)
    gathered = lax.all_gather(packed, "shard", axis=0, tiled=True)
    near = lax.all_gather(low_rows[NEAR_START:], "shard", axis=1, tiled=True)
    near = jnp.pad(near, ((0, NEAR - NEAR_REAL), (0, 0))).reshape(NEAR, LANES, 128).transpose(1, 0, 2)

    ids = lax.all_gather(jnp.concatenate([timesteps, labels]), everyone, axis=0)
    all_steps, all_labels = ids[:, 0], ids[:, 1]
    freq_low = time_freq(all_steps, FREQ).astype(bf16)
    own_pre = nn(freq_low, w_time1) + b_time1
    time_low = lax.all_gather(jax.nn.silu(own_pre).astype(bf16), "shard", axis=1, tiled=True)
    one_hot = (all_labels[:, None] == jnp.arange(NCLASS, dtype=jnp.int32)[None, :]).astype(bf16)
    own_cond = nn(time_low, w_time2) + b_time2 + nn(one_hot, table)
    cond_low = lax.all_gather(jax.nn.silu(own_cond).astype(bf16), "shard", axis=1, tiled=True)
    group_cond = lax.dynamic_slice(cond_low, (lax.axis_index("grp") * shard_count, 0), (shard_count, D))
    part_mod = ada_front(row_of, col_of, blocked(group_cond), tile_master)
    part_mod = part_mod.transpose(1, 0, 2).reshape(shard_count, 6, D)
    part_final = jnp.stack([nn(group_cond, w_final[0]), nn(group_cond, w_final[1])], axis=1)
    spread = jnp.zeros((shard_count, 8, D), f32)
    spread = lax.dynamic_update_slice(
        spread,
        jnp.concatenate([jnp.zeros((shard_count, 6, columns), f32), part_final], axis=1) + b_mod[None].astype(f32),
        (0, 0, me * columns),
    )
    spread = spread + jnp.concatenate([part_mod, jnp.zeros((shard_count, 2, D), f32)], axis=1)
    mods = lax.psum_scatter(spread, "shard", scatter_dimension=0, tiled=True)[0]
    label = jnp.broadcast_to(all_labels.astype(f32)[:, None], (all_labels.shape[0], 128))

    def lanes(array):
        return array.reshape(-1, LANES, 128).transpose(1, 0, 2)

    return (
        gathered, near, mods.reshape(8 * LANES, 128), freq_low, label, lanes(time_low), lanes(cond_low), own_pre, own_cond,
    )


def collect_plain(left_of, right_of, row_of, col_of, count, acts, dmod, ends, stats, times, conds, freq_low, label, own_pre, own_cond,
                  row_master, tile_master):
    everyone = ("grp", "shard")
    me = lax.axis_index("shard")
    columns = row_master.shape[1]
    low_rows = row_master.astype(bf16)
    w_time2 = low_rows[NCLASS + FREQ : NCLASS + FREQ + D]
    w_final = [low_rows[NCLASS + FREQ + (1 + i) * D : NCLASS + FREQ + (2 + i) * D] for i in range(2)]
    one_hot = (label[:, :1].astype(jnp.int32) == jnp.arange(NCLASS, dtype=jnp.int32)[None, :]).astype(bf16)
    time_low, cond_low = (array.transpose(1, 0, 2).reshape(-1, D) for array in (times, conds))
    partial = tile_grads(left_of, right_of, acts)
    own_tiles = lax.psum_scatter(partial, "shard", scatter_dimension=0, tiled=True)
    own_tiles = lax.psum(own_tiles, "grp")

    all_dmod = lax.all_gather(dmod.reshape(1, -1).astype(bf16), everyone, axis=0, tiled=True)
    dmod_blocks = blocked(all_dmod[:, : 6 * D])
    own_dmod = lax.dynamic_slice(all_dmod.reshape(-1, 8, D), (0, 0, me * columns), (all_dmod.shape[0], 8, columns))
    part_cond = ada_back(row_of, col_of, dmod_blocks, tile_master).transpose(1, 0, 2).reshape(-1, D)
    part_cond = part_cond + nt(own_dmod[:, 6], w_final[0]) + nt(own_dmod[:, 7], w_final[1])
    own_dcond = lax.psum_scatter(part_cond, "shard", scatter_dimension=1, tiled=True) * silu_slope(own_cond)
    dcond_low = own_dcond.astype(bf16)
    own_dpre = lax.psum_scatter(nt(dcond_low, w_time2), "shard", scatter_dimension=1, tiled=True)
    own_dpre = own_dpre * silu_slope(own_pre)
    wide_dmod = own_dmod.astype(f32)

    token_rows = ends.transpose(1, 0, 2).reshape(TOKEN_ROWS, D)
    token_rows = lax.psum_scatter(token_rows, "shard", scatter_dimension=1, tiled=True)
    token_rows = lax.psum(token_rows, "grp")
    own_rows = jnp.concatenate(
        [
            tn(one_hot.astype(f32), own_dcond),
            tn(freq_low, own_dpre.astype(bf16)),
            tn(time_low, dcond_low),
            tn(cond_low, own_dmod[:, 6]),
            tn(cond_low, own_dmod[:, 7]),
            token_rows[: T_PATCH + 1],
            jnp.sum(own_dpre, axis=0)[None],
            jnp.sum(own_dcond, axis=0)[None],
            token_rows[T_QUERY : T_VALUE + 1],
            token_rows[T_OUT : T_DOWN + 1],
            jnp.sum(wide_dmod[:, :6], axis=0),
            token_rows[T_UP:T_END],
            jnp.sum(wide_dmod[:, 6:], axis=0),
        ],
        axis=0,
    )
    whole_stats = lax.psum(stats[:4, 0], everyone)
    cond_gram = nt(cond_low, cond_low)
    dmod_gram = nt(all_dmod[:, : 6 * D], all_dmod[:, : 6 * D])
    counted = jnp.arange(own_tiles.shape[0], dtype=jnp.int32) < count
    wide_tiles = jnp.where(counted[:, None, None], own_tiles.astype(f32), 0.0)
    square_part = jnp.sum(wide_tiles * wide_tiles) + jnp.sum(own_rows * own_rows)
    square_sum = lax.psum(square_part, "shard") + jnp.sum(cond_gram * dmod_gram)
    return own_tiles, dmod_blocks, own_rows, jnp.broadcast_to(square_sum, (8, 128)), whole_stats


def pack_body(slot_ref, tile_ref, out_ref):
    out_ref[...] = tile_ref[...].astype(bf16)


def pack_tiles(slot_of, tile_master):
    per = tile_master.shape[0]
    return pl.pallas_call(
        pack_body,
        grid_spec=pltpu.PrefetchScalarGridSpec(
            num_scalar_prefetch=1,
            grid=(per,),
            in_specs=[pl.BlockSpec((1, BLK, BLK), lambda p, slots: (slots[p], 0, 0))],
            out_specs=pl.BlockSpec((1, BLK, BLK), lambda p, slots: (p, 0, 0)),
        ),
        out_shape=jax.ShapeDtypeStruct(tile_master.shape, bf16),
        name="pack_tiles",
    )(slot_of, tile_master)


def shards(
    patches, noise, timesteps, labels, assign, tile_master, tile_bases, tile_moment, tile_second,
    row_master, row_moment, row_second,
):
    group_count, shard_count = lax.axis_size("grp"), lax.axis_size("shard")
    everyone = ("grp", "shard")
    me = lax.axis_index("shard")
    per = tile_master.shape[0]
    columns = row_master.shape[1]
    token_total = patches.shape[0] * group_count * shard_count
    tile_total = assign.shape[0]

    slot_ids = jnp.arange(tile_total, dtype=jnp.int32)
    mine = lax.dynamic_slice(assign, (me * per,), (per,))
    row_of = jnp.where(mine < ADA, mine // (6 * NB), 0).astype(jnp.int32)
    col_of = jnp.where(mine < ADA, mine % (6 * NB), -1).astype(jnp.int32)
    owned = assign.reshape(-1, per)
    local = jnp.arange(per, dtype=jnp.int32)
    ahead = (owned[:, None, :] % tile_total < ADA).astype(jnp.int32) * per + local[None, None, :]
    behind = (owned[:, :, None] < ADA).astype(jnp.int32) * per + local[None, :, None]
    rank = jnp.sum((ahead < behind).astype(jnp.int32), axis=2)
    place = (rank + jnp.arange(owned.shape[0], dtype=jnp.int32)[:, None] * per).reshape(-1)
    ordered = jnp.sum(jnp.where(place[None, :] == slot_ids[:, None], assign[None, :], 0), axis=1)
    inverse = jnp.sum(jnp.where(assign[None, :] == slot_ids[:, None], place[None, :], 0), axis=1)
    rank = lax.dynamic_slice(rank, (me, 0), (1, per))[0]
    slot_of = jnp.sum(jnp.where(rank[None, :] == local[:, None], local[None, :], 0), axis=1)

    fast = group_count == GROUPS and shard_count == SHARDS
    if fast:
        freq = time_freq(timesteps, FREQ).reshape(2, 128)
        ids = jnp.concatenate([freq, jnp.broadcast_to(labels.astype(f32)[:, None], (1, 128)), jnp.zeros((5, 128), f32)], axis=0)
        most = jnp.max(jnp.sum((owned >= ADA).astype(jnp.int32), axis=1))
        tier = sum((most > cap).astype(jnp.int32) for cap in CAPS)
        gathered, near, mods, freq_low, label, times, conds, own_pre, own_cond = lax.switch(
            tier, [functools.partial(spread, cap) for cap in CAPS + (per,)], slot_of, row_of, col_of, tile_master, row_master, ids
        )
        gathered = gathered.reshape(tile_total, BLK, BLK)
    else:
        gathered, near, mods, freq_low, label, times, conds, own_pre, own_cond = spread_plain(
            slot_of, row_of, col_of, tile_master, row_master, timesteps, labels
        )

    loss_scale = 1.0 / (token_total * PATCH_DIM)
    acts, dmod, ends, stats = block_step(
        inverse[ADA:], gathered, patches.T, noise.T, position_table(LAT // PATCH_SIDE, D), near, mods.reshape(8 * LANES, 128),
        2.0 * loss_scale,
    )

    left_of, right_of = factors_of(ordered)
    count = jnp.sum((col_of < 0).astype(jnp.int32)).reshape(1)
    if fast:
        own_tiles, dmod_blocks, own_rows, squares, totals = lax.switch(
            tier, [functools.partial(collect, cap) for cap in CAPS + (per,)], left_of, right_of, row_of, col_of, count, acts, dmod, ends, stats, times, conds, freq_low, label, own_pre,
            own_cond, row_master, tile_master,
        )
        whole_stats = totals[:4, 0]
    else:
        own_tiles, dmod_blocks, own_rows, squares, whole_stats = collect_plain(
            left_of, right_of, row_of, col_of, count, acts, dmod, ends, stats, times, conds, freq_low, label, own_pre,
            own_cond, row_master, tile_master,
        )
    grad_norm = jnp.sqrt(squares[0, 0])
    new_tile_moment, new_tile_second, tile_update, new_row_moment, new_row_second, row_update = adam(
        rank, row_of, col_of, squares, own_tiles, conds, dmod_blocks, tile_bases, tile_moment, tile_second,
        own_rows, row_master, row_moment, row_second,
    )
    loss = whole_stats[0] / (token_total * PATCH_DIM)
    act_rms = jnp.sqrt(whole_stats[1:] / (token_total * D))
    return (
        loss, grad_norm, act_rms, new_tile_moment, new_tile_second, tile_update, new_row_moment, new_row_second, row_update,
    )


def solution(mesh):
    placed = (
        P(("grp", "shard"), None),
        P(("grp", "shard"), None),
        P(("grp", "shard")),
        P(("grp", "shard")),
        P(),
        P("shard", None, None),
        P("shard", None, None, None),
        P("shard", None, None),
        P("shard", None, None),
        P(None, "shard"),
        P(None, "shard"),
        P(None, "shard"),
    )
    return jax.shard_map(
        shards,
        mesh=mesh,
        in_specs=placed,
        out_specs=(
            P(), P(), P(),
            P("shard", None, None), P("shard", None, None), P("shard", None, None),
            P(None, "shard"), P(None, "shard"), P(None, "shard"),
        ),
        check_vma=False,
    )
```

```python
import functools
import math

import jax
import jax.numpy as jnp
from jax import lax
from jax.experimental import pallas as pl
from jax.experimental.pallas import tpu as pltpu
from jax.sharding import PartitionSpec as P

D = 1024
HEADS = 16
HD = 64
FF = 4096
NCLASS = 1000
FREQ = 256
PATCH_SIDE = 2
LAT = 32
BLK = 256
PATCH_DIM = 16
SEQ = 256

NB = D // BLK
HB = FF // BLK
QB = 3 * NB
ADA = NB * 6 * NB
BIG = NB * QB + NB * NB + 2 * NB * HB
AT_QKV, AT_OUT, AT_UP, AT_DOWN = 0, NB * QB, NB * QB + NB * NB, NB * QB + NB * NB + NB * HB
L_ATT, L_OUT, L_MLP, L_HID = 0, NB, 2 * NB, 3 * NB
R_QKV = 3 * NB + HB
R_OUT = R_QKV + QB
R_UP = R_OUT + NB
R_DOWN = R_UP + HB
ACTS = R_DOWN + NB
B_OUT, B_UP, B_DOWN = QB, QB + NB, QB + NB + HB
ROW_STEP = 128
ADAM_GROUP = 3
LANES = D // 128
NEAR = 64
NEAR_START = NCLASS + FREQ + 3 * D
N_PATCH, N_TIME1, N_TIME2, N_QUERY, N_VALUE, N_OUT, N_DOWN, N_ADA = range(2 * PATCH_DIM, 2 * PATCH_DIM + 8)
N_UP = N_ADA + 6
N_FINAL = N_UP + FF // D
NEAR_REAL = N_FINAL + 2
T_PATCH, T_OUT, T_DOWN, T_QUERY, T_VALUE, T_UP = range(2 * PATCH_DIM, 2 * PATCH_DIM + 6)
T_END = T_UP + FF // D
TOKEN_ROWS = 48

CAPS = (28, 30)
GROUPS, SHARDS = 4, 8
MESH_ID = pl.DeviceIdType.MESH

ln_eps = 1e-06
beta_one = 0.5
beta_two = 0.5
adam_eps = 1e-08
rate_step = 0.01
decay_rate = 0.1
clip_at = 0.25

f32 = jnp.float32
bf16 = jnp.bfloat16


def nn(left, right):
    return lax.dot_general(left, right, (((1,), (0,)), ((), ())), preferred_element_type=f32)


def nt(left, right):
    return lax.dot_general(left, right, (((1,), (1,)), ((), ())), preferred_element_type=f32)


def tn(left, right):
    return lax.dot_general(left, right, (((0,), (0,)), ((), ())), preferred_element_type=f32)


def wide(ref, at, count=ROW_STEP):
    return jnp.concatenate([ref[r, pl.ds(at, count), :] for r in range(NB)], axis=1)


def put(ref, base, at, value, count=ROW_STEP):
    for r in range(NB):
        ref[base + r, pl.ds(at, count), :] = value[:, r * BLK : (r + 1) * BLK].astype(ref.dtype)


def fold(value):
    return jnp.sum(value.reshape(-1, 8, value.shape[-1]), axis=0)


def normed(value):
    centred = value - jnp.mean(value, axis=-1, keepdims=True)
    spread = jnp.mean(centred * centred, axis=-1, keepdims=True)
    back = lax.rsqrt(spread + ln_eps)
    return centred * back, back


def over_rows(body):
    def step(i, unused):
        body(pl.multiple_of(i * ROW_STEP, ROW_STEP))
        return unused

    lax.fori_loop(0, SEQ // ROW_STEP, step, 0)


def over(count, body):
    def step(i, unused):
        body(i)
        return unused

    lax.fori_loop(0, count, step, 0)


def norm_back(grad, value, scale):
    norm, back = normed(value)
    inner = grad * (1.0 + scale)
    mean_one = jnp.mean(inner, axis=-1, keepdims=True)
    mean_two = jnp.mean(inner * norm, axis=-1, keepdims=True)
    return norm, (inner - mean_one - norm * mean_two) * back


def gelu_pair(value):
    root = math.sqrt(2.0 / math.pi)
    square = value * value
    bend = jnp.tanh(root * (value + 0.044715 * value * square))
    half = 0.5 * (1.0 + bend)
    slope = half + 0.5 * value * (1.0 - bend * bend) * root * (1.0 + 3 * 0.044715 * square)
    return value * half, slope


def block_body(
    loss_factor, place_ref, tiles_ref, patches_ref, noise_ref, spot_ref, near_ref, mods_ref,
    acts_ref, dmod_ref, ends_ref, stats_ref,
    w_ref, stream, middle, last, out_att, out_mlp, low_in, low_att, qkv, hid, slope, probs, flow, sums,
    near_wide, bias_ref, mod_ref, dbias_ref, w_sem,
):
    att_scale = HD ** (-0.5)
    cuts = (AT_QKV, AT_OUT, AT_UP, AT_DOWN, BIG)

    def fetch(b, sem):
        pltpu.make_async_copy(tiles_ref.at[place_ref[ADA + b]], w_ref.at[b], w_sem.at[sem]).start()

    for m in range(4):
        over(cuts[m + 1] - cuts[m], lambda b, m=m: fetch(cuts[m] + b, m))

    def arrived(m):
        span = pl.ds(cuts[m], cuts[m + 1] - cuts[m])
        pltpu.make_async_copy(tiles_ref.at[pl.ds(0, cuts[m + 1] - cuts[m])], w_ref.at[span], w_sem.at[m]).wait()

    def mod(i):
        return mod_ref[i : i + 1, :]

    near_wide[...] = near_ref[...].astype(f32)

    def row_block(row, r):
        return jnp.concatenate([near_wide[2 * r, row : row + 1, :], near_wide[2 * r + 1, row : row + 1, :]], axis=1)

    def near_block(row, r):
        span = slice(row, row + PATCH_DIM)
        return jnp.concatenate([near_ref[2 * r, span, :], near_ref[2 * r + 1, span, :]], axis=1)

    for r in range(NB):
        bias_ref[r] = row_block(N_QUERY, r)
        bias_ref[NB + r] = jnp.zeros((1, BLK), f32)
        bias_ref[2 * NB + r] = row_block(N_VALUE, r)
        bias_ref[B_OUT + r] = row_block(N_OUT, r)
        bias_ref[B_DOWN + r] = row_block(N_DOWN, r)
        for i in range(FF // D):
            bias_ref[B_UP + i * NB + r] = row_block(N_UP + i, r)
    for i in range(8):
        mod_ref[i : i + 1, :] = jnp.concatenate([mods_ref[i * LANES + o : i * LANES + o + 1, :] for o in range(LANES)], axis=1)

    lane = lax.broadcasted_iota(jnp.int32, (SEQ, 128), 1)
    lower = lane < HD
    halves = (lower, jnp.logical_not(lower))

    def masked(value, side):
        return jnp.where(halves[side], value, jnp.zeros_like(value))

    sums[...] = jnp.zeros_like(sums)
    S_SQ_END, S_SQ_ATT, S_SQ_MLP = 0, 1, 2
    S_DSH_A, S_DSC_A, S_DG_A, S_DSH_M, S_DSC_M, S_DG_M, S_DSH_F, S_DSC_F = range(3, 11)
    S_PATCH, S_OUT, S_DOWN = 11, 12, 13

    def collect(which, value):
        sums[which] = sums[which] + fold(value)

    patches = patches_ref[...]
    side = LAT // PATCH_SIDE
    for r in range(NB):
        stream[r] = tn(patches, near_block(0, r)) + row_block(N_PATCH, r)
    for i in range(side):
        span = slice(i * side, (i + 1) * side)
        for r in range(2):
            stream[r, span, :] = stream[r, span, :] + spot_ref[r, i : i + 1, :]
            stream[2 + r, span, :] = stream[2 + r, span, :] + spot_ref[r]

    def modulate(source, scale, shift):
        def body(at):
            norm, _ = normed(wide(source, at))
            put(low_in, 0, at, norm * (1.0 + scale) + shift)

        over_rows(body)

    def transposed(base, ref, count):
        over(count, lambda r: acts_ref.__setitem__(base + r, ref[r].T))

    modulate(stream, mod(1), mod(0))
    transposed(L_ATT, low_in, NB)
    arrived(0)

    def qkv_step(c):
        total = nn(low_in[0], w_ref[AT_QKV + c])
        for r in range(1, NB):
            total += nn(low_in[r], w_ref[AT_QKV + r * QB + c])
        qkv[c] = (total + bias_ref[c]).astype(bf16)

    over(QB, qkv_step)

    def attend(c):
        for half in range(2):
            span = slice(half * 128, (half + 1) * 128)
            q, k, v = qkv[c, :, span], qkv[NB + c, :, span], qkv[2 * NB + c, :, span]
            parts = []
            for side in range(2):
                scores = nt(masked(q, side), k) * att_scale
                top = jnp.max(scores, axis=-1, keepdims=True)
                power = jnp.exp(scores - top)
                prob = power / jnp.sum(power, axis=-1, keepdims=True)
                probs[c * 4 + half * 2 + side] = prob
                parts.append(nn(prob.astype(bf16), v))
            low_att[c, :, span] = jnp.where(lower, parts[0], parts[1]).astype(bf16)

    over(NB, attend)
    transposed(L_OUT, low_att, NB)
    arrived(1)

    def out_step(c):
        total = nn(low_att[0], w_ref[AT_OUT + c])
        for r in range(1, NB):
            total += nn(low_att[r], w_ref[AT_OUT + r * NB + c])
        out_att[c] = total + bias_ref[B_OUT + c]

    over(NB, out_step)

    def mid_step(at):
        branch = mod(2) * wide(out_att, at)
        collect(S_SQ_ATT, branch * branch)
        value = wide(stream, at) + branch
        put(middle, 0, at, value)
        norm, _ = normed(value)
        put(low_in, 0, at, norm * (1.0 + mod(4)) + mod(3))

    over_rows(mid_step)
    transposed(L_MLP, low_in, NB)
    arrived(2)

    def up_step(c):
        total = nn(low_in[0], w_ref[AT_UP + c])
        for r in range(1, NB):
            total += nn(low_in[r], w_ref[AT_UP + r * HB + c])
        value, back = gelu_pair(total + bias_ref[B_UP + c])
        slope[c] = back
        low = value.astype(bf16)
        hid[c] = low
        acts_ref[L_HID + c] = low.T

    over(HB, up_step)
    arrived(3)

    def down_step(c):
        total = nn(hid[0], w_ref[AT_DOWN + c])
        for r in range(1, HB):
            total += nn(hid[r], w_ref[AT_DOWN + r * NB + c])
        out_mlp[c] = total + bias_ref[B_DOWN + c]

    over(NB, down_step)

    def end_step(at):
        branch = mod(5) * wide(out_mlp, at)
        collect(S_SQ_MLP, branch * branch)
        value = wide(middle, at) + branch
        collect(S_SQ_END, value * value)
        put(last, 0, at, value)
        norm, _ = normed(value)
        put(low_in, 0, at, norm * (1.0 + mod(7)) + mod(6))

    over_rows(end_step)
    predicted = nt(near_block(PATCH_DIM, 0), low_in[0])
    for r in range(1, NB):
        predicted += nt(near_block(PATCH_DIM, r), low_in[r])
    mismatch = predicted - noise_ref[...]
    loss_sum = jnp.sum(mismatch * mismatch)
    pred_low = (loss_factor * mismatch).astype(bf16)
    def put_rows(row, count, r, value):
        for i in range(2):
            ends_ref[2 * r + i, row : row + count, :] = value[:, i * 128 : (i + 1) * 128]

    for r in range(NB):
        put_rows(PATCH_DIM, PATCH_DIM, r, nn(pred_low, low_in[r]))
        flow[r] = tn(pred_low, near_block(PATCH_DIM, r))

    def end_back(at):
        grad = wide(flow, at)
        norm, value = norm_back(grad, wide(last, at), mod(7))
        collect(S_DSC_F, grad * norm)
        collect(S_DSH_F, grad)
        put(last, 0, at, value)
        collect(S_DG_M, value * wide(out_mlp, at))
        down = value * mod(5)
        collect(S_DOWN, down)
        put(acts_ref, R_DOWN, at, down)

    over_rows(end_back)

    def up_back(c):
        total = nt(acts_ref[R_DOWN], w_ref[AT_DOWN + c * NB])
        for j in range(1, NB):
            total += nt(acts_ref[R_DOWN + j], w_ref[AT_DOWN + c * NB + j])
        value = total * slope[c]
        dbias_ref[2 * NB + c] = jnp.sum(value, axis=0, keepdims=True)
        acts_ref[R_UP + c] = value.astype(bf16)

    over(HB, up_back)

    def mlp_back(r):
        total = nt(acts_ref[R_UP], w_ref[AT_UP + r * HB])
        for c in range(1, HB):
            total += nt(acts_ref[R_UP + c], w_ref[AT_UP + r * HB + c])
        flow[r] = total

    over(NB, mlp_back)

    def mid_back(at):
        grad = wide(flow, at)
        norm, value = norm_back(grad, wide(middle, at), mod(4))
        collect(S_DSC_M, grad * norm)
        collect(S_DSH_M, grad)
        value = value + wide(last, at)
        put(middle, 0, at, value)
        collect(S_DG_A, value * wide(out_att, at))
        proj = value * mod(2)
        collect(S_OUT, proj)
        put(acts_ref, R_OUT, at, proj)

    over_rows(mid_back)

    def att_back(r):
        total = nt(acts_ref[R_OUT], w_ref[AT_OUT + r * NB])
        for c in range(1, NB):
            total += nt(acts_ref[R_OUT + c], w_ref[AT_OUT + r * NB + c])
        low_att[r] = total.astype(bf16)

    over(NB, att_back)

    def attend_back(c):
        for half in range(2):
            span = slice(half * 128, (half + 1) * 128)
            q, k, v = qkv[c, :, span], qkv[NB + c, :, span], qkv[2 * NB + c, :, span]
            grad = low_att[c, :, span]
            found = []
            for side in range(2):
                prob = probs[c * 4 + half * 2 + side]
                dprob = nt(masked(grad, side), v)
                dvalue = tn(prob.astype(bf16), grad)
                dscore = prob * (dprob - jnp.sum(dprob * prob, axis=-1, keepdims=True))
                low = dscore.astype(bf16)
                found.append((nn(low, k) * att_scale, tn(low, q) * att_scale, dvalue))
            merged = [jnp.where(lower, one, two) for one, two in zip(*found)]
            for i in range(3):
                acts_ref[R_QKV + i * NB + c, :, span] = merged[i].astype(bf16)
            dbias_ref[c, :, span] = jnp.sum(merged[0], axis=0, keepdims=True)
            dbias_ref[NB + c, :, span] = jnp.sum(merged[2], axis=0, keepdims=True)

    over(NB, attend_back)

    def in_back(r):
        total = nt(acts_ref[R_QKV], w_ref[AT_QKV + r * QB])
        for c in range(1, QB):
            total += nt(acts_ref[R_QKV + c], w_ref[AT_QKV + r * QB + c])
        flow[r] = total

    over(NB, in_back)

    def first_back(at):
        grad = wide(flow, at)
        norm, value = norm_back(grad, wide(stream, at), mod(1))
        collect(S_DSC_A, grad * norm)
        collect(S_DSH_A, grad)
        value = value + wide(middle, at)
        collect(S_PATCH, value)
        put(low_in, 0, at, value)

    over_rows(first_back)
    for r in range(NB):
        put_rows(0, PATCH_DIM, r, nn(patches, low_in[r]))

    def total_of(which):
        return jnp.sum(sums[which], axis=0, keepdims=True)

    for i in range(8):
        value = total_of(S_DSH_A + i)
        for o in range(LANES):
            dmod_ref[i * LANES + o : i * LANES + o + 1, :] = value[:, o * 128 : (o + 1) * 128]
    for row, which in ((T_PATCH, S_PATCH), (T_OUT, S_OUT), (T_DOWN, S_DOWN)):
        value = total_of(which)
        for r in range(NB):
            put_rows(row, 1, r, value[:, r * BLK : (r + 1) * BLK])
    for r in range(NB):
        put_rows(T_QUERY, 1, r, dbias_ref[r])
        put_rows(T_VALUE, 1, r, dbias_ref[NB + r])
        for i in range(FF // D):
            put_rows(T_UP + i, 1, r, dbias_ref[2 * NB + i * NB + r])
    ends_ref[:, T_END:, :] = jnp.zeros((LANES, TOKEN_ROWS - T_END, 128), f32)
    row = lax.broadcasted_iota(jnp.int32, (8, 128), 0)
    found = jnp.where(row == 0, loss_sum, 0.0)
    for i in range(3):
        found = jnp.where(row == i + 1, jnp.sum(sums[i]), found)
    stats_ref[...] = found


def block_step(place, tiles, patches, noise, spots, near, mods, loss_factor):
    vmem = pl.BlockSpec(memory_space=pltpu.VMEM)
    macs = 3 * SEQ * BIG * BLK * BLK
    return pl.pallas_call(
        functools.partial(block_body, loss_factor),
        out_shape=[
            jax.ShapeDtypeStruct((ACTS, BLK, BLK), bf16),
            jax.ShapeDtypeStruct((8 * LANES, 128), f32),
            jax.ShapeDtypeStruct((LANES, TOKEN_ROWS, 128), f32),
            jax.ShapeDtypeStruct((8, 128), f32),
        ],
        in_specs=[pl.BlockSpec(memory_space=pltpu.SMEM), pl.BlockSpec(memory_space=pl.ANY)] + [vmem] * 5,
        out_specs=[vmem] * 4,
        scratch_shapes=[
            pltpu.VMEM((BIG, BLK, BLK), bf16),
            pltpu.VMEM((NB, SEQ, BLK), f32),
            pltpu.VMEM((NB, SEQ, BLK), f32),
            pltpu.VMEM((NB, SEQ, BLK), f32),
            pltpu.VMEM((NB, SEQ, BLK), f32),
            pltpu.VMEM((NB, SEQ, BLK), f32),
            pltpu.VMEM((NB, SEQ, BLK), bf16),
            pltpu.VMEM((NB, SEQ, BLK), bf16),
            pltpu.VMEM((QB, SEQ, BLK), bf16),
            pltpu.VMEM((HB, SEQ, BLK), bf16),
            pltpu.VMEM((HB, SEQ, BLK), f32),
            pltpu.VMEM((HEADS, SEQ, SEQ), f32),
            pltpu.VMEM((NB, SEQ, BLK), f32),
            pltpu.VMEM((14, 8, D), f32),
            pltpu.VMEM((LANES, NEAR, 128), f32),
            pltpu.VMEM((B_DOWN + NB, 1, BLK), f32),
            pltpu.VMEM((8, D), f32),
            pltpu.VMEM((2 * NB + HB, 1, BLK), f32),
            pltpu.SemaphoreType.DMA((4,)),
        ],
        compiler_params=pltpu.CompilerParams(vmem_limit_bytes=54 << 20),
        cost_estimate=pl.CostEstimate(flops=2 * macs, bytes_accessed=BIG * BLK * BLK * 4, transcendentals=0),
        name="block_step",
    )(place, tiles, patches, noise, spots, near, mods)


def ada_front_body(row_ref, col_ref, cond_ref, tile_ref, out_ref):
    s = pl.program_id(0)

    @pl.when(s == 0)
    def _():
        out_ref[...] = jnp.zeros_like(out_ref)

    @pl.when(col_ref[s] >= 0)
    def _():
        c = col_ref[s]
        out_ref[c] = out_ref[c] + nn(cond_ref[row_ref[s]], tile_ref[0].astype(bf16))


def ada_front(row_of, col_of, cond_blocks, tile_master):
    per, images = tile_master.shape[0], cond_blocks.shape[1]
    return pl.pallas_call(
        ada_front_body,
        grid_spec=pltpu.PrefetchScalarGridSpec(
            num_scalar_prefetch=2,
            grid=(per,),
            in_specs=[
                pl.BlockSpec(cond_blocks.shape, lambda s, r, c: (0, 0, 0)),
                pl.BlockSpec((1, BLK, BLK), lambda s, r, c: (s, 0, 0)),
            ],
            out_specs=pl.BlockSpec((6 * NB, images, BLK), lambda s, r, c: (0, 0, 0)),
        ),
        out_shape=jax.ShapeDtypeStruct((6 * NB, images, BLK), f32),
        name="ada_front",
    )(row_of, col_of, cond_blocks, tile_master)


def ada_back_body(row_ref, col_ref, dmod_ref, tile_ref, out_ref):
    s = pl.program_id(0)

    @pl.when(s == 0)
    def _():
        out_ref[...] = jnp.zeros_like(out_ref)

    @pl.when(col_ref[s] >= 0)
    def _():
        r = row_ref[s]
        out_ref[r] = out_ref[r] + nt(dmod_ref[col_ref[s]], tile_ref[0].astype(bf16))


def ada_back(row_of, col_of, dmod_blocks, tile_master):
    per, images = tile_master.shape[0], dmod_blocks.shape[1]
    return pl.pallas_call(
        ada_back_body,
        grid_spec=pltpu.PrefetchScalarGridSpec(
            num_scalar_prefetch=2,
            grid=(per,),
            in_specs=[
                pl.BlockSpec(dmod_blocks.shape, lambda s, r, c: (0, 0, 0)),
                pl.BlockSpec((1, BLK, BLK), lambda s, r, c: (s, 0, 0)),
            ],
            out_specs=pl.BlockSpec((NB, images, BLK), lambda s, r, c: (0, 0, 0)),
        ),
        out_shape=jax.ShapeDtypeStruct((NB, images, BLK), f32),
        name="ada_back",
    )(row_of, col_of, dmod_blocks, tile_master)


def tile_grad_body(left_ref, right_ref, acts_ref, out_ref):
    s = pl.program_id(0)
    out_ref[0] = nn(acts_ref[left_ref[s]], acts_ref[right_ref[s]]).astype(bf16)


def tile_grads(left_of, right_of, acts):
    count = left_of.shape[0]
    return pl.pallas_call(
        tile_grad_body,
        grid_spec=pltpu.PrefetchScalarGridSpec(
            num_scalar_prefetch=2,
            grid=(count,),
            in_specs=[pl.BlockSpec(acts.shape, lambda s, a, b: (0, 0, 0))],
            out_specs=pl.BlockSpec((1, BLK, BLK), lambda s, a, b: (s, 0, 0)),
        ),
        out_shape=jax.ShapeDtypeStruct((count, BLK, BLK), bf16),
        compiler_params=pltpu.CompilerParams(vmem_limit_bytes=40 << 20),
        name="tile_grads",
    )(left_of, right_of, acts)


def adam_body(
    group, factors, where_ref, row_ref, col_ref,
    norm_ref, totals_ref, grads_ref, cond_ref, dmod_ref, bases_ref, moment_ref, second_ref, row_grad_ref, row_master_ref, row_moment_ref, row_second_ref,
    new_moment_ref, new_second_ref, update_ref, new_row_moment_ref, new_row_second_ref, row_update_ref,
    loss_ref, grad_norm_ref, act_rms_ref,
):
    step = pl.program_id(0)

    @pl.when(step == 0)
    def _():
        loss_ref[0] = totals_ref[0, 0] * factors[0]
        grad_norm_ref[0] = jnp.sqrt(norm_ref[...])[0, 0]
        roots = jnp.sqrt(totals_ref[...] * factors[1])
        for i in range(3):
            act_rms_ref[i] = roots[i + 1, 0]

    factor = clip_at / jnp.maximum(jnp.sqrt(norm_ref[0:1, 0:1]), clip_at)

    def moved(moment, second, grad):
        new_moment = beta_one * moment + (1.0 - beta_one) * grad
        new_second = beta_two * second + (1.0 - beta_two) * grad * grad
        return new_moment, new_second, new_moment / (jnp.sqrt(new_second) + adam_eps)

    for j in range(group):
        s = step * group + j
        r, c = row_ref[s], col_ref[s]
        cond = jnp.concatenate([cond_ref[2 * r], cond_ref[2 * r + 1]], axis=1)
        thin = tn(cond, dmod_ref[jnp.maximum(c, 0)]).astype(bf16)
        grad = jnp.where(c >= 0, thin, grads_ref[where_ref[s]])
        left, right = bases_ref[j, 0].astype(bf16), bases_ref[j, 1].astype(bf16)
        turned = factor * tn(left, nn(grad, right).astype(bf16))
        moment, second, direction = moved(moment_ref[j], second_ref[j], turned)
        new_moment_ref[j] = moment
        new_second_ref[j] = second
        update_ref[j] = -rate_step * nt(nn(left, direction.astype(bf16)).astype(bf16), right)

    moment, second, direction = moved(row_moment_ref[...], row_second_ref[...], factor * row_grad_ref[...])
    new_row_moment_ref[...] = moment
    new_row_second_ref[...] = second
    row_update_ref[...] = -rate_step * (direction + decay_rate * row_master_ref[...])


def adam(factors, where, row_of, col_of, norm, totals, grads, conds, dmod_blocks, bases, moment, second, row_grad, row_master, row_moment, row_second):
    per = moment.shape[0]
    group = next(g for g in (ADAM_GROUP, 3, 2, 1) if per % g == 0)
    steps = per // group
    tile = pl.BlockSpec((group, BLK, BLK), lambda s, *_: (s, 0, 0))
    row_count, columns = row_master.shape
    row = pl.BlockSpec((-(-row_count // (8 * steps)) * 8, columns), lambda s, *_: (s, 0))

    def whole(array):
        return pl.BlockSpec(array.shape, lambda s, *_: (0,) * array.ndim)

    shape = jax.ShapeDtypeStruct(moment.shape, f32)
    row_shape = jax.ShapeDtypeStruct(row_master.shape, f32)
    return pl.pallas_call(
        functools.partial(adam_body, group, factors),
        grid_spec=pltpu.PrefetchScalarGridSpec(
            num_scalar_prefetch=3,
            grid=(steps,),
            in_specs=[
                whole(norm),
                whole(totals),
                whole(grads),
                whole(conds),
                whole(dmod_blocks),
                pl.BlockSpec((group, 2, BLK, BLK), lambda s, *_: (s, 0, 0, 0)),
                tile,
                tile,
                row,
                row,
                row,
                row,
            ],
            out_specs=[tile] * 3 + [row] * 3 + [pl.BlockSpec(memory_space=pltpu.SMEM)] * 3,
        ),
        out_shape=[shape] * 3 + [row_shape] * 3 + [jax.ShapeDtypeStruct((n,), f32) for n in (1, 1, 3)],
        compiler_params=pltpu.CompilerParams(vmem_limit_bytes=61 << 20),
        name="adam",
    )(where, row_of, col_of, norm, totals, grads, conds, dmod_blocks, bases, moment, second, row_grad, row_master, row_moment, row_second)


def spread_body(
    cap, n_third,
    slot_ref, row_ref, col_ref, step_ref, name_ref, tiles_ref, rows_ref,
    out_ref, near_ref, mods_ref, freq_ref, label_ref, time_ref, cond_ref, pre_ref, own_cond_ref,
    tile, pack, ids, near, times, conds, near_wide, cond_group, product, part, part_out, part_in,
    load_sem, keep_sem, send_sem, recv_sem, small_send, small_recv,
):
    z, s = lax.axis_index("grp"), lax.axis_index("shard")
    per = tile.shape[0]
    images = GROUPS * SHARDS
    third = cap // 3
    both = cap - 2 * third
    x_at, y_at, c_at, z_at = (z, s ^ 2), (z, s ^ 4), (z, s ^ 1), (z ^ 1, s)
    far_z = [(lax.rem(z + i, GROUPS), s) for i in range(1, GROUPS)]
    near_s = [(z, s ^ i) for i in range(1, SHARDS)]

    barrier = pltpu.get_barrier_semaphore()
    for peer in far_z + near_s:
        pl.semaphore_signal(barrier, inc=1, device_id=peer, device_id_type=MESH_ID)
    load = pltpu.make_async_copy(tiles_ref, tile, load_sem)
    load.start()

    def block_rows(index, count):
        return pl.ds(pl.multiple_of(index * count, count), count)

    lane = lax.broadcasted_iota(jnp.int32, (8, 128), 1).astype(f32)
    angle = step_ref[0].astype(f32) * jnp.exp(-math.log(10000.0) * lane / (FREQ // 2))
    line = lax.broadcasted_iota(jnp.int32, (8, 128), 0)
    known = jnp.where(line == 0, jnp.cos(angle), jnp.where(line == 1, jnp.sin(angle), name_ref[0].astype(f32)))
    ids[block_rows(s * GROUPS + z, 8), :] = known
    near_wide[...] = jnp.zeros_like(near_wide)
    near_wide[: NEAR_REAL - 3, :] = rows_ref[NEAR_START : NEAR_START + NEAR_REAL - 3, :]
    near_wide[NEAR_REAL - 3 : NEAR_REAL, :] = rows_ref[NEAR_START + NEAR_REAL - 3 : NEAR_START + NEAR_REAL, :]
    near[s] = near_wide[...].astype(bf16)
    near_wide[...] = near_wide[...].astype(bf16).astype(f32)
    pl.semaphore_wait(barrier, len(far_z) + len(near_s))

    sent = []

    def push(src, dst, peer, index):
        copy = pltpu.make_async_remote_copy(
            src_ref=src, dst_ref=dst, send_sem=small_send.at[index], recv_sem=small_recv.at[index],
            device_id=peer, device_id_type=MESH_ID,
        )
        copy.start()
        sent.append(copy)
        return copy

    def to_group(stage, pairs):
        first = len(far_z) + stage * len(near_s)
        return [push(*pairs(peer[1]), peer, first + i) for i, peer in enumerate(near_s)]

    def got(copies):
        for copy in copies:
            copy.wait_recv()

    own_ids = ids.at[block_rows(s * GROUPS + z, 8)]
    id_far = [push(own_ids, own_ids, peer, i) for i, peer in enumerate(far_z)]
    near_copies = to_group(0, lambda p: (near.at[s], near.at[s]))

    parity = lax.rem(z, 2)
    starts = (both + parity * third, 0, both + third - parity * third)

    def chunk_of(index):
        kind, at = divmod(index, n_third)
        size = both if kind == 1 else third
        first, last = at * size // n_third, (at + 1) * size // n_third
        return starts[kind] + first, last - first

    def chunk(index):
        return pl.ds(*chunk_of(index))

    load.wait()
    big = []

    def send(kind, stream, index, peer, src, owner, arrives):
        copy = pltpu.make_async_remote_copy(
            src_ref=src, dst_ref=out_ref.at[owner, chunk(index)],
            send_sem=send_sem.at[kind, index], recv_sem=recv_sem.at[stream, arrives],
            device_id=peer, device_id_type=MESH_ID,
        )
        copy.start()
        big.append(copy)

    def wait_for(stream, index, owner):
        place = out_ref.at[owner, chunk(index)]
        pltpu.make_async_remote_copy(
            src_ref=place, dst_ref=place, send_sem=send_sem.at[0, index], recv_sem=recv_sem.at[stream, index],
            device_id=x_at, device_id_type=MESH_ID,
        ).wait_recv()

    def pack_chunk(index):
        start, count = chunk_of(index)

        def one(i, unused):
            p = start + i
            pack[p] = tile[slot_ref[p]].astype(bf16)
            return unused

        lax.fori_loop(0, count, one, 0)

    def send_mine(index):
        src = pack.at[chunk(index)]
        if index < 2 * n_third:
            send(0, 0, index, x_at, src, s, index)
            send(1, 1, index, y_at, src, s, index)
        send(2, 3, index, c_at, src, s, index)

    owners = (s ^ 2, s ^ 4, s ^ 6)

    def pass_on(which, index):
        owner = owners[which]
        wait_for(which, index, owner)
        here = out_ref.at[owner, chunk(index)]
        if index < 2 * n_third:
            if which == 0 and index % 2 == 0:
                send(6, 2, index, y_at, here, owner, index)
            if which == 1 and index % 2 == 1:
                send(7, 2, index, x_at, here, owner, index)
        if index < n_third:
            send(8 + which, which, index, z_at, here, owner, 2 * n_third + index)
        send(3 + which, 4 + which, index, c_at, here, owner, index)

    for j in range(n_third):
        pack_chunk(j)
        send_mine(j)
    got(id_far)
    span = block_rows(s, 8 * GROUPS)
    id_near = to_group(1, lambda p: (ids.at[span], ids.at[span]))
    for j in range(n_third, 3 * n_third):
        pack_chunk(j)
    keep = pltpu.make_async_copy(pack, out_ref.at[s, pl.ds(0, cap)], keep_sem)
    keep.start()
    stages = {}

    def silu_low(value):
        return (value * jax.nn.sigmoid(value)).astype(bf16)

    def row_slice(start, count):
        return rows_ref[start : start + count, :].astype(bf16)

    def time_stage():
        got(id_near)
        freq = jnp.concatenate([ids[pl.ds(i, images, stride=8), :] for i in range(2)], axis=1).astype(bf16)
        freq_ref[...] = freq
        label_ref[...] = ids[pl.ds(2, images, stride=8), :]
        pre = nn(freq, row_slice(NCLASS, FREQ)) + near_wide[N_TIME1 : N_TIME1 + 1, :]
        pre_ref[...] = pre
        times[s] = silu_low(pre)
        stages["time"] = to_group(2, lambda p: (times.at[s], times.at[s]))

    def cond_stage():
        got(stages["time"])
        total = jnp.zeros((images, 128), f32) + near_wide[N_TIME2 : N_TIME2 + 1, :]
        for o in range(SHARDS):
            total += nn(times[o], row_slice(NCLASS + FREQ + o * 128, 128))
        hot = label_ref[...].astype(jnp.int32)[:, :1] == lax.broadcasted_iota(jnp.int32, (images, D), 1)
        total += nn(hot.astype(bf16), row_slice(0, D))
        own_cond_ref[...] = total
        conds[s] = silu_low(total)
        stages["cond"] = to_group(3, lambda p: (conds.at[s], conds.at[s]))

    def group_stage():
        got(stages["cond"])
        at = lax.broadcasted_iota(jnp.int32, (SHARDS, images), 1)
        row = lax.broadcasted_iota(jnp.int32, (SHARDS, images), 0)
        pick = (at == row * GROUPS + z).astype(bf16)
        for o in range(SHARDS):
            half = o % 2
            cond_group[o // 2, :, half * 128 : (half + 1) * 128] = nn(pick, conds[o])

    def ada_stage(start, count):
        for j in range(start, start + count):
            product[j] = nn(cond_group[row_ref[j]].astype(bf16), tile[j].astype(bf16))

    def part_stage():
        part[...] = jnp.zeros_like(part)

        def column(c, unused):
            total = jnp.zeros((SHARDS, BLK), f32)
            for j in range(per):
                total += jnp.where(col_ref[j] == c, 1.0, 0.0) * product[j]
            for half in range(2):
                part[block_rows(2 * c + half, 8), :] = total[:, half * 128 : (half + 1) * 128]
            return unused

        lax.fori_loop(0, 6 * NB, column, 0)
        for i in range(6):
            place = block_rows(i * LANES + s, 8)
            part[place, :] = part[place, :] + near_wide[N_ADA + i : N_ADA + i + 1, :]
        for i in range(2):
            total = jnp.zeros((SHARDS, 128), f32) + near_wide[N_FINAL + i : N_FINAL + i + 1, :]
            for r in range(NB):
                weight = row_slice(NCLASS + FREQ + D + i * D + r * BLK, BLK)
                total += nn(cond_group[r].astype(bf16), weight)
            part[block_rows((6 + i) * LANES + s, 8), :] = total
        for o in range(SHARDS):
            part_out[o] = part[pl.ds(o, 8 * LANES, stride=8), :]
        part_in[s] = part_out[s]
        stages["part"] = to_group(4, lambda p: (part_out.at[p], part_in.at[s]))

    def mod_stage():
        got(stages["part"])
        total = part_in[0]
        for o in range(1, SHARDS):
            total += part_in[o]
        mods_ref[...] = total
        got(near_copies)
        near_ref[...] = near[...]
        time_ref[...] = times[...]
        cond_ref[...] = conds[...]

    cut = per // 3
    hooks = [
        (0.10, time_stage), (0.30, cond_stage), (0.50, group_stage), (0.55, lambda: ada_stage(0, cut)),
        (0.60, lambda: ada_stage(cut, cut)), (0.65, lambda: ada_stage(2 * cut, per - 2 * cut)), (0.70, part_stage), (2.0, mod_stage),
    ]
    seen = [0]
    steps = [0]

    def hook(last=False):
        steps[0] += 1
        while hooks and (last or steps[0] >= hooks[0][0] * 3 * n_third):
            hooks.pop(0)[1]()

    def z_next():
        order = [(w, 2 * n_third + j) for j in range(n_third) for w in (0, 1)]
        order += [(2, 2 * n_third + j) for j in range(n_third)]
        if seen[0] < len(order):
            pass_on(*order[seen[0]])
            seen[0] += 1

    for j in range(n_third):
        pass_on(0, j)
        pass_on(1, j)
        hook()
        if j:
            z_next()
    for j in range(n_third, 3 * n_third):
        send_mine(j)
    for j in range(n_third):
        pass_on(2, j)
        if j % 2:
            z_next()
            hook()
    for j in range(n_third, 2 * n_third):
        pass_on(0, j)
        pass_on(1, j)
        hook()
        z_next()
    for j in range(n_third, 2 * n_third):
        pass_on(2, j)
        if j % 2:
            z_next()
            hook()
    while seen[0] < 3 * n_third:
        z_next()
    hook(last=True)
    for index in range(3 * n_third):
        wait_for(3, index, s ^ 1)
        for which in range(3):
            wait_for(4 + which, index, owners[which] ^ 1)
    keep.wait()
    for copy in big + sent:
        copy.wait_send()


def spread(cap, slot_of, row_of, col_of, timesteps, labels, tile_master, row_master):
    per = tile_master.shape[0]
    n_third = 5
    images = GROUPS * SHARDS
    vmem = pl.BlockSpec(memory_space=pltpu.VMEM)
    smem = pl.BlockSpec(memory_space=pltpu.SMEM)
    anywhere = pl.BlockSpec(memory_space=pl.ANY)
    small = (GROUPS - 1) + 5 * (SHARDS - 1)
    return pl.pallas_call(
        functools.partial(spread_body, cap, n_third),
        out_shape=[
            jax.ShapeDtypeStruct((SHARDS, per, BLK, BLK), bf16),
            jax.ShapeDtypeStruct((LANES, NEAR, 128), bf16),
            jax.ShapeDtypeStruct((8 * LANES, 128), f32),
            jax.ShapeDtypeStruct((images, FREQ), bf16),
            jax.ShapeDtypeStruct((images, 128), f32),
            jax.ShapeDtypeStruct((SHARDS, images, 128), bf16),
            jax.ShapeDtypeStruct((SHARDS, images, 128), bf16),
            jax.ShapeDtypeStruct((images, 128), f32),
            jax.ShapeDtypeStruct((images, 128), f32),
        ],
        in_specs=[smem] * 5 + [anywhere, vmem],
        out_specs=[anywhere] + [vmem] * 8,
        scratch_shapes=[
            pltpu.VMEM((per, BLK, BLK), f32),
            pltpu.VMEM((cap, BLK, BLK), bf16),
            pltpu.VMEM((images * 8, 128), f32),
            pltpu.VMEM((LANES, NEAR, 128), bf16),
            pltpu.VMEM((SHARDS, images, 128), bf16),
            pltpu.VMEM((SHARDS, images, 128), bf16),
            pltpu.VMEM((NEAR, 128), f32),
            pltpu.VMEM((NB, SHARDS, BLK), f32),
            pltpu.VMEM((per, SHARDS, BLK), f32),
            pltpu.VMEM((8 * LANES * 8, 128), f32),
            pltpu.VMEM((SHARDS, 8 * LANES, 128), f32),
            pltpu.VMEM((SHARDS, 8 * LANES, 128), f32),
            pltpu.SemaphoreType.DMA,
            pltpu.SemaphoreType.DMA,
            pltpu.SemaphoreType.DMA((11, 3 * n_third)),
            pltpu.SemaphoreType.DMA((7, 3 * n_third)),
            pltpu.SemaphoreType.DMA((small,)),
            pltpu.SemaphoreType.DMA((small,)),
        ],
        compiler_params=pltpu.CompilerParams(collective_id=cap, has_side_effects=True, vmem_limit_bytes=61 << 20),
        name="spread",
    )(slot_of, row_of, col_of, timesteps, labels, tile_master, row_master)

RING = 6
SUM_LAG = 2
Z_STEP = 1
Z_LAG = SUM_LAG + 4 * Z_STEP
ADA_PARTS = 6


def collect_body(
    cap, ch,
    left_ref, right_ref, row_ref, col_ref, count_ref,
    acts_ref, dmod_ref, ends_ref, stats_ref, time_ref, cond_ref, freq_ref, label_ref, pre_ref, own_cond_ref, rows_ref, tiles_ref,
    grads_ref, d_blocks_ref, own_rows_ref, norm_ref, stat_ref,
    out_c, in_c, out_d, out_x, out_y, in_dx, in_dy, in_x, in_y, total, low_in, high_in, final,
    tile, product, all_d, wide_d, all_stats, tok_in, tok_z, tokens, part_out, part_in, pre_out, pre_in, own_dcond, own_dpre,
    vectors, squares, square_in,
    c_send, c_recv, d_send, dx_recv, dy_recv, x_send, x_recv, y_send, y_recv, up_send, low_recv, high_recv, final_recv, down_send,
    keep_sem, load_sem, small_send, small_recv,
):
    z, s = lax.axis_index("grp"), lax.axis_index("shard")
    per = product.shape[0]
    images = GROUPS * SHARDS
    chunks = cap // ch
    x_at, y_at, c_at = (z, s ^ 2), (z, s ^ 4), (z, s ^ 1)
    far_z = [(lax.rem(z + i, GROUPS), s) for i in range(1, GROUPS)]
    near_s = [(z, s ^ i) for i in range(1, SHARDS)]
    half = BLK // 2
    upper, lower = pl.ds(0, half), pl.ds(half, half)

    barrier = pltpu.get_barrier_semaphore()
    for peer in far_z + near_s:
        pl.semaphore_signal(barrier, inc=1, device_id=peer, device_id_type=MESH_ID)

    def remote(src, dst, sent, received, peer):
        return pltpu.make_async_remote_copy(
            src_ref=src, dst_ref=dst, send_sem=sent, recv_sem=received, device_id=peer, device_id_type=MESH_ID
        )

    def block_rows(index, count):
        return pl.ds(pl.multiple_of(index * count, count), count)

    def far(stage, src, dst):
        return [
            remote(src, dst, small_send.at[stage * 3 + i], small_recv.at[stage * 3 + i], peer) for i, peer in enumerate(far_z)
        ]

    def group(stage, src_of, dst):
        first = 9 + stage * 7
        return [
            remote(src_of(peer[1]), dst, small_send.at[first + i], small_recv.at[first + i], peer)
            for i, peer in enumerate(near_s)
        ]

    own_d = all_d.at[block_rows(s * GROUPS + z, 8 * LANES)]
    own_stat = all_stats.at[block_rows(s * GROUPS + z, 8)]
    group_d = all_d.at[block_rows(s, 8 * LANES * GROUPS)]
    group_stat = all_stats.at[block_rows(s, 8 * GROUPS)]

    def small_copies(name):
        if name == "d_far":
            return far(0, own_d, own_d)
        if name == "stat_far":
            return far(1, own_stat, own_stat)
        if name == "tok_far":
            return far(2, tok_z.at[z], tok_z.at[z])
        if name == "tok":
            return group(0, lambda p: ends_ref.at[p], tok_in.at[s])
        if name == "d":
            return group(1, lambda p: group_d, group_d)
        if name == "stat":
            return group(2, lambda p: group_stat, group_stat)
        if name == "part":
            return group(3, lambda p: part_out.at[p], part_in.at[s])
        if name == "pre":
            return group(4, lambda p: pre_out.at[p], pre_in.at[s])
        return group(5, lambda p: square_in.at[s], square_in.at[s])

    def begin(*names):
        for name in names:
            for copy in small_copies(name):
                copy.start()

    def got(*names):
        for name in names:
            for copy in small_copies(name):
                copy.wait_recv()

    def load(part):
        count = tile.shape[0]
        return pltpu.make_async_copy(tiles_ref.at[pl.ds(part * count, count)], tile, load_sem)

    load(0).start()
    own_d[...] = dmod_ref[...].astype(bf16)
    own_stat[...] = stats_ref[...]
    tok_in[s] = ends_ref[s]
    squares[...] = jnp.zeros_like(squares)
    pl.semaphore_wait(barrier, len(far_z) + len(near_s))
    begin("d_far", "stat_far", "tok")

    def spread_stage():
        got("d_far", "stat_far")
        begin("d", "stat")
        got("tok")
        value = tok_in[0]
        for o in range(1, SHARDS):
            value += tok_in[o]
        tok_z[z] = value
        begin("tok_far")

    def order_stage():
        got("d", "stat", "tok_far")
        value = tok_z[0]
        for i in range(1, GROUPS):
            value += tok_z[i]
        tokens[...] = value
        value = all_stats[pl.ds(0, 8), :]
        for i in range(1, images):
            value += all_stats[pl.ds(8 * i, 8), :]
        stat_ref[...] = value

        def widen(i, unused):
            place = block_rows(i, 8 * LANES)
            wide_d[place, :] = all_d[place, :].astype(f32)
            return unused

        lax.fori_loop(0, images, widen, 0)
        for q in range(6 * LANES):
            d_blocks_ref[q // 2, :, (q % 2) * 128 : (q % 2 + 1) * 128] = wide_d[
                pl.ds(q, images, stride=8 * LANES), :
            ].astype(bf16)

    def own_columns(i):
        return wide_d[pl.ds(i * LANES + s, images, stride=8 * LANES), :]

    def ada_stage(part):
        count = tile.shape[0]
        load(part).wait()

        for j in range(count):
            at = part * count + j
            product[at] = nt(d_blocks_ref[jnp.maximum(col_ref[at], 0)], tile[j].astype(bf16))
        if (part + 1) * count < per:
            load(part + 1).start()

    def row_slice(start, count):
        return rows_ref[start : start + count, :].astype(bf16)

    final_at = NCLASS + FREQ + D

    def part_stage():
        def add(j, values):
            chosen = [jnp.logical_and(col_ref[j] >= 0, row_ref[j] == r) for r in range(NB)]
            return tuple(value + jnp.where(one, 1.0, 0.0) * product[j] for one, value in zip(chosen, values))

        values = []
        for r in range(NB):
            value = jnp.zeros((images, BLK), f32)
            for i in range(2):
                value += nt(own_columns(6 + i).astype(bf16), row_slice(final_at + i * D + r * BLK, BLK))
            values.append(value)
        values = lax.fori_loop(0, per, add, tuple(values))
        for r in range(NB):
            for i in range(2):
                part_out[2 * r + i] = values[r][:, i * 128 : (i + 1) * 128]
        part_in[s] = part_out[s]
        begin("part")

    def slope(value):
        gate = jax.nn.sigmoid(value)
        return gate * (1.0 + value * (1.0 - gate))

    def cond_stage():
        got("part")
        value = part_in[0]
        for o in range(1, SHARDS):
            value += part_in[o]
        value = value * slope(own_cond_ref[...])
        own_dcond[...] = value
        for o in range(SHARDS):
            pre_out[o] = nt(value.astype(bf16), row_slice(NCLASS + FREQ + o * 128, 128))
        pre_in[s] = pre_out[s]
        begin("pre")

    def row_stage():
        got("pre")
        value = pre_in[0]
        for o in range(1, SHARDS):
            value += pre_in[o]
        value = value * slope(pre_ref[...])
        own_dpre[...] = value
        dpre_low, dcond = value.astype(bf16), own_dcond[...]
        dcond_low = dcond.astype(bf16)
        gathered = []

        def keep(start, value):
            own_rows_ref[start : start + value.shape[0], :] = value
            gathered.append(fold(value * value))

        hot = label_ref[...].astype(jnp.int32)[:, :1] == lax.broadcasted_iota(jnp.int32, (images, NCLASS), 1)
        keep(
            0,
            lax.dot_general(
                hot.astype(f32), dcond, (((0,), (0,)), ((), ())), preferred_element_type=f32, precision=lax.Precision.HIGHEST
            ),
        )
        keep(NCLASS, tn(freq_ref[...], dpre_low))
        for o in range(SHARDS):
            keep(NCLASS + FREQ + o * 128, tn(time_ref[o], dcond_low))
            for i in range(2):
                keep(final_at + i * D + o * 128, tn(cond_ref[o], own_columns(6 + i).astype(bf16)))
        keep(NEAR_START, tokens[: 2 * PATCH_DIM, :])

        vectors[...] = jnp.zeros_like(vectors)

        def vector(row, value):
            vectors[row : row + 1, :] = value

        vector(0, tokens[T_PATCH : T_PATCH + 1, :])
        vector(1, jnp.sum(value, axis=0, keepdims=True))
        vector(2, jnp.sum(dcond, axis=0, keepdims=True))
        vector(3, tokens[T_QUERY : T_QUERY + 1, :])
        vector(4, tokens[T_VALUE : T_VALUE + 1, :])
        vector(5, tokens[T_OUT : T_OUT + 1, :])
        vector(6, tokens[T_DOWN : T_DOWN + 1, :])
        for i in range(8):
            vector(7 + i if i < 6 else 7 + i + FF // D, jnp.sum(own_columns(i), axis=0, keepdims=True))
        for i in range(FF // D):
            vector(13 + i, tokens[T_UP + i : T_UP + i + 1, :])
        start = NEAR_START + 2 * PATCH_DIM
        rest = own_rows_ref.shape[0] - start
        whole = rest // 8 * 8
        own_rows_ref[start : start + whole, :] = vectors[:whole, :]
        own_rows_ref[start + whole : start + rest, :] = vectors[whole:rest, :]
        value = fold(vectors[...] * vectors[...])
        for piece in gathered:
            value += piece
        squares[:, :128] = squares[:, :128] + value

    def slot_of(i):
        return lax.rem(i + 2 * RING, RING)

    def block(owner, p):
        at = owner * per + p
        return nn(acts_ref[left_ref[at]], acts_ref[right_ref[at]])

    targets = (s ^ 6, s ^ 2, s ^ 4, s)

    def c_copy(slot, item):
        return remote(out_c.at[slot, item], in_c.at[slot, item], c_send.at[slot, item], c_recv.at[slot, item], c_at)

    def dx_copy(slot):
        return remote(out_d.at[slot, :, upper], in_dx.at[slot], d_send.at[slot, 0], dx_recv.at[slot], x_at)

    def dy_copy(slot):
        return remote(out_d.at[slot, :, lower], in_dy.at[slot], d_send.at[slot, 1], dy_recv.at[slot], y_at)

    def x_copy(slot):
        return remote(out_x.at[slot], in_x.at[slot], x_send.at[slot], x_recv.at[slot], x_at)

    def y_copy(slot):
        return remote(out_y.at[slot], in_y.at[slot], y_send.at[slot], y_recv.at[slot], y_at)

    def inside(i):
        return jnp.logical_and(i >= 0, i < chunks)

    def each(body):
        if ch == 1:
            body(0)
            return

        def one(c, unused):
            body(c)
            return unused

        lax.fori_loop(0, ch, one, 0)

    def for_sibling(n):
        slot = slot_of(n)
        for items, at in (((0,), n + 1), ((1, 2, 3), n)):

            @pl.when(inside(at))
            def _():
                for item in items:
                    each(lambda c: out_c.__setitem__((slot, item, c), block(targets[item] ^ 1, at * ch + c).astype(bf16)))
                for item in items:
                    c_copy(slot, item).start()

    def for_owners(i):
        slot, before = slot_of(i), slot_of(i - 1)

        @pl.when(inside(i + 1))
        def _():
            c_copy(slot, 0).wait_recv()

            def one(c):
                value = block(targets[0], (i + 1) * ch + c) + in_c[slot, 0, c].astype(f32)
                out_d[slot, c] = value.astype(bf16)

            each(one)
            dx_copy(slot).start()
            dy_copy(slot).start()

        @pl.when(inside(i))
        def _():
            for item in (1, 2, 3):
                c_copy(slot, item).wait_recv()
            dy_copy(before).wait_recv()
            dx_copy(before).wait_recv()

            def one(c):
                value = block(targets[1], i * ch + c) + in_c[slot, 1, c].astype(f32)
                out_x[slot, c, upper] = value[:half].astype(bf16)
                out_x[slot, c, lower] = (value[half:] + in_dy[before, c].astype(f32)).astype(bf16)

            def two(c):
                value = block(targets[2], i * ch + c) + in_c[slot, 2, c].astype(f32)
                out_y[slot, c, upper] = (value[:half] + in_dx[before, c].astype(f32)).astype(bf16)
                out_y[slot, c, lower] = value[half:].astype(bf16)

            def three(c):
                value = block(targets[3], i * ch + c) + in_c[slot, 3, c].astype(f32)
                total[i * ch + c] = value.astype(bf16)

            each(one)
            each(two)
            x_copy(slot).start()
            y_copy(slot).start()
            each(three)

        old = slot_of(i - SUM_LAG)

        @pl.when(inside(i - SUM_LAG))
        def _():
            x_copy(old).wait_recv()
            y_copy(old).wait_recv()

            def one(c):
                at = (i - SUM_LAG) * ch + c
                value = total[at].astype(f32) + in_x[old, c].astype(f32) + in_y[old, c].astype(f32)
                total[at] = value.astype(bf16)

            each(one)

    def along(j):
        even = lax.rem(j, 2) == 0
        rank = jnp.where(even, z, GROUPS - 1 - z)
        down = jnp.where(even, lax.rem(z + GROUPS - 1, GROUPS), lax.rem(z + 1, GROUPS))
        up = jnp.where(even, lax.rem(z + 1, GROUPS), lax.rem(z + GROUPS - 1, GROUPS))
        return rank, (down, s), (up, s)

    def z_copy(name, j):
        _, down, up = along(j)
        span = pl.ds(j * ch, ch)
        if name == "rise":
            return remote(total.at[span], low_in.at[span], up_send.at[j], low_recv.at[j], up)
        if name == "sink":
            return remote(total.at[span], high_in.at[span], up_send.at[j], high_recv.at[j], down)
        if name == "final_down":
            return remote(final.at[span], final.at[span], down_send.at[0, j], final_recv.at[j], down)
        return remote(final.at[span], final.at[span], down_send.at[1, j], final_recv.at[j], up)

    def over_z(i):
        j = i - SUM_LAG

        @pl.when(inside(j))
        def _():
            rank, _, _ = along(j)

            @pl.when(rank == 0)
            def _():
                z_copy("rise", j).start()

            @pl.when(rank == 3)
            def _():
                z_copy("sink", j).start()

        j2 = j - Z_STEP

        @pl.when(jnp.logical_and(inside(j2), along(j2)[0] == 2))
        def _():
            z_copy("sink", j2).wait_recv()

            def one(c):
                at = j2 * ch + c
                total[at] = (total[at].astype(f32) + high_in[at].astype(f32)).astype(bf16)

            each(one)
            z_copy("sink", j2).start()

        j3 = j - 2 * Z_STEP

        @pl.when(jnp.logical_and(inside(j3), along(j3)[0] == 1))
        def _():
            z_copy("rise", j3).wait_recv()
            z_copy("sink", j3).wait_recv()

            def one(c):
                at = j3 * ch + c
                value = total[at].astype(f32) + low_in[at].astype(f32) + high_in[at].astype(f32)
                final[at] = value.astype(bf16)

            each(one)
            z_copy("final_down", j3).start()
            z_copy("final_up", j3).start()

        j4 = j - 3 * Z_STEP

        @pl.when(jnp.logical_and(inside(j4), along(j4)[0] == 2))
        def _():
            z_copy("final_up", j4).wait_recv()
            z_copy("final_up", j4).start()

        j5 = i - Z_LAG

        @pl.when(inside(j5))
        def _():
            rank = along(j5)[0]

            @pl.when(jnp.logical_or(rank == 0, rank == 3))
            def _():
                z_copy("final_up", j5).wait_recv()

            span = pl.ds(j5 * ch, ch)
            pltpu.make_async_copy(final.at[span], grads_ref.at[span], keep_sem.at[j5]).start()

            def one(c):
                at = j5 * ch + c
                value = final[at].astype(f32) * jnp.where(at < count_ref[0], 1.0, 0.0)
                squares[...] = squares[...] + fold(value * value)

            each(one)

    def settle(i):
        n = i - 2
        slot = slot_of(n)
        for item in range(4):

            @pl.when(inside(n + 1 if item == 0 else n))
            def _():
                c_copy(slot, item).wait_send()

        n2 = i - 3
        slot2 = slot_of(n2)

        @pl.when(inside(n2 + 1))
        def _():
            dx_copy(slot2).wait_send()
            dy_copy(slot2).wait_send()

        @pl.when(inside(n2))
        def _():
            x_copy(slot2).wait_send()
            y_copy(slot2).wait_send()

    hooks = {
        0: spread_stage, 5: order_stage, 13: part_stage, 18: cond_stage, 24: row_stage,
    }
    hooks.update({6 + part: functools.partial(ada_stage, part) for part in range(ADA_PARTS)})

    for_sibling(-1)

    def iteration(step, unused):
        i = step - 1
        for_sibling(i + 1)
        for_owners(i)
        over_z(i)
        settle(i)
        for at, stage in hooks.items():
            pl.when(i == at)(stage)
        return unused

    lax.fori_loop(0, chunks + 1 + Z_LAG, iteration, 0)

    square_in[s] = jnp.zeros((8, 128), f32) + jnp.sum(squares[...])
    begin("square")

    cond_gram = jnp.zeros((images, images), f32)
    for o in range(SHARDS):
        cond_gram += nt(cond_ref[o], cond_ref[o])

    def gram(c, value):
        return value + nt(d_blocks_ref[c], d_blocks_ref[c])

    d_gram = lax.fori_loop(0, 6 * NB, gram, jnp.zeros((images, images), f32))
    got("square")
    value = square_in[0]
    for o in range(1, SHARDS):
        value += square_in[o]
    norm_ref[...] = value + jnp.sum(cond_gram * d_gram)

    def finish(j, unused):
        span = pl.ds(j * ch, ch)
        pltpu.make_async_copy(final.at[span], grads_ref.at[span], keep_sem.at[j]).wait()
        rank = along(j)[0]

        @pl.when(rank == 0)
        def _():
            z_copy("rise", j).wait_send()

        @pl.when(rank >= 2)
        def _():
            z_copy("sink", j).wait_send()

        @pl.when(rank == 1)
        def _():
            z_copy("final_down", j).wait_send()

        @pl.when(jnp.logical_or(rank == 1, rank == 2))
        def _():
            z_copy("final_up", j).wait_send()

        return unused

    lax.fori_loop(0, chunks, finish, 0)
    for name in ("d_far", "stat_far", "tok_far", "tok", "d", "stat", "part", "pre", "square"):
        for copy in small_copies(name):
            copy.wait_send()


def collect(cap, left_of, right_of, row_of, col_of, count, acts, dmod, ends, stats, times, conds, freq_low, label, own_pre, own_cond,
            row_master, tile_master):
    per = tile_master.shape[0]
    ch = 1
    chunks = cap // ch
    images = GROUPS * SHARDS
    vmem = pl.BlockSpec(memory_space=pltpu.VMEM)
    smem = pl.BlockSpec(memory_space=pltpu.SMEM)
    anywhere = pl.BlockSpec(memory_space=pl.ANY)
    small = 9 + 6 * (SHARDS - 1)
    dma = pltpu.SemaphoreType.DMA

    def blocks(*lead):
        return pltpu.VMEM(lead + (BLK, BLK), bf16)

    return pl.pallas_call(
        functools.partial(collect_body, cap, ch),
        out_shape=[
            jax.ShapeDtypeStruct((per, BLK, BLK), bf16),
            jax.ShapeDtypeStruct((6 * NB, images, BLK), bf16),
            jax.ShapeDtypeStruct(row_master.shape, f32),
            jax.ShapeDtypeStruct((8, 128), f32),
            jax.ShapeDtypeStruct((8, 128), f32),
        ],
        in_specs=[smem] * 5 + [vmem] * 11 + [anywhere],
        out_specs=[anywhere] + [vmem] * 4,
        scratch_shapes=[
            blocks(RING, 4, ch),
            blocks(RING, 4, ch),
            blocks(RING, ch),
            blocks(RING, ch),
            blocks(RING, ch),
            pltpu.VMEM((RING, ch, BLK // 2, BLK), bf16),
            pltpu.VMEM((RING, ch, BLK // 2, BLK), bf16),
            blocks(RING, ch),
            blocks(RING, ch),
            blocks(cap),
            blocks(cap),
            blocks(cap),
            blocks(cap),
            pltpu.VMEM((per // ADA_PARTS, BLK, BLK), f32),
            pltpu.VMEM((per, images, BLK), f32),
            pltpu.VMEM((images * 8 * LANES, 128), bf16),
            pltpu.VMEM((images * 8 * LANES, 128), f32),
            pltpu.VMEM((images * 8, 128), f32),
            pltpu.VMEM((SHARDS, TOKEN_ROWS, 128), f32),
            pltpu.VMEM((GROUPS, TOKEN_ROWS, 128), f32),
            pltpu.VMEM((TOKEN_ROWS, 128), f32),
            pltpu.VMEM((SHARDS, images, 128), f32),
            pltpu.VMEM((SHARDS, images, 128), f32),
            pltpu.VMEM((SHARDS, images, 128), f32),
            pltpu.VMEM((SHARDS, images, 128), f32),
            pltpu.VMEM((images, 128), f32),
            pltpu.VMEM((images, 128), f32),
            pltpu.VMEM((24, 128), f32),
            pltpu.VMEM((8, BLK), f32),
            pltpu.VMEM((SHARDS, 8, 128), f32),
            dma((RING, 4)),
            dma((RING, 4)),
            dma((RING, 2)),
            dma((RING,)),
            dma((RING,)),
            dma((RING,)),
            dma((RING,)),
            dma((RING,)),
            dma((RING,)),
            dma((chunks,)),
            dma((chunks,)),
            dma((chunks,)),
            dma((chunks,)),
            dma((2, chunks)),
            dma((chunks,)),
            dma,
            dma((small,)),
            dma((small,)),
        ],
        compiler_params=pltpu.CompilerParams(
            collective_id=100 + cap, has_side_effects=True, vmem_limit_bytes=50 << 20
        ),
        name="collect",
    )(left_of, right_of, row_of, col_of, count, acts, dmod, ends, stats, times, conds, freq_low, label, own_pre, own_cond,
      row_master, tile_master)


def position_table(grid_side, model_width):
    quarter = model_width // 4
    omega = 1.0 / 10000.0 ** (jnp.arange(quarter, dtype=f32) / quarter)
    angle = jnp.arange(grid_side).astype(f32)[:, None] * omega[None, :]
    return jnp.stack([jnp.sin(angle), jnp.cos(angle)])


def time_freq(step_values, freq_width):
    half_width = freq_width // 2
    freqs = jnp.exp(-math.log(10000.0) * jnp.arange(half_width, dtype=f32) / half_width)
    angle_arg = step_values.astype(f32)[:, None] * freqs[None, :]
    return jnp.concatenate([jnp.cos(angle_arg), jnp.sin(angle_arg)], axis=1)


def silu_slope(value):
    gate = jax.nn.sigmoid(value)
    return gate * (1.0 + value * (1.0 - gate))


def blocked(array):
    count = array.shape[0]
    return array.reshape(count, -1, BLK).transpose(1, 0, 2)


def factors_of(block):
    n = jnp.maximum(block - ADA, 0)
    out, up, down = n - AT_OUT, n - AT_UP, n - AT_DOWN
    row = lax.div(n, jnp.int32(QB))
    left = jnp.where(n < AT_OUT, L_ATT + row, jnp.where(n < AT_UP, L_OUT + (out >> 2), jnp.where(n < AT_DOWN, L_MLP + (up >> 4), L_HID + (down >> 2))))
    right = jnp.where(
        n < AT_OUT,
        R_QKV + n - row * QB,
        jnp.where(n < AT_UP, R_OUT + (out & (NB - 1)), jnp.where(n < AT_DOWN, R_UP + (up & (HB - 1)), R_DOWN + (down & (NB - 1)))),
    )
    return left, right


def places_body(
    per, assign_ref, slot_ref, row_ref, col_ref, rank_ref, inverse_ref, left_ref, right_ref, count_ref, tier_ref
):
    me = lax.axis_index("shard")

    def place_in(block, s, before):
        return jnp.where(block < ADA, per - 1 - (s - before), before), before + jnp.where(block < ADA, 0, 1)

    def owner(o, most):
        def slot(s, before):
            block = assign_ref[o * per + s]
            p, after = place_in(block, s, before)
            place = o * per + p
            inverse_ref[block] = place
            left, right = factors_of(block)
            left_ref[place] = left
            right_ref[place] = right
            return after

        return jnp.maximum(most, lax.fori_loop(0, per, slot, jnp.int32(0), unroll=True))

    most = lax.fori_loop(0, assign_ref.shape[0] // per, owner, jnp.int32(0))
    tier_ref[0] = sum(jnp.where(most > cap, 1, 0) for cap in CAPS)

    def own(s, before):
        block = assign_ref[me * per + s]
        p, after = place_in(block, s, before)
        slot_ref[p] = s
        rank_ref[s] = p
        row_ref[s] = jnp.where(block < ADA, block // (6 * NB), 0)
        col_ref[s] = jnp.where(block < ADA, block % (6 * NB), -1)
        return after

    count_ref[0] = lax.fori_loop(0, per, own, jnp.int32(0), unroll=True)


def find_places(assign, per):
    smem = pl.BlockSpec(memory_space=pltpu.SMEM)

    def ints(count):
        return jax.ShapeDtypeStruct((count,), jnp.int32)

    total = assign.shape[0]
    return pl.pallas_call(
        functools.partial(places_body, per),
        out_shape=[ints(per)] * 4 + [ints(total)] * 3 + [ints(1)] * 2,
        in_specs=[smem],
        out_specs=[smem] * 9,
        name="find_places",
    )(assign)


def spread_plain(slot_of, row_of, col_of, tile_master, row_master, timesteps, labels):
    shard_count = lax.axis_size("shard")
    everyone = ("grp", "shard")
    me = lax.axis_index("shard")
    per, columns = tile_master.shape[0], row_master.shape[1]
    low_rows = row_master.astype(bf16)
    at = [0]

    def take(count):
        at[0] += count
        return low_rows[at[0] - count : at[0]]

    table, w_time1, w_time2 = take(NCLASS), take(FREQ), take(D)
    w_final = (take(D), take(D))
    take(2 * PATCH_DIM)
    take(1)
    b_time1, b_time2 = take(1), take(1)
    take(4)
    b_ada = take(6)
    take(FF // D)
    b_final = take(2)
    b_mod = jnp.concatenate([b_ada, b_final], axis=0)

    packed = pack_tiles(slot_of, tile_master)
    gathered = lax.all_gather(packed, "shard", axis=0, tiled=True)
    near = lax.all_gather(low_rows[NEAR_START:], "shard", axis=1, tiled=True)
    near = jnp.pad(near, ((0, NEAR - NEAR_REAL), (0, 0))).reshape(NEAR, LANES, 128).transpose(1, 0, 2)

    ids = lax.all_gather(jnp.concatenate([timesteps, labels]), everyone, axis=0)
    all_steps, all_labels = ids[:, 0], ids[:, 1]
    freq_low = time_freq(all_steps, FREQ).astype(bf16)
    own_pre = nn(freq_low, w_time1) + b_time1
    time_low = lax.all_gather(jax.nn.silu(own_pre).astype(bf16), "shard", axis=1, tiled=True)
    one_hot = (all_labels[:, None] == jnp.arange(NCLASS, dtype=jnp.int32)[None, :]).astype(bf16)
    own_cond = nn(time_low, w_time2) + b_time2 + nn(one_hot, table)
    cond_low = lax.all_gather(jax.nn.silu(own_cond).astype(bf16), "shard", axis=1, tiled=True)
    group_cond = lax.dynamic_slice(cond_low, (lax.axis_index("grp") * shard_count, 0), (shard_count, D))
    part_mod = ada_front(row_of, col_of, blocked(group_cond), tile_master)
    part_mod = part_mod.transpose(1, 0, 2).reshape(shard_count, 6, D)
    part_final = jnp.stack([nn(group_cond, w_final[0]), nn(group_cond, w_final[1])], axis=1)
    spread = jnp.zeros((shard_count, 8, D), f32)
    spread = lax.dynamic_update_slice(
        spread,
        jnp.concatenate([jnp.zeros((shard_count, 6, columns), f32), part_final], axis=1) + b_mod[None].astype(f32),
        (0, 0, me * columns),
    )
    spread = spread + jnp.concatenate([part_mod, jnp.zeros((shard_count, 2, D), f32)], axis=1)
    mods = lax.psum_scatter(spread, "shard", scatter_dimension=0, tiled=True)[0]
    label = jnp.broadcast_to(all_labels.astype(f32)[:, None], (all_labels.shape[0], 128))

    def lanes(array):
        return array.reshape(-1, LANES, 128).transpose(1, 0, 2)

    return (
        gathered, near, mods.reshape(8 * LANES, 128), freq_low, label, lanes(time_low), lanes(cond_low), own_pre, own_cond,
    )


def collect_plain(left_of, right_of, row_of, col_of, count, acts, dmod, ends, stats, times, conds, freq_low, label, own_pre, own_cond,
                  row_master, tile_master):
    everyone = ("grp", "shard")
    me = lax.axis_index("shard")
    columns = row_master.shape[1]
    low_rows = row_master.astype(bf16)
    w_time2 = low_rows[NCLASS + FREQ : NCLASS + FREQ + D]
    w_final = [low_rows[NCLASS + FREQ + (1 + i) * D : NCLASS + FREQ + (2 + i) * D] for i in range(2)]
    one_hot = (label[:, :1].astype(jnp.int32) == jnp.arange(NCLASS, dtype=jnp.int32)[None, :]).astype(bf16)
    time_low, cond_low = (array.transpose(1, 0, 2).reshape(-1, D) for array in (times, conds))
    partial = tile_grads(left_of, right_of, acts)
    own_tiles = lax.psum_scatter(partial, "shard", scatter_dimension=0, tiled=True)
    own_tiles = lax.psum(own_tiles, "grp")

    all_dmod = lax.all_gather(dmod.reshape(1, -1).astype(bf16), everyone, axis=0, tiled=True)
    dmod_blocks = blocked(all_dmod[:, : 6 * D])
    own_dmod = lax.dynamic_slice(all_dmod.reshape(-1, 8, D), (0, 0, me * columns), (all_dmod.shape[0], 8, columns))
    part_cond = ada_back(row_of, col_of, dmod_blocks, tile_master).transpose(1, 0, 2).reshape(-1, D)
    part_cond = part_cond + nt(own_dmod[:, 6], w_final[0]) + nt(own_dmod[:, 7], w_final[1])
    own_dcond = lax.psum_scatter(part_cond, "shard", scatter_dimension=1, tiled=True) * silu_slope(own_cond)
    dcond_low = own_dcond.astype(bf16)
    own_dpre = lax.psum_scatter(nt(dcond_low, w_time2), "shard", scatter_dimension=1, tiled=True)
    own_dpre = own_dpre * silu_slope(own_pre)
    wide_dmod = own_dmod.astype(f32)

    token_rows = ends.transpose(1, 0, 2).reshape(TOKEN_ROWS, D)
    token_rows = lax.psum_scatter(token_rows, "shard", scatter_dimension=1, tiled=True)
    token_rows = lax.psum(token_rows, "grp")
    own_rows = jnp.concatenate(
        [
            tn(one_hot.astype(f32), own_dcond),
            tn(freq_low, own_dpre.astype(bf16)),
            tn(time_low, dcond_low),
            tn(cond_low, own_dmod[:, 6]),
            tn(cond_low, own_dmod[:, 7]),
            token_rows[: T_PATCH + 1],
            jnp.sum(own_dpre, axis=0)[None],
            jnp.sum(own_dcond, axis=0)[None],
            token_rows[T_QUERY : T_VALUE + 1],
            token_rows[T_OUT : T_DOWN + 1],
            jnp.sum(wide_dmod[:, :6], axis=0),
            token_rows[T_UP:T_END],
            jnp.sum(wide_dmod[:, 6:], axis=0),
        ],
        axis=0,
    )
    totals = lax.psum(stats, everyone)
    cond_gram = nt(cond_low, cond_low)
    dmod_gram = nt(all_dmod[:, : 6 * D], all_dmod[:, : 6 * D])
    counted = jnp.arange(own_tiles.shape[0], dtype=jnp.int32) < count
    wide_tiles = jnp.where(counted[:, None, None], own_tiles.astype(f32), 0.0)
    square_part = jnp.sum(wide_tiles * wide_tiles) + jnp.sum(own_rows * own_rows)
    square_sum = lax.psum(square_part, "shard") + jnp.sum(cond_gram * dmod_gram)
    return own_tiles, dmod_blocks, own_rows, jnp.broadcast_to(square_sum, (8, 128)), totals


def pack_body(slot_ref, tile_ref, out_ref):
    out_ref[...] = tile_ref[...].astype(bf16)


def pack_tiles(slot_of, tile_master):
    per = tile_master.shape[0]
    return pl.pallas_call(
        pack_body,
        grid_spec=pltpu.PrefetchScalarGridSpec(
            num_scalar_prefetch=1,
            grid=(per,),
            in_specs=[pl.BlockSpec((1, BLK, BLK), lambda p, slots: (slots[p], 0, 0))],
            out_specs=pl.BlockSpec((1, BLK, BLK), lambda p, slots: (p, 0, 0)),
        ),
        out_shape=jax.ShapeDtypeStruct(tile_master.shape, bf16),
        name="pack_tiles",
    )(slot_of, tile_master)


def shards(
    patches, noise, timesteps, labels, assign, tile_master, tile_bases, tile_moment, tile_second,
    row_master, row_moment, row_second,
):
    group_count, shard_count = lax.axis_size("grp"), lax.axis_size("shard")
    everyone = ("grp", "shard")
    me = lax.axis_index("shard")
    per = tile_master.shape[0]
    columns = row_master.shape[1]
    token_total = patches.shape[0] * group_count * shard_count
    tile_total = assign.shape[0]

    slot_of, row_of, col_of, rank, inverse, left_of, right_of, count, tier = find_places(assign, per)
    fast = group_count == GROUPS and shard_count == SHARDS
    if fast:
        tier = tier[0]
        gathered, near, mods, freq_low, label, times, conds, own_pre, own_cond = lax.switch(
            tier, [functools.partial(spread, cap) for cap in CAPS + (per,)], slot_of, row_of, col_of, timesteps, labels, tile_master, row_master,
        )
        gathered = gathered.reshape(tile_total, BLK, BLK)
    else:
        gathered, near, mods, freq_low, label, times, conds, own_pre, own_cond = spread_plain(
            slot_of, row_of, col_of, tile_master, row_master, timesteps, labels
        )

    loss_scale = 1.0 / (token_total * PATCH_DIM)
    acts, dmod, ends, stats = block_step(
        inverse, gathered, patches.T, noise.T, position_table(LAT // PATCH_SIDE, D), near, mods.reshape(8 * LANES, 128),
        2.0 * loss_scale,
    )

    if fast:
        own_tiles, dmod_blocks, own_rows, squares, totals = lax.switch(
            tier, [functools.partial(collect, cap) for cap in CAPS + (per,)], left_of, right_of, row_of, col_of, count, acts, dmod, ends, stats, times, conds, freq_low, label, own_pre,
            own_cond, row_master, tile_master,
        )
    else:
        own_tiles, dmod_blocks, own_rows, squares, totals = collect_plain(
            left_of, right_of, row_of, col_of, count, acts, dmod, ends, stats, times, conds, freq_low, label, own_pre,
            own_cond, row_master, tile_master,
        )
    new_tile_moment, new_tile_second, tile_update, new_row_moment, new_row_second, row_update, loss, grad_norm, act_rms = adam(
        (1.0 / (token_total * PATCH_DIM), 1.0 / (token_total * D)), rank, row_of, col_of, squares, totals, own_tiles, conds,
        dmod_blocks, tile_bases, tile_moment, tile_second, own_rows, row_master, row_moment, row_second,
    )
    loss, grad_norm = loss.reshape(()), grad_norm.reshape(())
    return (
        loss, grad_norm, act_rms, new_tile_moment, new_tile_second, tile_update, new_row_moment, new_row_second, row_update,
    )


def solution(mesh):
    placed = (
        P(("grp", "shard"), None),
        P(("grp", "shard"), None),
        P(("grp", "shard")),
        P(("grp", "shard")),
        P(),
        P("shard", None, None),
        P("shard", None, None, None),
        P("shard", None, None),
        P("shard", None, None),
        P(None, "shard"),
        P(None, "shard"),
        P(None, "shard"),
    )
    return jax.shard_map(
        shards,
        mesh=mesh,
        in_specs=placed,
        out_specs=(
            P(), P(), P(),
            P("shard", None, None), P("shard", None, None), P("shard", None, None),
            P(None, "shard"), P(None, "shard"), P(None, "shard"),
        ),
        check_vma=False,
    )
```

```python
import functools
import math

import jax
import jax.numpy as jnp
from jax import lax
from jax.experimental import pallas as pl
from jax.experimental.pallas import tpu as pltpu
from jax.sharding import PartitionSpec as P

D = 1024
HEADS = 16
HD = 64
FF = 4096
NCLASS = 1000
FREQ = 256
PATCH_SIDE = 2
LAT = 32
BLK = 256
PATCH_DIM = 16
SEQ = 256

NB = D // BLK
HB = FF // BLK
QB = 3 * NB
ADA = NB * 6 * NB
BIG = NB * QB + NB * NB + 2 * NB * HB
AT_QKV, AT_OUT, AT_UP, AT_DOWN = 0, NB * QB, NB * QB + NB * NB, NB * QB + NB * NB + NB * HB
L_ATT, L_OUT, L_MLP, L_HID = 0, NB, 2 * NB, 3 * NB
R_QKV = 3 * NB + HB
R_OUT = R_QKV + QB
R_UP = R_OUT + NB
R_DOWN = R_UP + HB
ACTS = R_DOWN + NB
B_OUT, B_UP, B_DOWN = QB, QB + NB, QB + NB + HB
ROW_STEP = 128
ADAM_GROUP = 3
LANES = D // 128
NEAR = 64
NEAR_START = NCLASS + FREQ + 3 * D
N_PATCH, N_TIME1, N_TIME2, N_QUERY, N_VALUE, N_OUT, N_DOWN, N_ADA = range(2 * PATCH_DIM, 2 * PATCH_DIM + 8)
N_UP = N_ADA + 6
N_FINAL = N_UP + FF // D
NEAR_REAL = N_FINAL + 2
T_PATCH, T_OUT, T_DOWN, T_QUERY, T_VALUE, T_UP = range(2 * PATCH_DIM, 2 * PATCH_DIM + 6)
T_END = T_UP + FF // D
TOKEN_ROWS = 48

CAPS = (28, 30)
GROUPS, SHARDS = 4, 8
MESH_ID = pl.DeviceIdType.MESH

ln_eps = 1e-06
beta_one = 0.5
beta_two = 0.5
adam_eps = 1e-08
rate_step = 0.01
decay_rate = 0.1
clip_at = 0.25

f32 = jnp.float32
bf16 = jnp.bfloat16


def nn(left, right):
    return lax.dot_general(left, right, (((1,), (0,)), ((), ())), preferred_element_type=f32)


def nt(left, right):
    return lax.dot_general(left, right, (((1,), (1,)), ((), ())), preferred_element_type=f32)


def tn(left, right):
    return lax.dot_general(left, right, (((0,), (0,)), ((), ())), preferred_element_type=f32)


def wide(ref, at, count=ROW_STEP):
    return jnp.concatenate([ref[r, pl.ds(at, count), :] for r in range(NB)], axis=1)


def put(ref, base, at, value, count=ROW_STEP):
    for r in range(NB):
        ref[base + r, pl.ds(at, count), :] = value[:, r * BLK : (r + 1) * BLK].astype(ref.dtype)


def fold(value):
    return jnp.sum(value.reshape(-1, 8, value.shape[-1]), axis=0)


def normed(value):
    centred = value - jnp.mean(value, axis=-1, keepdims=True)
    spread = jnp.mean(centred * centred, axis=-1, keepdims=True)
    back = lax.rsqrt(spread + ln_eps)
    return centred * back, back


def over_rows(body):
    def step(i, unused):
        body(pl.multiple_of(i * ROW_STEP, ROW_STEP))
        return unused

    lax.fori_loop(0, SEQ // ROW_STEP, step, 0)


def over(count, body, together=2):
    def step(i, unused):
        body(i)
        return unused

    lax.fori_loop(0, count, step, 0, unroll=together)


def norm_back(grad, value, scale):
    norm, back = normed(value)
    inner = grad * (1.0 + scale)
    mean_one = jnp.mean(inner, axis=-1, keepdims=True)
    mean_two = jnp.mean(inner * norm, axis=-1, keepdims=True)
    return norm, (inner - mean_one - norm * mean_two) * back


def gelu_pair(value):
    root = math.sqrt(2.0 / math.pi)
    square = value * value
    bend = jnp.tanh(root * (value + 0.044715 * value * square))
    half = 0.5 * (1.0 + bend)
    slope = half + 0.5 * value * (1.0 - bend * bend) * root * (1.0 + 3 * 0.044715 * square)
    return value * half, slope


def block_body(
    loss_factor, place_ref, tiles_ref, patches_ref, noise_ref, spot_ref, near_ref, mods_ref,
    acts_ref, dmod_ref, ends_ref, stats_ref,
    w_ref, stream, middle, last, out_att, out_mlp, low_in, low_att, qkv, hid, slope, probs, flow, sums,
    near_wide, bias_ref, mod_ref, dbias_ref, w_sem,
):
    att_scale = HD ** (-0.5)
    cuts = (AT_QKV, AT_OUT, AT_UP, AT_DOWN, BIG)

    def fetch(b, sem):
        pltpu.make_async_copy(tiles_ref.at[place_ref[ADA + b]], w_ref.at[b], w_sem.at[sem]).start()

    for m in range(4):
        over(cuts[m + 1] - cuts[m], lambda b, m=m: fetch(cuts[m] + b, m))

    def arrived(m):
        span = pl.ds(cuts[m], cuts[m + 1] - cuts[m])
        pltpu.make_async_copy(tiles_ref.at[pl.ds(0, cuts[m + 1] - cuts[m])], w_ref.at[span], w_sem.at[m]).wait()

    def mod(i):
        return mod_ref[i : i + 1, :]

    near_wide[...] = near_ref[...].astype(f32)

    def row_block(row, r):
        return jnp.concatenate([near_wide[2 * r, row : row + 1, :], near_wide[2 * r + 1, row : row + 1, :]], axis=1)

    def near_block(row, r):
        span = slice(row, row + PATCH_DIM)
        return jnp.concatenate([near_ref[2 * r, span, :], near_ref[2 * r + 1, span, :]], axis=1)

    for r in range(NB):
        bias_ref[r] = row_block(N_QUERY, r)
        bias_ref[NB + r] = jnp.zeros((1, BLK), f32)
        bias_ref[2 * NB + r] = row_block(N_VALUE, r)
        bias_ref[B_OUT + r] = row_block(N_OUT, r)
        bias_ref[B_DOWN + r] = row_block(N_DOWN, r)
        for i in range(FF // D):
            bias_ref[B_UP + i * NB + r] = row_block(N_UP + i, r)
    for i in range(8):
        mod_ref[i : i + 1, :] = jnp.concatenate([mods_ref[i * LANES + o : i * LANES + o + 1, :] for o in range(LANES)], axis=1)

    lane = lax.broadcasted_iota(jnp.int32, (SEQ, 128), 1)
    lower = lane < HD
    halves = (lower, jnp.logical_not(lower))

    def masked(value, side):
        return jnp.where(halves[side], value, jnp.zeros_like(value))

    sums[...] = jnp.zeros_like(sums)
    S_SQ_END, S_SQ_ATT, S_SQ_MLP = 0, 1, 2
    S_DSH_A, S_DSC_A, S_DG_A, S_DSH_M, S_DSC_M, S_DG_M, S_DSH_F, S_DSC_F = range(3, 11)
    S_PATCH, S_OUT, S_DOWN = 11, 12, 13

    def collect(which, value):
        sums[which] = sums[which] + fold(value)

    patches = patches_ref[...]
    side = LAT // PATCH_SIDE
    for r in range(NB):
        stream[r] = tn(patches, near_block(0, r)) + row_block(N_PATCH, r)
    for i in range(side):
        span = slice(i * side, (i + 1) * side)
        for r in range(2):
            stream[r, span, :] = stream[r, span, :] + spot_ref[r, i : i + 1, :]
            stream[2 + r, span, :] = stream[2 + r, span, :] + spot_ref[r]

    def modulate(source, scale, shift):
        def body(at):
            norm, _ = normed(wide(source, at))
            put(low_in, 0, at, norm * (1.0 + scale) + shift)

        over_rows(body)

    def transposed(base, ref, count):
        over(count, lambda r: acts_ref.__setitem__(base + r, ref[r].T))

    modulate(stream, mod(1), mod(0))
    transposed(L_ATT, low_in, NB)
    arrived(0)

    def qkv_step(c):
        total = nn(low_in[0], w_ref[AT_QKV + c])
        for r in range(1, NB):
            total += nn(low_in[r], w_ref[AT_QKV + r * QB + c])
        qkv[c] = (total + bias_ref[c]).astype(bf16)

    over(QB, qkv_step)

    def attend(c):
        for half in range(2):
            span = slice(half * 128, (half + 1) * 128)
            q, k, v = qkv[c, :, span], qkv[NB + c, :, span], qkv[2 * NB + c, :, span]
            parts = []
            for side in range(2):
                scores = nt(masked(q, side), k) * att_scale
                top = jnp.max(scores, axis=-1, keepdims=True)
                power = jnp.exp(scores - top)
                prob = power / jnp.sum(power, axis=-1, keepdims=True)
                probs[c * 4 + half * 2 + side] = prob
                parts.append(nn(prob.astype(bf16), v))
            low_att[c, :, span] = jnp.where(lower, parts[0], parts[1]).astype(bf16)

    over(NB, attend)
    transposed(L_OUT, low_att, NB)
    arrived(1)

    def out_step(c):
        total = nn(low_att[0], w_ref[AT_OUT + c])
        for r in range(1, NB):
            total += nn(low_att[r], w_ref[AT_OUT + r * NB + c])
        out_att[c] = total + bias_ref[B_OUT + c]

    over(NB, out_step)

    def mid_step(at):
        branch = mod(2) * wide(out_att, at)
        collect(S_SQ_ATT, branch * branch)
        value = wide(stream, at) + branch
        put(middle, 0, at, value)
        norm, _ = normed(value)
        put(low_in, 0, at, norm * (1.0 + mod(4)) + mod(3))

    over_rows(mid_step)
    transposed(L_MLP, low_in, NB)
    arrived(2)

    def up_step(c):
        total = nn(low_in[0], w_ref[AT_UP + c])
        for r in range(1, NB):
            total += nn(low_in[r], w_ref[AT_UP + r * HB + c])
        value, back = gelu_pair(total + bias_ref[B_UP + c])
        slope[c] = back
        low = value.astype(bf16)
        hid[c] = low
        acts_ref[L_HID + c] = low.T

    over(HB, up_step)
    arrived(3)

    def down_step(c):
        total = nn(hid[0], w_ref[AT_DOWN + c])
        for r in range(1, HB):
            total += nn(hid[r], w_ref[AT_DOWN + r * NB + c])
        out_mlp[c] = total + bias_ref[B_DOWN + c]

    over(NB, down_step)

    def end_step(at):
        branch = mod(5) * wide(out_mlp, at)
        collect(S_SQ_MLP, branch * branch)
        value = wide(middle, at) + branch
        collect(S_SQ_END, value * value)
        put(last, 0, at, value)
        norm, _ = normed(value)
        put(low_in, 0, at, norm * (1.0 + mod(7)) + mod(6))

    over_rows(end_step)
    predicted = nt(near_block(PATCH_DIM, 0), low_in[0])
    for r in range(1, NB):
        predicted += nt(near_block(PATCH_DIM, r), low_in[r])
    mismatch = predicted - noise_ref[...]
    loss_sum = jnp.sum(mismatch * mismatch)
    pred_low = (loss_factor * mismatch).astype(bf16)
    def put_rows(row, count, r, value):
        for i in range(2):
            ends_ref[2 * r + i, row : row + count, :] = value[:, i * 128 : (i + 1) * 128]

    for r in range(NB):
        put_rows(PATCH_DIM, PATCH_DIM, r, nn(pred_low, low_in[r]))
        flow[r] = tn(pred_low, near_block(PATCH_DIM, r))

    def end_back(at):
        grad = wide(flow, at)
        norm, value = norm_back(grad, wide(last, at), mod(7))
        collect(S_DSC_F, grad * norm)
        collect(S_DSH_F, grad)
        put(last, 0, at, value)
        collect(S_DG_M, value * wide(out_mlp, at))
        down = value * mod(5)
        collect(S_DOWN, down)
        put(acts_ref, R_DOWN, at, down)

    over_rows(end_back)

    def up_back(c):
        total = nt(acts_ref[R_DOWN], w_ref[AT_DOWN + c * NB])
        for j in range(1, NB):
            total += nt(acts_ref[R_DOWN + j], w_ref[AT_DOWN + c * NB + j])
        value = total * slope[c]
        dbias_ref[2 * NB + c] = jnp.sum(value, axis=0, keepdims=True)
        acts_ref[R_UP + c] = value.astype(bf16)

    over(HB, up_back)

    def mlp_back(r):
        total = nt(acts_ref[R_UP], w_ref[AT_UP + r * HB])
        for c in range(1, HB):
            total += nt(acts_ref[R_UP + c], w_ref[AT_UP + r * HB + c])
        flow[r] = total

    over(NB, mlp_back)

    def mid_back(at):
        grad = wide(flow, at)
        norm, value = norm_back(grad, wide(middle, at), mod(4))
        collect(S_DSC_M, grad * norm)
        collect(S_DSH_M, grad)
        value = value + wide(last, at)
        put(middle, 0, at, value)
        collect(S_DG_A, value * wide(out_att, at))
        proj = value * mod(2)
        collect(S_OUT, proj)
        put(acts_ref, R_OUT, at, proj)

    over_rows(mid_back)

    def att_back(r):
        total = nt(acts_ref[R_OUT], w_ref[AT_OUT + r * NB])
        for c in range(1, NB):
            total += nt(acts_ref[R_OUT + c], w_ref[AT_OUT + r * NB + c])
        low_att[r] = total.astype(bf16)

    over(NB, att_back)

    def attend_back(c):
        for half in range(2):
            span = slice(half * 128, (half + 1) * 128)
            q, k, v = qkv[c, :, span], qkv[NB + c, :, span], qkv[2 * NB + c, :, span]
            grad = low_att[c, :, span]
            found = []
            for side in range(2):
                prob = probs[c * 4 + half * 2 + side]
                dprob = nt(masked(grad, side), v)
                dvalue = tn(prob.astype(bf16), grad)
                dscore = prob * (dprob - jnp.sum(dprob * prob, axis=-1, keepdims=True))
                low = dscore.astype(bf16)
                found.append((nn(low, k) * att_scale, tn(low, q) * att_scale, dvalue))
            merged = [jnp.where(lower, one, two) for one, two in zip(*found)]
            for i in range(3):
                acts_ref[R_QKV + i * NB + c, :, span] = merged[i].astype(bf16)
            dbias_ref[c, :, span] = jnp.sum(merged[0], axis=0, keepdims=True)
            dbias_ref[NB + c, :, span] = jnp.sum(merged[2], axis=0, keepdims=True)

    over(NB, attend_back)

    def in_back(r):
        total = nt(acts_ref[R_QKV], w_ref[AT_QKV + r * QB])
        for c in range(1, QB):
            total += nt(acts_ref[R_QKV + c], w_ref[AT_QKV + r * QB + c])
        flow[r] = total

    over(NB, in_back)

    def first_back(at):
        grad = wide(flow, at)
        norm, value = norm_back(grad, wide(stream, at), mod(1))
        collect(S_DSC_A, grad * norm)
        collect(S_DSH_A, grad)
        value = value + wide(middle, at)
        collect(S_PATCH, value)
        put(low_in, 0, at, value)

    over_rows(first_back)
    for r in range(NB):
        put_rows(0, PATCH_DIM, r, nn(patches, low_in[r]))

    def total_of(which):
        return jnp.sum(sums[which], axis=0, keepdims=True)

    for i in range(8):
        value = total_of(S_DSH_A + i)
        for o in range(LANES):
            dmod_ref[i * LANES + o : i * LANES + o + 1, :] = value[:, o * 128 : (o + 1) * 128]
    for row, which in ((T_PATCH, S_PATCH), (T_OUT, S_OUT), (T_DOWN, S_DOWN)):
        value = total_of(which)
        for r in range(NB):
            put_rows(row, 1, r, value[:, r * BLK : (r + 1) * BLK])
    for r in range(NB):
        put_rows(T_QUERY, 1, r, dbias_ref[r])
        put_rows(T_VALUE, 1, r, dbias_ref[NB + r])
        for i in range(FF // D):
            put_rows(T_UP + i, 1, r, dbias_ref[2 * NB + i * NB + r])
    ends_ref[:, T_END:, :] = jnp.zeros((LANES, TOKEN_ROWS - T_END, 128), f32)
    row = lax.broadcasted_iota(jnp.int32, (8, 128), 0)
    found = jnp.where(row == 0, loss_sum, 0.0)
    for i in range(3):
        found = jnp.where(row == i + 1, jnp.sum(sums[i]), found)
    stats_ref[...] = found


def block_step(place, tiles, patches, noise, spots, near, mods, loss_factor):
    vmem = pl.BlockSpec(memory_space=pltpu.VMEM)
    macs = 3 * SEQ * BIG * BLK * BLK
    return pl.pallas_call(
        functools.partial(block_body, loss_factor),
        out_shape=[
            jax.ShapeDtypeStruct((ACTS, BLK, BLK), bf16),
            jax.ShapeDtypeStruct((8 * LANES, 128), f32),
            jax.ShapeDtypeStruct((LANES, TOKEN_ROWS, 128), f32),
            jax.ShapeDtypeStruct((8, 128), f32),
        ],
        in_specs=[pl.BlockSpec(memory_space=pltpu.SMEM), pl.BlockSpec(memory_space=pl.ANY)] + [vmem] * 5,
        out_specs=[vmem] * 4,
        scratch_shapes=[
            pltpu.VMEM((BIG, BLK, BLK), bf16),
            pltpu.VMEM((NB, SEQ, BLK), f32),
            pltpu.VMEM((NB, SEQ, BLK), f32),
            pltpu.VMEM((NB, SEQ, BLK), f32),
            pltpu.VMEM((NB, SEQ, BLK), f32),
            pltpu.VMEM((NB, SEQ, BLK), f32),
            pltpu.VMEM((NB, SEQ, BLK), bf16),
            pltpu.VMEM((NB, SEQ, BLK), bf16),
            pltpu.VMEM((QB, SEQ, BLK), bf16),
            pltpu.VMEM((HB, SEQ, BLK), bf16),
            pltpu.VMEM((HB, SEQ, BLK), f32),
            pltpu.VMEM((HEADS, SEQ, SEQ), f32),
            pltpu.VMEM((NB, SEQ, BLK), f32),
            pltpu.VMEM((14, 8, D), f32),
            pltpu.VMEM((LANES, NEAR, 128), f32),
            pltpu.VMEM((B_DOWN + NB, 1, BLK), f32),
            pltpu.VMEM((8, D), f32),
            pltpu.VMEM((2 * NB + HB, 1, BLK), f32),
            pltpu.SemaphoreType.DMA((4,)),
        ],
        compiler_params=pltpu.CompilerParams(vmem_limit_bytes=54 << 20),
        cost_estimate=pl.CostEstimate(flops=2 * macs, bytes_accessed=BIG * BLK * BLK * 4, transcendentals=0),
        name="block_step",
    )(place, tiles, patches, noise, spots, near, mods)


def ada_front_body(row_ref, col_ref, cond_ref, tile_ref, out_ref):
    s = pl.program_id(0)

    @pl.when(s == 0)
    def _():
        out_ref[...] = jnp.zeros_like(out_ref)

    @pl.when(col_ref[s] >= 0)
    def _():
        c = col_ref[s]
        out_ref[c] = out_ref[c] + nn(cond_ref[row_ref[s]], tile_ref[0].astype(bf16))


def ada_front(row_of, col_of, cond_blocks, tile_master):
    per, images = tile_master.shape[0], cond_blocks.shape[1]
    return pl.pallas_call(
        ada_front_body,
        grid_spec=pltpu.PrefetchScalarGridSpec(
            num_scalar_prefetch=2,
            grid=(per,),
            in_specs=[
                pl.BlockSpec(cond_blocks.shape, lambda s, r, c: (0, 0, 0)),
                pl.BlockSpec((1, BLK, BLK), lambda s, r, c: (s, 0, 0)),
            ],
            out_specs=pl.BlockSpec((6 * NB, images, BLK), lambda s, r, c: (0, 0, 0)),
        ),
        out_shape=jax.ShapeDtypeStruct((6 * NB, images, BLK), f32),
        name="ada_front",
    )(row_of, col_of, cond_blocks, tile_master)


def ada_back_body(row_ref, col_ref, dmod_ref, tile_ref, out_ref):
    s = pl.program_id(0)

    @pl.when(s == 0)
    def _():
        out_ref[...] = jnp.zeros_like(out_ref)

    @pl.when(col_ref[s] >= 0)
    def _():
        r = row_ref[s]
        out_ref[r] = out_ref[r] + nt(dmod_ref[col_ref[s]], tile_ref[0].astype(bf16))


def ada_back(row_of, col_of, dmod_blocks, tile_master):
    per, images = tile_master.shape[0], dmod_blocks.shape[1]
    return pl.pallas_call(
        ada_back_body,
        grid_spec=pltpu.PrefetchScalarGridSpec(
            num_scalar_prefetch=2,
            grid=(per,),
            in_specs=[
                pl.BlockSpec(dmod_blocks.shape, lambda s, r, c: (0, 0, 0)),
                pl.BlockSpec((1, BLK, BLK), lambda s, r, c: (s, 0, 0)),
            ],
            out_specs=pl.BlockSpec((NB, images, BLK), lambda s, r, c: (0, 0, 0)),
        ),
        out_shape=jax.ShapeDtypeStruct((NB, images, BLK), f32),
        name="ada_back",
    )(row_of, col_of, dmod_blocks, tile_master)


def tile_grad_body(left_ref, right_ref, acts_ref, out_ref):
    s = pl.program_id(0)
    out_ref[0] = nn(acts_ref[left_ref[s]], acts_ref[right_ref[s]]).astype(bf16)


def tile_grads(left_of, right_of, acts):
    count = left_of.shape[0]
    return pl.pallas_call(
        tile_grad_body,
        grid_spec=pltpu.PrefetchScalarGridSpec(
            num_scalar_prefetch=2,
            grid=(count,),
            in_specs=[pl.BlockSpec(acts.shape, lambda s, a, b: (0, 0, 0))],
            out_specs=pl.BlockSpec((1, BLK, BLK), lambda s, a, b: (s, 0, 0)),
        ),
        out_shape=jax.ShapeDtypeStruct((count, BLK, BLK), bf16),
        compiler_params=pltpu.CompilerParams(vmem_limit_bytes=40 << 20),
        name="tile_grads",
    )(left_of, right_of, acts)


def adam_body(
    group, factors, where_ref, row_ref, col_ref,
    norm_ref, totals_ref, grads_ref, cond_ref, dmod_ref, bases_ref, moment_ref, second_ref, row_grad_ref, row_master_ref, row_moment_ref, row_second_ref,
    new_moment_ref, new_second_ref, update_ref, new_row_moment_ref, new_row_second_ref, row_update_ref,
    loss_ref, grad_norm_ref, act_rms_ref,
):
    step = pl.program_id(0)

    @pl.when(step == 0)
    def _():
        loss_ref[0] = totals_ref[0, 0] * factors[0]
        grad_norm_ref[0] = jnp.sqrt(norm_ref[...])[0, 0]
        roots = jnp.sqrt(totals_ref[...] * factors[1])
        for i in range(3):
            act_rms_ref[i] = roots[i + 1, 0]

    factor = clip_at / jnp.maximum(jnp.sqrt(norm_ref[0:1, 0:1]), clip_at)

    def moved(moment, second, grad):
        new_moment = beta_one * moment + (1.0 - beta_one) * grad
        new_second = beta_two * second + (1.0 - beta_two) * grad * grad
        return new_moment, new_second, new_moment / (jnp.sqrt(new_second) + adam_eps)

    for j in range(group):
        s = step * group + j
        r, c = row_ref[s], col_ref[s]
        cond = jnp.concatenate([cond_ref[2 * r], cond_ref[2 * r + 1]], axis=1)
        thin = tn(cond, dmod_ref[jnp.maximum(c, 0)]).astype(bf16)
        grad = jnp.where(c >= 0, thin, grads_ref[where_ref[s]])
        left, right = bases_ref[j, 0].astype(bf16), bases_ref[j, 1].astype(bf16)
        turned = factor * tn(left, nn(grad, right).astype(bf16))
        moment, second, direction = moved(moment_ref[j], second_ref[j], turned)
        new_moment_ref[j] = moment
        new_second_ref[j] = second
        update_ref[j] = -rate_step * nt(nn(left, direction.astype(bf16)).astype(bf16), right)

    moment, second, direction = moved(row_moment_ref[...], row_second_ref[...], factor * row_grad_ref[...])
    new_row_moment_ref[...] = moment
    new_row_second_ref[...] = second
    row_update_ref[...] = -rate_step * (direction + decay_rate * row_master_ref[...])


def adam(factors, where, row_of, col_of, norm, totals, grads, conds, dmod_blocks, bases, moment, second, row_grad, row_master, row_moment, row_second):
    per = moment.shape[0]
    group = next(g for g in (ADAM_GROUP, 3, 2, 1) if per % g == 0)
    steps = per // group
    tile = pl.BlockSpec((group, BLK, BLK), lambda s, *_: (s, 0, 0))
    row_count, columns = row_master.shape
    row = pl.BlockSpec((-(-row_count // (8 * steps)) * 8, columns), lambda s, *_: (s, 0))

    def whole(array):
        return pl.BlockSpec(array.shape, lambda s, *_: (0,) * array.ndim)

    shape = jax.ShapeDtypeStruct(moment.shape, f32)
    row_shape = jax.ShapeDtypeStruct(row_master.shape, f32)
    return pl.pallas_call(
        functools.partial(adam_body, group, factors),
        grid_spec=pltpu.PrefetchScalarGridSpec(
            num_scalar_prefetch=3,
            grid=(steps,),
            in_specs=[
                whole(norm),
                whole(totals),
                whole(grads),
                whole(conds),
                whole(dmod_blocks),
                pl.BlockSpec((group, 2, BLK, BLK), lambda s, *_: (s, 0, 0, 0)),
                tile,
                tile,
                row,
                row,
                row,
                row,
            ],
            out_specs=[tile] * 3 + [row] * 3 + [pl.BlockSpec(memory_space=pltpu.SMEM)] * 3,
        ),
        out_shape=[shape] * 3 + [row_shape] * 3 + [jax.ShapeDtypeStruct((n,), f32) for n in (1, 1, 3)],
        compiler_params=pltpu.CompilerParams(vmem_limit_bytes=61 << 20),
        name="adam",
    )(where, row_of, col_of, norm, totals, grads, conds, dmod_blocks, bases, moment, second, row_grad, row_master, row_moment, row_second)


def spread_body(
    cap, n_third,
    slot_ref, row_ref, col_ref, step_ref, name_ref, tiles_ref, rows_ref,
    out_ref, near_ref, mods_ref, freq_ref, label_ref, time_ref, cond_ref, pre_ref, own_cond_ref,
    tile, pack, ids, near, times, conds, near_wide, cond_group, product, part, part_out, part_in,
    load_sem, keep_sem, send_sem, recv_sem, small_send, small_recv,
):
    z, s = lax.axis_index("grp"), lax.axis_index("shard")
    per = tile.shape[0]
    images = GROUPS * SHARDS
    third = cap // 3
    both = cap - 2 * third
    x_at, y_at, c_at, z_at = (z, s ^ 2), (z, s ^ 4), (z, s ^ 1), (z ^ 1, s)
    far_z = [(lax.rem(z + i, GROUPS), s) for i in range(1, GROUPS)]
    near_s = [(z, s ^ i) for i in range(1, SHARDS)]

    barrier = pltpu.get_barrier_semaphore()
    for peer in far_z + near_s:
        pl.semaphore_signal(barrier, inc=1, device_id=peer, device_id_type=MESH_ID)
    load = pltpu.make_async_copy(tiles_ref, tile, load_sem)
    load.start()

    def block_rows(index, count):
        return pl.ds(pl.multiple_of(index * count, count), count)

    lane = lax.broadcasted_iota(jnp.int32, (8, 128), 1).astype(f32)
    angle = step_ref[0].astype(f32) * jnp.exp(-math.log(10000.0) * lane / (FREQ // 2))
    line = lax.broadcasted_iota(jnp.int32, (8, 128), 0)
    known = jnp.where(line == 0, jnp.cos(angle), jnp.where(line == 1, jnp.sin(angle), name_ref[0].astype(f32)))
    ids[block_rows(s * GROUPS + z, 8), :] = known
    near_wide[...] = jnp.zeros_like(near_wide)
    near_wide[: NEAR_REAL - 3, :] = rows_ref[NEAR_START : NEAR_START + NEAR_REAL - 3, :]
    near_wide[NEAR_REAL - 3 : NEAR_REAL, :] = rows_ref[NEAR_START + NEAR_REAL - 3 : NEAR_START + NEAR_REAL, :]
    near[s] = near_wide[...].astype(bf16)
    near_wide[...] = near_wide[...].astype(bf16).astype(f32)
    pl.semaphore_wait(barrier, len(far_z) + len(near_s))

    sent = []

    def push(src, dst, peer, index):
        copy = pltpu.make_async_remote_copy(
            src_ref=src, dst_ref=dst, send_sem=small_send.at[index], recv_sem=small_recv.at[index],
            device_id=peer, device_id_type=MESH_ID,
        )
        copy.start()
        sent.append(copy)
        return copy

    def to_group(stage, pairs):
        first = len(far_z) + stage * len(near_s)
        return [push(*pairs(peer[1]), peer, first + i) for i, peer in enumerate(near_s)]

    def got(copies):
        for copy in copies:
            copy.wait_recv()

    own_ids = ids.at[block_rows(s * GROUPS + z, 8)]
    id_far = [push(own_ids, own_ids, peer, i) for i, peer in enumerate(far_z)]
    near_copies = to_group(0, lambda p: (near.at[s], near.at[s]))

    parity = lax.rem(z, 2)
    starts = (both + parity * third, 0, both + third - parity * third)

    def chunk_of(index):
        kind, at = divmod(index, n_third)
        size = both if kind == 1 else third
        first, last = at * size // n_third, (at + 1) * size // n_third
        return starts[kind] + first, last - first

    def chunk(index):
        return pl.ds(*chunk_of(index))

    load.wait()
    big = []

    def send(kind, stream, index, peer, src, owner, arrives):
        copy = pltpu.make_async_remote_copy(
            src_ref=src, dst_ref=out_ref.at[owner, chunk(index)],
            send_sem=send_sem.at[kind, index], recv_sem=recv_sem.at[stream, arrives],
            device_id=peer, device_id_type=MESH_ID,
        )
        copy.start()
        big.append(copy)

    def wait_for(stream, index, owner):
        place = out_ref.at[owner, chunk(index)]
        pltpu.make_async_remote_copy(
            src_ref=place, dst_ref=place, send_sem=send_sem.at[0, index], recv_sem=recv_sem.at[stream, index],
            device_id=x_at, device_id_type=MESH_ID,
        ).wait_recv()

    def pack_chunk(index):
        start, count = chunk_of(index)

        def one(i, unused):
            p = start + i
            pack[p] = tile[slot_ref[p]].astype(bf16)
            return unused

        lax.fori_loop(0, count, one, 0)

    def send_mine(index):
        src = pack.at[chunk(index)]
        if index < 2 * n_third:
            send(0, 0, index, x_at, src, s, index)
            send(1, 1, index, y_at, src, s, index)
        send(2, 3, index, c_at, src, s, index)

    owners = (s ^ 2, s ^ 4, s ^ 6)

    def pass_on(which, index):
        owner = owners[which]
        wait_for(which, index, owner)
        here = out_ref.at[owner, chunk(index)]
        if index < 2 * n_third:
            if which == 0 and index % 2 == 0:
                send(6, 2, index, y_at, here, owner, index)
            if which == 1 and index % 2 == 1:
                send(7, 2, index, x_at, here, owner, index)
        if index < n_third:
            send(8 + which, which, index, z_at, here, owner, 2 * n_third + index)
        send(3 + which, 4 + which, index, c_at, here, owner, index)

    for j in range(n_third):
        pack_chunk(j)
        send_mine(j)
    got(id_far)
    span = block_rows(s, 8 * GROUPS)
    id_near = to_group(1, lambda p: (ids.at[span], ids.at[span]))
    for j in range(n_third, 3 * n_third):
        pack_chunk(j)
    keep = pltpu.make_async_copy(pack, out_ref.at[s, pl.ds(0, cap)], keep_sem)
    keep.start()
    stages = {}

    def silu_low(value):
        return (value * jax.nn.sigmoid(value)).astype(bf16)

    def row_slice(start, count):
        return rows_ref[start : start + count, :].astype(bf16)

    def time_stage():
        got(id_near)
        freq = jnp.concatenate([ids[pl.ds(i, images, stride=8), :] for i in range(2)], axis=1).astype(bf16)
        freq_ref[...] = freq
        label_ref[...] = ids[pl.ds(2, images, stride=8), :]
        pre = nn(freq, row_slice(NCLASS, FREQ)) + near_wide[N_TIME1 : N_TIME1 + 1, :]
        pre_ref[...] = pre
        times[s] = silu_low(pre)
        stages["time"] = to_group(2, lambda p: (times.at[s], times.at[s]))

    def cond_stage():
        got(stages["time"])
        total = jnp.zeros((images, 128), f32) + near_wide[N_TIME2 : N_TIME2 + 1, :]
        for o in range(SHARDS):
            total += nn(times[o], row_slice(NCLASS + FREQ + o * 128, 128))
        hot = label_ref[...].astype(jnp.int32)[:, :1] == lax.broadcasted_iota(jnp.int32, (images, D), 1)
        total += nn(hot.astype(bf16), row_slice(0, D))
        own_cond_ref[...] = total
        conds[s] = silu_low(total)
        stages["cond"] = to_group(3, lambda p: (conds.at[s], conds.at[s]))

    def group_stage():
        got(stages["cond"])
        at = lax.broadcasted_iota(jnp.int32, (SHARDS, images), 1)
        row = lax.broadcasted_iota(jnp.int32, (SHARDS, images), 0)
        pick = (at == row * GROUPS + z).astype(bf16)
        for o in range(SHARDS):
            half = o % 2
            cond_group[o // 2, :, half * 128 : (half + 1) * 128] = nn(pick, conds[o])

    def ada_stage(start, count):
        for j in range(start, start + count):
            product[j] = nn(cond_group[row_ref[j]].astype(bf16), tile[j].astype(bf16))

    def part_stage():
        part[...] = jnp.zeros_like(part)

        def column(c, unused):
            total = jnp.zeros((SHARDS, BLK), f32)
            for j in range(per):
                total += jnp.where(col_ref[j] == c, 1.0, 0.0) * product[j]
            for half in range(2):
                part[block_rows(2 * c + half, 8), :] = total[:, half * 128 : (half + 1) * 128]
            return unused

        lax.fori_loop(0, 6 * NB, column, 0)
        for i in range(6):
            place = block_rows(i * LANES + s, 8)
            part[place, :] = part[place, :] + near_wide[N_ADA + i : N_ADA + i + 1, :]
        for i in range(2):
            total = jnp.zeros((SHARDS, 128), f32) + near_wide[N_FINAL + i : N_FINAL + i + 1, :]
            for r in range(NB):
                weight = row_slice(NCLASS + FREQ + D + i * D + r * BLK, BLK)
                total += nn(cond_group[r].astype(bf16), weight)
            part[block_rows((6 + i) * LANES + s, 8), :] = total
        for o in range(SHARDS):
            part_out[o] = part[pl.ds(o, 8 * LANES, stride=8), :]
        part_in[s] = part_out[s]
        stages["part"] = to_group(4, lambda p: (part_out.at[p], part_in.at[s]))

    def mod_stage():
        got(stages["part"])
        total = part_in[0]
        for o in range(1, SHARDS):
            total += part_in[o]
        mods_ref[...] = total
        got(near_copies)
        near_ref[...] = near[...]
        time_ref[...] = times[...]
        cond_ref[...] = conds[...]

    cut = per // 3
    hooks = [
        (0.10, time_stage), (0.30, cond_stage), (0.50, group_stage), (0.55, lambda: ada_stage(0, cut)),
        (0.60, lambda: ada_stage(cut, cut)), (0.65, lambda: ada_stage(2 * cut, per - 2 * cut)), (0.70, part_stage), (2.0, mod_stage),
    ]
    seen = [0]
    steps = [0]

    def hook(last=False):
        steps[0] += 1
        while hooks and (last or steps[0] >= hooks[0][0] * 3 * n_third):
            hooks.pop(0)[1]()

    def z_next():
        order = [(w, 2 * n_third + j) for j in range(n_third) for w in (0, 1)]
        order += [(2, 2 * n_third + j) for j in range(n_third)]
        if seen[0] < len(order):
            pass_on(*order[seen[0]])
            seen[0] += 1

    for j in range(n_third):
        pass_on(0, j)
        pass_on(1, j)
        hook()
        if j:
            z_next()
    for j in range(n_third, 3 * n_third):
        send_mine(j)
    for j in range(n_third):
        pass_on(2, j)
        if j % 2:
            z_next()
            hook()
    for j in range(n_third, 2 * n_third):
        pass_on(0, j)
        pass_on(1, j)
        hook()
        z_next()
    for j in range(n_third, 2 * n_third):
        pass_on(2, j)
        if j % 2:
            z_next()
            hook()
    while seen[0] < 3 * n_third:
        z_next()
    hook(last=True)
    for index in range(3 * n_third):
        wait_for(3, index, s ^ 1)
        for which in range(3):
            wait_for(4 + which, index, owners[which] ^ 1)
    keep.wait()
    for copy in big + sent:
        copy.wait_send()


def spread(cap, slot_of, row_of, col_of, timesteps, labels, tile_master, row_master):
    per = tile_master.shape[0]
    n_third = 5
    images = GROUPS * SHARDS
    vmem = pl.BlockSpec(memory_space=pltpu.VMEM)
    smem = pl.BlockSpec(memory_space=pltpu.SMEM)
    anywhere = pl.BlockSpec(memory_space=pl.ANY)
    small = (GROUPS - 1) + 5 * (SHARDS - 1)
    return pl.pallas_call(
        functools.partial(spread_body, cap, n_third),
        out_shape=[
            jax.ShapeDtypeStruct((SHARDS, per, BLK, BLK), bf16),
            jax.ShapeDtypeStruct((LANES, NEAR, 128), bf16),
            jax.ShapeDtypeStruct((8 * LANES, 128), f32),
            jax.ShapeDtypeStruct((images, FREQ), bf16),
            jax.ShapeDtypeStruct((images, 128), f32),
            jax.ShapeDtypeStruct((SHARDS, images, 128), bf16),
            jax.ShapeDtypeStruct((SHARDS, images, 128), bf16),
            jax.ShapeDtypeStruct((images, 128), f32),
            jax.ShapeDtypeStruct((images, 128), f32),
        ],
        in_specs=[smem] * 5 + [anywhere, vmem],
        out_specs=[anywhere] + [vmem] * 8,
        scratch_shapes=[
            pltpu.VMEM((per, BLK, BLK), f32),
            pltpu.VMEM((cap, BLK, BLK), bf16),
            pltpu.VMEM((images * 8, 128), f32),
            pltpu.VMEM((LANES, NEAR, 128), bf16),
            pltpu.VMEM((SHARDS, images, 128), bf16),
            pltpu.VMEM((SHARDS, images, 128), bf16),
            pltpu.VMEM((NEAR, 128), f32),
            pltpu.VMEM((NB, SHARDS, BLK), f32),
            pltpu.VMEM((per, SHARDS, BLK), f32),
            pltpu.VMEM((8 * LANES * 8, 128), f32),
            pltpu.VMEM((SHARDS, 8 * LANES, 128), f32),
            pltpu.VMEM((SHARDS, 8 * LANES, 128), f32),
            pltpu.SemaphoreType.DMA,
            pltpu.SemaphoreType.DMA,
            pltpu.SemaphoreType.DMA((11, 3 * n_third)),
            pltpu.SemaphoreType.DMA((7, 3 * n_third)),
            pltpu.SemaphoreType.DMA((small,)),
            pltpu.SemaphoreType.DMA((small,)),
        ],
        compiler_params=pltpu.CompilerParams(collective_id=cap, has_side_effects=True, vmem_limit_bytes=61 << 20),
        name="spread",
    )(slot_of, row_of, col_of, timesteps, labels, tile_master, row_master)

RING = 6
SUM_LAG = 2
Z_STEP = 1
Z_LAG = SUM_LAG + 4 * Z_STEP
ADA_PARTS = 6


def collect_body(
    cap, ch,
    left_ref, right_ref, row_ref, col_ref, count_ref,
    acts_ref, dmod_ref, ends_ref, stats_ref, time_ref, cond_ref, freq_ref, label_ref, pre_ref, own_cond_ref, rows_ref, tiles_ref,
    grads_ref, d_blocks_ref, own_rows_ref, norm_ref, stat_ref,
    out_c, in_c, out_d, out_x, out_y, in_dx, in_dy, in_x, in_y, total, low_in, high_in, final,
    tile, product, all_d, wide_d, all_stats, tok_out, tok_in, tok_z, tokens, part_out, part_in, pre_out, pre_in, own_dcond, own_dpre,
    vectors, squares, square_in,
    c_send, c_recv, d_send, dx_recv, dy_recv, x_send, x_recv, y_send, y_recv, up_send, low_recv, high_recv, final_recv, down_send,
    keep_sem, load_sem, small_send, small_recv,
):
    z, s = lax.axis_index("grp"), lax.axis_index("shard")
    per = product.shape[0]
    images = GROUPS * SHARDS
    chunks = cap // ch
    x_at, y_at, c_at = (z, s ^ 2), (z, s ^ 4), (z, s ^ 1)
    far_z = [(lax.rem(z + i, GROUPS), s) for i in range(1, GROUPS)]
    near_s = [(z, s ^ i) for i in range(1, SHARDS)]
    half = BLK // 2
    upper, lower = pl.ds(0, half), pl.ds(half, half)

    barrier = pltpu.get_barrier_semaphore()
    for peer in far_z + near_s:
        pl.semaphore_signal(barrier, inc=1, device_id=peer, device_id_type=MESH_ID)

    def remote(src, dst, sent, received, peer):
        return pltpu.make_async_remote_copy(
            src_ref=src, dst_ref=dst, send_sem=sent, recv_sem=received, device_id=peer, device_id_type=MESH_ID
        )

    def block_rows(index, count):
        return pl.ds(pl.multiple_of(index * count, count), count)

    def far(stage, src, dst):
        return [
            remote(src, dst, small_send.at[stage * 3 + i], small_recv.at[stage * 3 + i], peer) for i, peer in enumerate(far_z)
        ]

    def group(stage, src_of, dst):
        first = 9 + stage * 7
        return [
            remote(src_of(peer[1]), dst, small_send.at[first + i], small_recv.at[first + i], peer)
            for i, peer in enumerate(near_s)
        ]

    def direct(stage, ref):
        first = 9 + stage * 7
        return [
            remote(ref, ref, small_send.at[first + i], small_recv.at[first + i], peer)
            for i, peer in enumerate((x_at, y_at, (z, s ^ 6), c_at))
        ]

    def passed(stage, ref_of):
        first = 9 + stage * 7 + 4
        return [
            remote(ref_of(o), ref_of(o), small_send.at[first + i], small_recv.at[first + i], c_at)
            for i, o in enumerate((s ^ 2, s ^ 4, s ^ 6))
        ]

    own_d = all_d.at[block_rows(s * GROUPS + z, 8 * LANES)]
    own_stat = all_stats.at[block_rows(s * GROUPS + z, 8)]
    group_d = all_d.at[block_rows(s, 8 * LANES * GROUPS)]
    group_stat = all_stats.at[block_rows(s, 8 * GROUPS)]

    def small_copies(name):
        if name == "d_far":
            return far(0, own_d, own_d)
        if name == "stat_far":
            return far(1, own_stat, own_stat)
        if name == "tok_far":
            return far(2, tok_z.at[z], tok_z.at[z])
        if name == "tok":
            return group(0, lambda p: tok_out.at[p], tok_in.at[s])
        if name == "d":
            return direct(1, group_d)
        if name == "stat":
            return direct(2, group_stat)
        if name == "d_more":
            return passed(1, lambda o: all_d.at[block_rows(o, 8 * LANES * GROUPS)])
        if name == "stat_more":
            return passed(2, lambda o: all_stats.at[block_rows(o, 8 * GROUPS)])
        if name == "part":
            return group(3, lambda p: part_out.at[p], part_in.at[s])
        if name == "pre":
            return group(4, lambda p: pre_out.at[p], pre_in.at[s])
        return group(5, lambda p: square_in.at[s], square_in.at[s])

    def begin(*names):
        for name in names:
            for copy in small_copies(name):
                copy.start()

    def got(*names):
        for name in names:
            for copy in small_copies(name):
                copy.wait_recv()

    def load(part):
        count = tile.shape[0]
        return pltpu.make_async_copy(tiles_ref.at[pl.ds(part * count, count)], tile, load_sem)

    load(0).start()
    own_d[...] = dmod_ref[...].astype(bf16)
    own_stat[...] = stats_ref[...]
    tok_out[...] = ends_ref[...].astype(bf16)
    tok_in[s] = tok_out[s]
    squares[...] = jnp.zeros_like(squares)
    pl.semaphore_wait(barrier, len(far_z) + len(near_s))
    begin("d_far", "stat_far", "tok")

    def spread_stage():
        got("d_far", "stat_far")
        begin("d", "stat")
        got("tok")
        value = tok_in[0].astype(f32)
        for o in range(1, SHARDS):
            value += tok_in[o].astype(f32)
        tok_z[z] = value
        begin("tok_far")

    def pass_stage():
        got("d", "stat")
        begin("d_more", "stat_more")

    def order_stage():
        got("d_more", "stat_more", "tok_far")
        value = tok_z[0]
        for i in range(1, GROUPS):
            value += tok_z[i]
        tokens[...] = value
        value = all_stats[pl.ds(0, 8), :]
        for i in range(1, images):
            value += all_stats[pl.ds(8 * i, 8), :]
        stat_ref[...] = value

        def widen(i, unused):
            place = block_rows(i, 8 * LANES)
            wide_d[place, :] = all_d[place, :].astype(f32)
            return unused

        lax.fori_loop(0, images, widen, 0)
        for q in range(6 * LANES):
            d_blocks_ref[q // 2, :, (q % 2) * 128 : (q % 2 + 1) * 128] = wide_d[
                pl.ds(q, images, stride=8 * LANES), :
            ].astype(bf16)

    def own_columns(i):
        return wide_d[pl.ds(i * LANES + s, images, stride=8 * LANES), :]

    def ada_stage(part):
        count = tile.shape[0]
        load(part).wait()

        for j in range(count):
            at = part * count + j
            product[at] = nt(d_blocks_ref[jnp.maximum(col_ref[at], 0)], tile[j].astype(bf16))
        if (part + 1) * count < per:
            load(part + 1).start()

    def row_slice(start, count):
        return rows_ref[start : start + count, :].astype(bf16)

    final_at = NCLASS + FREQ + D

    def part_stage():
        def add(j, values):
            chosen = [jnp.logical_and(col_ref[j] >= 0, row_ref[j] == r) for r in range(NB)]
            return tuple(value + jnp.where(one, 1.0, 0.0) * product[j] for one, value in zip(chosen, values))

        values = []
        for r in range(NB):
            value = jnp.zeros((images, BLK), f32)
            for i in range(2):
                value += nt(own_columns(6 + i).astype(bf16), row_slice(final_at + i * D + r * BLK, BLK))
            values.append(value)
        values = lax.fori_loop(0, per, add, tuple(values))
        for r in range(NB):
            for i in range(2):
                part_out[2 * r + i] = values[r][:, i * 128 : (i + 1) * 128].astype(bf16)
        part_in[s] = part_out[s]
        begin("part")

    def slope(value):
        gate = jax.nn.sigmoid(value)
        return gate * (1.0 + value * (1.0 - gate))

    def cond_stage():
        got("part")
        value = part_in[0].astype(f32)
        for o in range(1, SHARDS):
            value += part_in[o].astype(f32)
        value = value * slope(own_cond_ref[...])
        own_dcond[...] = value
        for o in range(SHARDS):
            pre_out[o] = nt(value.astype(bf16), row_slice(NCLASS + FREQ + o * 128, 128)).astype(bf16)
        pre_in[s] = pre_out[s]
        begin("pre")

    def row_stage():
        got("pre")
        value = pre_in[0].astype(f32)
        for o in range(1, SHARDS):
            value += pre_in[o].astype(f32)
        value = value * slope(pre_ref[...])
        own_dpre[...] = value
        dpre_low, dcond = value.astype(bf16), own_dcond[...]
        dcond_low = dcond.astype(bf16)
        gathered = []

        def keep(start, value):
            own_rows_ref[start : start + value.shape[0], :] = value
            gathered.append(fold(value * value))

        hot = label_ref[...].astype(jnp.int32)[:, :1] == lax.broadcasted_iota(jnp.int32, (images, NCLASS), 1)
        keep(
            0,
            lax.dot_general(
                hot.astype(f32), dcond, (((0,), (0,)), ((), ())), preferred_element_type=f32, precision=lax.Precision.HIGHEST
            ),
        )
        keep(NCLASS, tn(freq_ref[...], dpre_low))
        for o in range(SHARDS):
            keep(NCLASS + FREQ + o * 128, tn(time_ref[o], dcond_low))
            for i in range(2):
                keep(final_at + i * D + o * 128, tn(cond_ref[o], own_columns(6 + i).astype(bf16)))
        keep(NEAR_START, tokens[: 2 * PATCH_DIM, :])

        vectors[...] = jnp.zeros_like(vectors)

        def vector(row, value):
            vectors[row : row + 1, :] = value

        vector(0, tokens[T_PATCH : T_PATCH + 1, :])
        vector(1, jnp.sum(value, axis=0, keepdims=True))
        vector(2, jnp.sum(dcond, axis=0, keepdims=True))
        vector(3, tokens[T_QUERY : T_QUERY + 1, :])
        vector(4, tokens[T_VALUE : T_VALUE + 1, :])
        vector(5, tokens[T_OUT : T_OUT + 1, :])
        vector(6, tokens[T_DOWN : T_DOWN + 1, :])
        for i in range(8):
            vector(7 + i if i < 6 else 7 + i + FF // D, jnp.sum(own_columns(i), axis=0, keepdims=True))
        for i in range(FF // D):
            vector(13 + i, tokens[T_UP + i : T_UP + i + 1, :])
        start = NEAR_START + 2 * PATCH_DIM
        rest = own_rows_ref.shape[0] - start
        whole = rest // 8 * 8
        own_rows_ref[start : start + whole, :] = vectors[:whole, :]
        own_rows_ref[start + whole : start + rest, :] = vectors[whole:rest, :]
        value = fold(vectors[...] * vectors[...])
        for piece in gathered:
            value += piece
        squares[:, :128] = squares[:, :128] + value

    def slot_of(i):
        return lax.rem(i + 2 * RING, RING)

    def block(owner, p):
        at = owner * per + p
        return nn(acts_ref[left_ref[at]], acts_ref[right_ref[at]])

    targets = (s ^ 6, s ^ 2, s ^ 4, s)

    def c_copy(slot, item):
        return remote(out_c.at[slot, item], in_c.at[slot, item], c_send.at[slot, item], c_recv.at[slot, item], c_at)

    def dx_copy(slot):
        return remote(out_d.at[slot, :, upper], in_dx.at[slot], d_send.at[slot, 0], dx_recv.at[slot], x_at)

    def dy_copy(slot):
        return remote(out_d.at[slot, :, lower], in_dy.at[slot], d_send.at[slot, 1], dy_recv.at[slot], y_at)

    def x_copy(slot):
        return remote(out_x.at[slot], in_x.at[slot], x_send.at[slot], x_recv.at[slot], x_at)

    def y_copy(slot):
        return remote(out_y.at[slot], in_y.at[slot], y_send.at[slot], y_recv.at[slot], y_at)

    def inside(i):
        return jnp.logical_and(i >= 0, i < chunks)

    def each(body):
        if ch == 1:
            body(0)
            return

        def one(c, unused):
            body(c)
            return unused

        lax.fori_loop(0, ch, one, 0)

    def for_sibling(n):
        slot = slot_of(n)
        for items, at in (((0,), n + 1), ((1, 2, 3), n)):

            @pl.when(inside(at))
            def _():
                for item in items:
                    each(lambda c: out_c.__setitem__((slot, item, c), block(targets[item] ^ 1, at * ch + c).astype(bf16)))
                for item in items:
                    c_copy(slot, item).start()

    def for_owners(i):
        slot, before = slot_of(i), slot_of(i - 1)

        @pl.when(inside(i + 1))
        def _():
            c_copy(slot, 0).wait_recv()

            def one(c):
                value = block(targets[0], (i + 1) * ch + c) + in_c[slot, 0, c].astype(f32)
                out_d[slot, c] = value.astype(bf16)

            each(one)
            dx_copy(slot).start()
            dy_copy(slot).start()

        @pl.when(inside(i))
        def _():
            for item in (1, 2, 3):
                c_copy(slot, item).wait_recv()
            dy_copy(before).wait_recv()
            dx_copy(before).wait_recv()

            def one(c):
                value = block(targets[1], i * ch + c) + in_c[slot, 1, c].astype(f32)
                out_x[slot, c, upper] = value[:half].astype(bf16)
                out_x[slot, c, lower] = (value[half:] + in_dy[before, c].astype(f32)).astype(bf16)

            def two(c):
                value = block(targets[2], i * ch + c) + in_c[slot, 2, c].astype(f32)
                out_y[slot, c, upper] = (value[:half] + in_dx[before, c].astype(f32)).astype(bf16)
                out_y[slot, c, lower] = value[half:].astype(bf16)

            def three(c):
                value = block(targets[3], i * ch + c) + in_c[slot, 3, c].astype(f32)
                total[i * ch + c] = value.astype(bf16)

            each(one)
            each(two)
            x_copy(slot).start()
            y_copy(slot).start()
            each(three)

        old = slot_of(i - SUM_LAG)

        @pl.when(inside(i - SUM_LAG))
        def _():
            x_copy(old).wait_recv()
            y_copy(old).wait_recv()

            def one(c):
                at = (i - SUM_LAG) * ch + c
                value = total[at].astype(f32) + in_x[old, c].astype(f32) + in_y[old, c].astype(f32)
                total[at] = value.astype(bf16)

            each(one)

    def along(j):
        even = lax.rem(j, 2) == 0
        rank = jnp.where(even, z, GROUPS - 1 - z)
        down = jnp.where(even, lax.rem(z + GROUPS - 1, GROUPS), lax.rem(z + 1, GROUPS))
        up = jnp.where(even, lax.rem(z + 1, GROUPS), lax.rem(z + GROUPS - 1, GROUPS))
        return rank, (down, s), (up, s)

    def z_copy(name, j):
        _, down, up = along(j)
        span = pl.ds(j * ch, ch)
        if name == "rise":
            return remote(total.at[span], low_in.at[span], up_send.at[j], low_recv.at[j], up)
        if name == "sink":
            return remote(total.at[span], high_in.at[span], up_send.at[j], high_recv.at[j], down)
        if name == "final_down":
            return remote(final.at[span], final.at[span], down_send.at[0, j], final_recv.at[j], down)
        return remote(final.at[span], final.at[span], down_send.at[1, j], final_recv.at[j], up)

    def over_z(i):
        j = i - SUM_LAG

        @pl.when(inside(j))
        def _():
            rank, _, _ = along(j)

            @pl.when(rank == 0)
            def _():
                z_copy("rise", j).start()

            @pl.when(rank == 3)
            def _():
                z_copy("sink", j).start()

        j2 = j - Z_STEP

        @pl.when(jnp.logical_and(inside(j2), along(j2)[0] == 2))
        def _():
            z_copy("sink", j2).wait_recv()

            def one(c):
                at = j2 * ch + c
                total[at] = (total[at].astype(f32) + high_in[at].astype(f32)).astype(bf16)

            each(one)
            z_copy("sink", j2).start()

        j3 = j - 2 * Z_STEP

        @pl.when(jnp.logical_and(inside(j3), along(j3)[0] == 1))
        def _():
            z_copy("rise", j3).wait_recv()
            z_copy("sink", j3).wait_recv()

            def one(c):
                at = j3 * ch + c
                value = total[at].astype(f32) + low_in[at].astype(f32) + high_in[at].astype(f32)
                final[at] = value.astype(bf16)

            each(one)
            z_copy("final_down", j3).start()
            z_copy("final_up", j3).start()

        j4 = j - 3 * Z_STEP

        @pl.when(jnp.logical_and(inside(j4), along(j4)[0] == 2))
        def _():
            z_copy("final_up", j4).wait_recv()
            z_copy("final_up", j4).start()

        j5 = i - Z_LAG

        @pl.when(inside(j5))
        def _():
            rank = along(j5)[0]

            @pl.when(jnp.logical_or(rank == 0, rank == 3))
            def _():
                z_copy("final_up", j5).wait_recv()

            span = pl.ds(j5 * ch, ch)
            pltpu.make_async_copy(final.at[span], grads_ref.at[span], keep_sem.at[j5]).start()

            def one(c):
                at = j5 * ch + c
                value = final[at].astype(f32) * jnp.where(at < count_ref[0], 1.0, 0.0)
                squares[...] = squares[...] + fold(value * value)

            each(one)

    def settle(i):
        n = i - 2
        slot = slot_of(n)
        for item in range(4):

            @pl.when(inside(n + 1 if item == 0 else n))
            def _():
                c_copy(slot, item).wait_send()

        n2 = i - 3
        slot2 = slot_of(n2)

        @pl.when(inside(n2 + 1))
        def _():
            dx_copy(slot2).wait_send()
            dy_copy(slot2).wait_send()

        @pl.when(inside(n2))
        def _():
            x_copy(slot2).wait_send()
            y_copy(slot2).wait_send()

    hooks = {
        0: spread_stage, 3: pass_stage, 6: order_stage, 13: part_stage, 17: cond_stage, 21: row_stage,
    }
    hooks.update({7 + part: functools.partial(ada_stage, part) for part in range(ADA_PARTS)})

    for_sibling(-1)

    def iteration(step, unused):
        i = step - 1
        for_sibling(i + 1)
        for_owners(i)
        over_z(i)
        settle(i)
        for at, stage in hooks.items():
            pl.when(i == at)(stage)
        return unused

    lax.fori_loop(0, chunks + 1 + Z_LAG, iteration, 0)

    square_in[s] = jnp.zeros((8, 128), f32) + jnp.sum(squares[...])
    begin("square")

    cond_gram = jnp.zeros((images, images), f32)
    for o in range(SHARDS):
        cond_gram += nt(cond_ref[o], cond_ref[o])

    def gram(c, value):
        return value + nt(d_blocks_ref[c], d_blocks_ref[c])

    d_gram = lax.fori_loop(0, 6 * NB, gram, jnp.zeros((images, images), f32))
    got("square")
    value = square_in[0]
    for o in range(1, SHARDS):
        value += square_in[o]
    norm_ref[...] = value + jnp.sum(cond_gram * d_gram)

    def finish(j, unused):
        span = pl.ds(j * ch, ch)
        pltpu.make_async_copy(final.at[span], grads_ref.at[span], keep_sem.at[j]).wait()
        rank = along(j)[0]

        @pl.when(rank == 0)
        def _():
            z_copy("rise", j).wait_send()

        @pl.when(rank >= 2)
        def _():
            z_copy("sink", j).wait_send()

        @pl.when(rank == 1)
        def _():
            z_copy("final_down", j).wait_send()

        @pl.when(jnp.logical_or(rank == 1, rank == 2))
        def _():
            z_copy("final_up", j).wait_send()

        return unused

    lax.fori_loop(0, chunks, finish, 0)
    for name in ("d_far", "stat_far", "tok_far", "tok", "d", "stat", "d_more", "stat_more", "part", "pre", "square"):
        for copy in small_copies(name):
            copy.wait_send()


def collect(cap, left_of, right_of, row_of, col_of, count, acts, dmod, ends, stats, times, conds, freq_low, label, own_pre, own_cond,
            row_master, tile_master):
    per = tile_master.shape[0]
    ch = 1
    chunks = cap // ch
    images = GROUPS * SHARDS
    vmem = pl.BlockSpec(memory_space=pltpu.VMEM)
    smem = pl.BlockSpec(memory_space=pltpu.SMEM)
    anywhere = pl.BlockSpec(memory_space=pl.ANY)
    small = 9 + 6 * (SHARDS - 1)
    dma = pltpu.SemaphoreType.DMA

    def blocks(*lead):
        return pltpu.VMEM(lead + (BLK, BLK), bf16)

    return pl.pallas_call(
        functools.partial(collect_body, cap, ch),
        out_shape=[
            jax.ShapeDtypeStruct((per, BLK, BLK), bf16),
            jax.ShapeDtypeStruct((6 * NB, images, BLK), bf16),
            jax.ShapeDtypeStruct(row_master.shape, f32),
            jax.ShapeDtypeStruct((8, 128), f32),
            jax.ShapeDtypeStruct((8, 128), f32),
        ],
        in_specs=[smem] * 5 + [vmem] * 11 + [anywhere],
        out_specs=[anywhere] + [vmem] * 4,
        scratch_shapes=[
            blocks(RING, 4, ch),
            blocks(RING, 4, ch),
            blocks(RING, ch),
            blocks(RING, ch),
            blocks(RING, ch),
            pltpu.VMEM((RING, ch, BLK // 2, BLK), bf16),
            pltpu.VMEM((RING, ch, BLK // 2, BLK), bf16),
            blocks(RING, ch),
            blocks(RING, ch),
            blocks(cap),
            blocks(cap),
            blocks(cap),
            blocks(cap),
            pltpu.VMEM((per // ADA_PARTS, BLK, BLK), f32),
            pltpu.VMEM((per, images, BLK), f32),
            pltpu.VMEM((images * 8 * LANES, 128), bf16),
            pltpu.VMEM((images * 8 * LANES, 128), f32),
            pltpu.VMEM((images * 8, 128), f32),
            pltpu.VMEM((SHARDS, TOKEN_ROWS, 128), bf16),
            pltpu.VMEM((SHARDS, TOKEN_ROWS, 128), bf16),
            pltpu.VMEM((GROUPS, TOKEN_ROWS, 128), f32),
            pltpu.VMEM((TOKEN_ROWS, 128), f32),
            pltpu.VMEM((SHARDS, images, 128), bf16),
            pltpu.VMEM((SHARDS, images, 128), bf16),
            pltpu.VMEM((SHARDS, images, 128), bf16),
            pltpu.VMEM((SHARDS, images, 128), bf16),
            pltpu.VMEM((images, 128), f32),
            pltpu.VMEM((images, 128), f32),
            pltpu.VMEM((24, 128), f32),
            pltpu.VMEM((8, BLK), f32),
            pltpu.VMEM((SHARDS, 8, 128), f32),
            dma((RING, 4)),
            dma((RING, 4)),
            dma((RING, 2)),
            dma((RING,)),
            dma((RING,)),
            dma((RING,)),
            dma((RING,)),
            dma((RING,)),
            dma((RING,)),
            dma((chunks,)),
            dma((chunks,)),
            dma((chunks,)),
            dma((chunks,)),
            dma((2, chunks)),
            dma((chunks,)),
            dma,
            dma((small,)),
            dma((small,)),
        ],
        compiler_params=pltpu.CompilerParams(
            collective_id=100 + cap, has_side_effects=True, vmem_limit_bytes=50 << 20
        ),
        name="collect",
    )(left_of, right_of, row_of, col_of, count, acts, dmod, ends, stats, times, conds, freq_low, label, own_pre, own_cond,
      row_master, tile_master)


def position_table(grid_side, model_width):
    quarter = model_width // 4
    omega = 1.0 / 10000.0 ** (jnp.arange(quarter, dtype=f32) / quarter)
    angle = jnp.arange(grid_side).astype(f32)[:, None] * omega[None, :]
    return jnp.stack([jnp.sin(angle), jnp.cos(angle)])


def time_freq(step_values, freq_width):
    half_width = freq_width // 2
    freqs = jnp.exp(-math.log(10000.0) * jnp.arange(half_width, dtype=f32) / half_width)
    angle_arg = step_values.astype(f32)[:, None] * freqs[None, :]
    return jnp.concatenate([jnp.cos(angle_arg), jnp.sin(angle_arg)], axis=1)


def silu_slope(value):
    gate = jax.nn.sigmoid(value)
    return gate * (1.0 + value * (1.0 - gate))


def blocked(array):
    count = array.shape[0]
    return array.reshape(count, -1, BLK).transpose(1, 0, 2)


def factors_of(block):
    n = jnp.maximum(block - ADA, 0)
    out, up, down = n - AT_OUT, n - AT_UP, n - AT_DOWN
    row = lax.div(n, jnp.int32(QB))
    left = jnp.where(n < AT_OUT, L_ATT + row, jnp.where(n < AT_UP, L_OUT + (out >> 2), jnp.where(n < AT_DOWN, L_MLP + (up >> 4), L_HID + (down >> 2))))
    right = jnp.where(
        n < AT_OUT,
        R_QKV + n - row * QB,
        jnp.where(n < AT_UP, R_OUT + (out & (NB - 1)), jnp.where(n < AT_DOWN, R_UP + (up & (HB - 1)), R_DOWN + (down & (NB - 1)))),
    )
    return left, right


def places_body(
    per, assign_ref, slot_ref, row_ref, col_ref, rank_ref, inverse_ref, left_ref, right_ref, count_ref, tier_ref
):
    me = lax.axis_index("shard")

    def place_in(block, s, before):
        return jnp.where(block < ADA, per - 1 - (s - before), before), before + jnp.where(block < ADA, 0, 1)

    def owner(o, most):
        def slot(s, before):
            block = assign_ref[o * per + s]
            p, after = place_in(block, s, before)
            place = o * per + p
            inverse_ref[block] = place
            left, right = factors_of(block)
            left_ref[place] = left
            right_ref[place] = right
            return after

        return jnp.maximum(most, lax.fori_loop(0, per, slot, jnp.int32(0), unroll=True))

    most = lax.fori_loop(0, assign_ref.shape[0] // per, owner, jnp.int32(0))
    tier_ref[0] = sum(jnp.where(most > cap, 1, 0) for cap in CAPS)

    def own(s, before):
        block = assign_ref[me * per + s]
        p, after = place_in(block, s, before)
        slot_ref[p] = s
        rank_ref[s] = p
        row_ref[s] = jnp.where(block < ADA, block // (6 * NB), 0)
        col_ref[s] = jnp.where(block < ADA, block % (6 * NB), -1)
        return after

    count_ref[0] = lax.fori_loop(0, per, own, jnp.int32(0), unroll=True)


def find_places(assign, per):
    smem = pl.BlockSpec(memory_space=pltpu.SMEM)

    def ints(count):
        return jax.ShapeDtypeStruct((count,), jnp.int32)

    total = assign.shape[0]
    return pl.pallas_call(
        functools.partial(places_body, per),
        out_shape=[ints(per)] * 4 + [ints(total)] * 3 + [ints(1)] * 2,
        in_specs=[smem],
        out_specs=[smem] * 9,
        name="find_places",
    )(assign)


def spread_plain(slot_of, row_of, col_of, tile_master, row_master, timesteps, labels):
    shard_count = lax.axis_size("shard")
    everyone = ("grp", "shard")
    me = lax.axis_index("shard")
    per, columns = tile_master.shape[0], row_master.shape[1]
    low_rows = row_master.astype(bf16)
    at = [0]

    def take(count):
        at[0] += count
        return low_rows[at[0] - count : at[0]]

    table, w_time1, w_time2 = take(NCLASS), take(FREQ), take(D)
    w_final = (take(D), take(D))
    take(2 * PATCH_DIM)
    take(1)
    b_time1, b_time2 = take(1), take(1)
    take(4)
    b_ada = take(6)
    take(FF // D)
    b_final = take(2)
    b_mod = jnp.concatenate([b_ada, b_final], axis=0)

    packed = pack_tiles(slot_of, tile_master)
    gathered = lax.all_gather(packed, "shard", axis=0, tiled=True)
    near = lax.all_gather(low_rows[NEAR_START:], "shard", axis=1, tiled=True)
    near = jnp.pad(near, ((0, NEAR - NEAR_REAL), (0, 0))).reshape(NEAR, LANES, 128).transpose(1, 0, 2)

    ids = lax.all_gather(jnp.concatenate([timesteps, labels]), everyone, axis=0)
    all_steps, all_labels = ids[:, 0], ids[:, 1]
    freq_low = time_freq(all_steps, FREQ).astype(bf16)
    own_pre = nn(freq_low, w_time1) + b_time1
    time_low = lax.all_gather(jax.nn.silu(own_pre).astype(bf16), "shard", axis=1, tiled=True)
    one_hot = (all_labels[:, None] == jnp.arange(NCLASS, dtype=jnp.int32)[None, :]).astype(bf16)
    own_cond = nn(time_low, w_time2) + b_time2 + nn(one_hot, table)
    cond_low = lax.all_gather(jax.nn.silu(own_cond).astype(bf16), "shard", axis=1, tiled=True)
    group_cond = lax.dynamic_slice(cond_low, (lax.axis_index("grp") * shard_count, 0), (shard_count, D))
    part_mod = ada_front(row_of, col_of, blocked(group_cond), tile_master)
    part_mod = part_mod.transpose(1, 0, 2).reshape(shard_count, 6, D)
    part_final = jnp.stack([nn(group_cond, w_final[0]), nn(group_cond, w_final[1])], axis=1)
    spread = jnp.zeros((shard_count, 8, D), f32)
    spread = lax.dynamic_update_slice(
        spread,
        jnp.concatenate([jnp.zeros((shard_count, 6, columns), f32), part_final], axis=1) + b_mod[None].astype(f32),
        (0, 0, me * columns),
    )
    spread = spread + jnp.concatenate([part_mod, jnp.zeros((shard_count, 2, D), f32)], axis=1)
    mods = lax.psum_scatter(spread, "shard", scatter_dimension=0, tiled=True)[0]
    label = jnp.broadcast_to(all_labels.astype(f32)[:, None], (all_labels.shape[0], 128))

    def lanes(array):
        return array.reshape(-1, LANES, 128).transpose(1, 0, 2)

    return (
        gathered, near, mods.reshape(8 * LANES, 128), freq_low, label, lanes(time_low), lanes(cond_low), own_pre, own_cond,
    )


def collect_plain(left_of, right_of, row_of, col_of, count, acts, dmod, ends, stats, times, conds, freq_low, label, own_pre, own_cond,
                  row_master, tile_master):
    everyone = ("grp", "shard")
    me = lax.axis_index("shard")
    columns = row_master.shape[1]
    low_rows = row_master.astype(bf16)
    w_time2 = low_rows[NCLASS + FREQ : NCLASS + FREQ + D]
    w_final = [low_rows[NCLASS + FREQ + (1 + i) * D : NCLASS + FREQ + (2 + i) * D] for i in range(2)]
    one_hot = (label[:, :1].astype(jnp.int32) == jnp.arange(NCLASS, dtype=jnp.int32)[None, :]).astype(bf16)
    time_low, cond_low = (array.transpose(1, 0, 2).reshape(-1, D) for array in (times, conds))
    partial = tile_grads(left_of, right_of, acts)
    own_tiles = lax.psum_scatter(partial, "shard", scatter_dimension=0, tiled=True)
    own_tiles = lax.psum(own_tiles, "grp")

    all_dmod = lax.all_gather(dmod.reshape(1, -1).astype(bf16), everyone, axis=0, tiled=True)
    dmod_blocks = blocked(all_dmod[:, : 6 * D])
    own_dmod = lax.dynamic_slice(all_dmod.reshape(-1, 8, D), (0, 0, me * columns), (all_dmod.shape[0], 8, columns))
    part_cond = ada_back(row_of, col_of, dmod_blocks, tile_master).transpose(1, 0, 2).reshape(-1, D)
    part_cond = part_cond + nt(own_dmod[:, 6], w_final[0]) + nt(own_dmod[:, 7], w_final[1])
    own_dcond = lax.psum_scatter(part_cond, "shard", scatter_dimension=1, tiled=True) * silu_slope(own_cond)
    dcond_low = own_dcond.astype(bf16)
    own_dpre = lax.psum_scatter(nt(dcond_low, w_time2), "shard", scatter_dimension=1, tiled=True)
    own_dpre = own_dpre * silu_slope(own_pre)
    wide_dmod = own_dmod.astype(f32)

    token_rows = ends.transpose(1, 0, 2).reshape(TOKEN_ROWS, D)
    token_rows = lax.psum_scatter(token_rows, "shard", scatter_dimension=1, tiled=True)
    token_rows = lax.psum(token_rows, "grp")
    own_rows = jnp.concatenate(
        [
            tn(one_hot.astype(f32), own_dcond),
            tn(freq_low, own_dpre.astype(bf16)),
            tn(time_low, dcond_low),
            tn(cond_low, own_dmod[:, 6]),
            tn(cond_low, own_dmod[:, 7]),
            token_rows[: T_PATCH + 1],
            jnp.sum(own_dpre, axis=0)[None],
            jnp.sum(own_dcond, axis=0)[None],
            token_rows[T_QUERY : T_VALUE + 1],
            token_rows[T_OUT : T_DOWN + 1],
            jnp.sum(wide_dmod[:, :6], axis=0),
            token_rows[T_UP:T_END],
            jnp.sum(wide_dmod[:, 6:], axis=0),
        ],
        axis=0,
    )
    totals = lax.psum(stats, everyone)
    cond_gram = nt(cond_low, cond_low)
    dmod_gram = nt(all_dmod[:, : 6 * D], all_dmod[:, : 6 * D])
    counted = jnp.arange(own_tiles.shape[0], dtype=jnp.int32) < count
    wide_tiles = jnp.where(counted[:, None, None], own_tiles.astype(f32), 0.0)
    square_part = jnp.sum(wide_tiles * wide_tiles) + jnp.sum(own_rows * own_rows)
    square_sum = lax.psum(square_part, "shard") + jnp.sum(cond_gram * dmod_gram)
    return own_tiles, dmod_blocks, own_rows, jnp.broadcast_to(square_sum, (8, 128)), totals


def pack_body(slot_ref, tile_ref, out_ref):
    out_ref[...] = tile_ref[...].astype(bf16)


def pack_tiles(slot_of, tile_master):
    per = tile_master.shape[0]
    return pl.pallas_call(
        pack_body,
        grid_spec=pltpu.PrefetchScalarGridSpec(
            num_scalar_prefetch=1,
            grid=(per,),
            in_specs=[pl.BlockSpec((1, BLK, BLK), lambda p, slots: (slots[p], 0, 0))],
            out_specs=pl.BlockSpec((1, BLK, BLK), lambda p, slots: (p, 0, 0)),
        ),
        out_shape=jax.ShapeDtypeStruct(tile_master.shape, bf16),
        name="pack_tiles",
    )(slot_of, tile_master)


def shards(
    patches, noise, timesteps, labels, assign, tile_master, tile_bases, tile_moment, tile_second,
    row_master, row_moment, row_second,
):
    group_count, shard_count = lax.axis_size("grp"), lax.axis_size("shard")
    everyone = ("grp", "shard")
    me = lax.axis_index("shard")
    per = tile_master.shape[0]
    columns = row_master.shape[1]
    token_total = patches.shape[0] * group_count * shard_count
    tile_total = assign.shape[0]

    slot_of, row_of, col_of, rank, inverse, left_of, right_of, count, tier = find_places(assign, per)
    fast = group_count == GROUPS and shard_count == SHARDS
    if fast:
        tier = tier[0]
        gathered, near, mods, freq_low, label, times, conds, own_pre, own_cond = lax.switch(
            tier, [functools.partial(spread, cap) for cap in CAPS + (per,)], slot_of, row_of, col_of, timesteps, labels, tile_master, row_master,
        )
        gathered = gathered.reshape(tile_total, BLK, BLK)
    else:
        gathered, near, mods, freq_low, label, times, conds, own_pre, own_cond = spread_plain(
            slot_of, row_of, col_of, tile_master, row_master, timesteps, labels
        )

    loss_scale = 1.0 / (token_total * PATCH_DIM)
    acts, dmod, ends, stats = block_step(
        inverse, gathered, patches.T, noise.T, position_table(LAT // PATCH_SIDE, D), near, mods.reshape(8 * LANES, 128),
        2.0 * loss_scale,
    )

    if fast:
        own_tiles, dmod_blocks, own_rows, squares, totals = lax.switch(
            tier, [functools.partial(collect, cap) for cap in CAPS + (per,)], left_of, right_of, row_of, col_of, count, acts, dmod, ends, stats, times, conds, freq_low, label, own_pre,
            own_cond, row_master, tile_master,
        )
    else:
        own_tiles, dmod_blocks, own_rows, squares, totals = collect_plain(
            left_of, right_of, row_of, col_of, count, acts, dmod, ends, stats, times, conds, freq_low, label, own_pre,
            own_cond, row_master, tile_master,
        )
    new_tile_moment, new_tile_second, tile_update, new_row_moment, new_row_second, row_update, loss, grad_norm, act_rms = adam(
        (1.0 / (token_total * PATCH_DIM), 1.0 / (token_total * D)), rank, row_of, col_of, squares, totals, own_tiles, conds,
        dmod_blocks, tile_bases, tile_moment, tile_second, own_rows, row_master, row_moment, row_second,
    )
    loss, grad_norm = loss.reshape(()), grad_norm.reshape(())
    return (
        loss, grad_norm, act_rms, new_tile_moment, new_tile_second, tile_update, new_row_moment, new_row_second, row_update,
    )


def solution(mesh):
    placed = (
        P(("grp", "shard"), None),
        P(("grp", "shard"), None),
        P(("grp", "shard")),
        P(("grp", "shard")),
        P(),
        P("shard", None, None),
        P("shard", None, None, None),
        P("shard", None, None),
        P("shard", None, None),
        P(None, "shard"),
        P(None, "shard"),
        P(None, "shard"),
    )
    return jax.shard_map(
        shards,
        mesh=mesh,
        in_specs=placed,
        out_specs=(
            P(), P(), P(),
            P("shard", None, None), P("shard", None, None), P("shard", None, None),
            P(None, "shard"), P(None, "shard"), P(None, "shard"),
        ),
        check_vma=False,
    )
```

```python
import functools
import math

import jax
import jax.numpy as jnp
from jax import lax
from jax.experimental import pallas as pl
from jax.experimental.pallas import tpu as pltpu
from jax.sharding import PartitionSpec as P

D = 1024
HEADS = 16
HD = 64
FF = 4096
NCLASS = 1000
FREQ = 256
PATCH_SIDE = 2
LAT = 32
BLK = 256
PATCH_DIM = 16
SEQ = 256

NB = D // BLK
HB = FF // BLK
QB = 3 * NB
ADA = NB * 6 * NB
BIG = NB * QB + NB * NB + 2 * NB * HB
AT_QKV, AT_OUT, AT_UP, AT_DOWN = 0, NB * QB, NB * QB + NB * NB, NB * QB + NB * NB + NB * HB
L_ATT, L_OUT, L_MLP, L_HID = 0, NB, 2 * NB, 3 * NB
R_QKV = 3 * NB + HB
R_OUT = R_QKV + QB
R_UP = R_OUT + NB
R_DOWN = R_UP + HB
ACTS = R_DOWN + NB
B_OUT, B_UP, B_DOWN = QB, QB + NB, QB + NB + HB
ROW_STEP = 128
ADAM_GROUP = 3
LANES = D // 128
NEAR = 64
NEAR_START = NCLASS + FREQ + 3 * D
N_PATCH, N_TIME1, N_TIME2, N_QUERY, N_VALUE, N_OUT, N_DOWN, N_ADA = range(2 * PATCH_DIM, 2 * PATCH_DIM + 8)
N_UP = N_ADA + 6
N_FINAL = N_UP + FF // D
NEAR_REAL = N_FINAL + 2
T_PATCH, T_OUT, T_DOWN, T_QUERY, T_VALUE, T_UP = range(2 * PATCH_DIM, 2 * PATCH_DIM + 6)
T_END = T_UP + FF // D
TOKEN_ROWS = 48

CAPS = (28, 30)
GROUPS, SHARDS = 4, 8
MESH_ID = pl.DeviceIdType.MESH

ln_eps = 1e-06
beta_one = 0.5
beta_two = 0.5
adam_eps = 1e-08
rate_step = 0.01
decay_rate = 0.1
clip_at = 0.25

f32 = jnp.float32
bf16 = jnp.bfloat16


def nn(left, right):
    return lax.dot_general(left, right, (((1,), (0,)), ((), ())), preferred_element_type=f32)


def nt(left, right):
    return lax.dot_general(left, right, (((1,), (1,)), ((), ())), preferred_element_type=f32)


def tn(left, right):
    return lax.dot_general(left, right, (((0,), (0,)), ((), ())), preferred_element_type=f32)


def wide(ref, at, count=ROW_STEP):
    return jnp.concatenate([ref[r, pl.ds(at, count), :] for r in range(NB)], axis=1)


def put(ref, base, at, value, count=ROW_STEP):
    for r in range(NB):
        ref[base + r, pl.ds(at, count), :] = value[:, r * BLK : (r + 1) * BLK].astype(ref.dtype)


def fold(value):
    return jnp.sum(value.reshape(-1, 8, value.shape[-1]), axis=0)


def normed(value):
    centred = value - jnp.mean(value, axis=-1, keepdims=True)
    spread = jnp.mean(centred * centred, axis=-1, keepdims=True)
    back = lax.rsqrt(spread + ln_eps)
    return centred * back, back


def over_rows(body):
    def step(i, unused):
        body(pl.multiple_of(i * ROW_STEP, ROW_STEP))
        return unused

    lax.fori_loop(0, SEQ // ROW_STEP, step, 0)


def over(count, body, together=2):
    def step(i, unused):
        body(i)
        return unused

    lax.fori_loop(0, count, step, 0, unroll=together)


def norm_back(grad, value, scale):
    norm, back = normed(value)
    inner = grad * (1.0 + scale)
    mean_one = jnp.mean(inner, axis=-1, keepdims=True)
    mean_two = jnp.mean(inner * norm, axis=-1, keepdims=True)
    return norm, (inner - mean_one - norm * mean_two) * back


def gelu_pair(value):
    root = math.sqrt(2.0 / math.pi)
    square = value * value
    bend = jnp.tanh(root * (value + 0.044715 * value * square))
    half = 0.5 * (1.0 + bend)
    slope = half + 0.5 * value * (1.0 - bend * bend) * root * (1.0 + 3 * 0.044715 * square)
    return value * half, slope


def block_body(
    loss_factor, place_ref, tiles_ref, patches_ref, noise_ref, spot_ref, near_ref, mods_ref,
    acts_ref, dmod_ref, ends_ref, stats_ref,
    w_ref, stream, middle, last, out_att, out_mlp, low_in, low_att, qkv, hid, slope, probs, flow, sums,
    near_wide, bias_ref, mod_ref, dbias_ref, w_sem,
):
    att_scale = HD ** (-0.5)
    cuts = (AT_QKV, AT_OUT, AT_UP, AT_DOWN, BIG)

    def fetch(b, sem):
        pltpu.make_async_copy(tiles_ref.at[place_ref[ADA + b]], w_ref.at[b], w_sem.at[sem]).start()

    for m in range(4):
        over(cuts[m + 1] - cuts[m], lambda b, m=m: fetch(cuts[m] + b, m))

    def arrived(m):
        span = pl.ds(cuts[m], cuts[m + 1] - cuts[m])
        pltpu.make_async_copy(tiles_ref.at[pl.ds(0, cuts[m + 1] - cuts[m])], w_ref.at[span], w_sem.at[m]).wait()

    def mod(i):
        return mod_ref[i : i + 1, :]

    near_wide[...] = near_ref[...].astype(f32)

    def row_block(row, r):
        return jnp.concatenate([near_wide[2 * r, row : row + 1, :], near_wide[2 * r + 1, row : row + 1, :]], axis=1)

    def near_block(row, r):
        span = slice(row, row + PATCH_DIM)
        return jnp.concatenate([near_ref[2 * r, span, :], near_ref[2 * r + 1, span, :]], axis=1)

    for r in range(NB):
        bias_ref[r] = row_block(N_QUERY, r)
        bias_ref[NB + r] = jnp.zeros((1, BLK), f32)
        bias_ref[2 * NB + r] = row_block(N_VALUE, r)
        bias_ref[B_OUT + r] = row_block(N_OUT, r)
        bias_ref[B_DOWN + r] = row_block(N_DOWN, r)
        for i in range(FF // D):
            bias_ref[B_UP + i * NB + r] = row_block(N_UP + i, r)
    for i in range(8):
        mod_ref[i : i + 1, :] = jnp.concatenate([mods_ref[i * LANES + o : i * LANES + o + 1, :] for o in range(LANES)], axis=1)

    lane = lax.broadcasted_iota(jnp.int32, (SEQ, 128), 1)
    lower = lane < HD
    halves = (lower, jnp.logical_not(lower))

    def masked(value, side):
        return jnp.where(halves[side], value, jnp.zeros_like(value))

    sums[...] = jnp.zeros_like(sums)
    S_SQ_END, S_SQ_ATT, S_SQ_MLP = 0, 1, 2
    S_DSH_A, S_DSC_A, S_DG_A, S_DSH_M, S_DSC_M, S_DG_M, S_DSH_F, S_DSC_F = range(3, 11)
    S_PATCH, S_OUT, S_DOWN = 11, 12, 13

    def collect(which, value):
        sums[which] = sums[which] + fold(value)

    patches = patches_ref[...]
    side = LAT // PATCH_SIDE
    for r in range(NB):
        stream[r] = tn(patches, near_block(0, r)) + row_block(N_PATCH, r)
    for i in range(side):
        span = slice(i * side, (i + 1) * side)
        for r in range(2):
            stream[r, span, :] = stream[r, span, :] + spot_ref[r, i : i + 1, :]
            stream[2 + r, span, :] = stream[2 + r, span, :] + spot_ref[r]

    def modulate(source, scale, shift):
        def body(at):
            norm, _ = normed(wide(source, at))
            put(low_in, 0, at, norm * (1.0 + scale) + shift)

        over_rows(body)

    def transposed(base, ref, count):
        over(count, lambda r: acts_ref.__setitem__(base + r, ref[r].T))

    modulate(stream, mod(1), mod(0))
    transposed(L_ATT, low_in, NB)
    arrived(0)

    def qkv_step(c):
        total = nn(low_in[0], w_ref[AT_QKV + c])
        for r in range(1, NB):
            total += nn(low_in[r], w_ref[AT_QKV + r * QB + c])
        qkv[c] = (total + bias_ref[c]).astype(bf16)

    over(QB, qkv_step)

    def attend(c):
        for half in range(2):
            span = slice(half * 128, (half + 1) * 128)
            q, k, v = qkv[c, :, span], qkv[NB + c, :, span], qkv[2 * NB + c, :, span]
            parts = []
            for side in range(2):
                scores = nt(masked(q, side), k) * att_scale
                top = jnp.max(scores, axis=-1, keepdims=True)
                power = jnp.exp(scores - top)
                prob = power / jnp.sum(power, axis=-1, keepdims=True)
                probs[c * 4 + half * 2 + side] = prob
                parts.append(nn(prob.astype(bf16), v))
            low_att[c, :, span] = jnp.where(lower, parts[0], parts[1]).astype(bf16)

    over(NB, attend)
    transposed(L_OUT, low_att, NB)
    arrived(1)

    def out_step(c):
        total = nn(low_att[0], w_ref[AT_OUT + c])
        for r in range(1, NB):
            total += nn(low_att[r], w_ref[AT_OUT + r * NB + c])
        out_att[c] = total + bias_ref[B_OUT + c]

    over(NB, out_step)

    def mid_step(at):
        branch = mod(2) * wide(out_att, at)
        collect(S_SQ_ATT, branch * branch)
        value = wide(stream, at) + branch
        put(middle, 0, at, value)
        norm, _ = normed(value)
        put(low_in, 0, at, norm * (1.0 + mod(4)) + mod(3))

    over_rows(mid_step)
    transposed(L_MLP, low_in, NB)
    arrived(2)

    def up_step(c):
        total = nn(low_in[0], w_ref[AT_UP + c])
        for r in range(1, NB):
            total += nn(low_in[r], w_ref[AT_UP + r * HB + c])
        value, back = gelu_pair(total + bias_ref[B_UP + c])
        slope[c] = back
        low = value.astype(bf16)
        hid[c] = low
        acts_ref[L_HID + c] = low.T

    over(HB, up_step)
    arrived(3)

    def down_step(c):
        total = nn(hid[0], w_ref[AT_DOWN + c])
        for r in range(1, HB):
            total += nn(hid[r], w_ref[AT_DOWN + r * NB + c])
        out_mlp[c] = total + bias_ref[B_DOWN + c]

    over(NB, down_step)

    def end_step(at):
        branch = mod(5) * wide(out_mlp, at)
        collect(S_SQ_MLP, branch * branch)
        value = wide(middle, at) + branch
        collect(S_SQ_END, value * value)
        put(last, 0, at, value)
        norm, _ = normed(value)
        put(low_in, 0, at, norm * (1.0 + mod(7)) + mod(6))

    over_rows(end_step)
    predicted = nt(near_block(PATCH_DIM, 0), low_in[0])
    for r in range(1, NB):
        predicted += nt(near_block(PATCH_DIM, r), low_in[r])
    mismatch = predicted - noise_ref[...]
    loss_sum = jnp.sum(mismatch * mismatch)
    pred_low = (loss_factor * mismatch).astype(bf16)
    def put_rows(row, count, r, value):
        for i in range(2):
            ends_ref[2 * r + i, row : row + count, :] = value[:, i * 128 : (i + 1) * 128]

    for r in range(NB):
        put_rows(PATCH_DIM, PATCH_DIM, r, nn(pred_low, low_in[r]))
        flow[r] = tn(pred_low, near_block(PATCH_DIM, r))

    def end_back(at):
        grad = wide(flow, at)
        norm, value = norm_back(grad, wide(last, at), mod(7))
        collect(S_DSC_F, grad * norm)
        collect(S_DSH_F, grad)
        put(last, 0, at, value)
        collect(S_DG_M, value * wide(out_mlp, at))
        down = value * mod(5)
        collect(S_DOWN, down)
        put(acts_ref, R_DOWN, at, down)

    over_rows(end_back)

    def up_back(c):
        total = nt(acts_ref[R_DOWN], w_ref[AT_DOWN + c * NB])
        for j in range(1, NB):
            total += nt(acts_ref[R_DOWN + j], w_ref[AT_DOWN + c * NB + j])
        value = total * slope[c]
        dbias_ref[2 * NB + c] = jnp.sum(value, axis=0, keepdims=True)
        acts_ref[R_UP + c] = value.astype(bf16)

    over(HB, up_back)

    def mlp_back(r):
        total = nt(acts_ref[R_UP], w_ref[AT_UP + r * HB])
        for c in range(1, HB):
            total += nt(acts_ref[R_UP + c], w_ref[AT_UP + r * HB + c])
        flow[r] = total

    over(NB, mlp_back)

    def mid_back(at):
        grad = wide(flow, at)
        norm, value = norm_back(grad, wide(middle, at), mod(4))
        collect(S_DSC_M, grad * norm)
        collect(S_DSH_M, grad)
        value = value + wide(last, at)
        put(middle, 0, at, value)
        collect(S_DG_A, value * wide(out_att, at))
        proj = value * mod(2)
        collect(S_OUT, proj)
        put(acts_ref, R_OUT, at, proj)

    over_rows(mid_back)

    def att_back(r):
        total = nt(acts_ref[R_OUT], w_ref[AT_OUT + r * NB])
        for c in range(1, NB):
            total += nt(acts_ref[R_OUT + c], w_ref[AT_OUT + r * NB + c])
        low_att[r] = total.astype(bf16)

    over(NB, att_back)

    def attend_back(c):
        for half in range(2):
            span = slice(half * 128, (half + 1) * 128)
            q, k, v = qkv[c, :, span], qkv[NB + c, :, span], qkv[2 * NB + c, :, span]
            grad = low_att[c, :, span]
            found = []
            for side in range(2):
                prob = probs[c * 4 + half * 2 + side]
                dprob = nt(masked(grad, side), v)
                dvalue = tn(prob.astype(bf16), grad)
                dscore = prob * (dprob - jnp.sum(dprob * prob, axis=-1, keepdims=True))
                low = dscore.astype(bf16)
                found.append((nn(low, k) * att_scale, tn(low, q) * att_scale, dvalue))
            merged = [jnp.where(lower, one, two) for one, two in zip(*found)]
            for i in range(3):
                acts_ref[R_QKV + i * NB + c, :, span] = merged[i].astype(bf16)
            dbias_ref[c, :, span] = jnp.sum(merged[0], axis=0, keepdims=True)
            dbias_ref[NB + c, :, span] = jnp.sum(merged[2], axis=0, keepdims=True)

    over(NB, attend_back)

    def in_back(r):
        total = nt(acts_ref[R_QKV], w_ref[AT_QKV + r * QB])
        for c in range(1, QB):
            total += nt(acts_ref[R_QKV + c], w_ref[AT_QKV + r * QB + c])
        flow[r] = total

    over(NB, in_back)

    def first_back(at):
        grad = wide(flow, at)
        norm, value = norm_back(grad, wide(stream, at), mod(1))
        collect(S_DSC_A, grad * norm)
        collect(S_DSH_A, grad)
        value = value + wide(middle, at)
        collect(S_PATCH, value)
        put(low_in, 0, at, value)

    over_rows(first_back)
    for r in range(NB):
        put_rows(0, PATCH_DIM, r, nn(patches, low_in[r]))

    def total_of(which):
        return jnp.sum(sums[which], axis=0, keepdims=True)

    for i in range(8):
        value = total_of(S_DSH_A + i)
        for o in range(LANES):
            dmod_ref[i * LANES + o : i * LANES + o + 1, :] = value[:, o * 128 : (o + 1) * 128]
    for row, which in ((T_PATCH, S_PATCH), (T_OUT, S_OUT), (T_DOWN, S_DOWN)):
        value = total_of(which)
        for r in range(NB):
            put_rows(row, 1, r, value[:, r * BLK : (r + 1) * BLK])
    for r in range(NB):
        put_rows(T_QUERY, 1, r, dbias_ref[r])
        put_rows(T_VALUE, 1, r, dbias_ref[NB + r])
        for i in range(FF // D):
            put_rows(T_UP + i, 1, r, dbias_ref[2 * NB + i * NB + r])
    ends_ref[:, T_END:, :] = jnp.zeros((LANES, TOKEN_ROWS - T_END, 128), f32)
    row = lax.broadcasted_iota(jnp.int32, (8, 128), 0)
    found = jnp.where(row == 0, loss_sum, 0.0)
    for i in range(3):
        found = jnp.where(row == i + 1, jnp.sum(sums[i]), found)
    stats_ref[...] = found


def block_step(place, tiles, patches, noise, spots, near, mods, loss_factor):
    vmem = pl.BlockSpec(memory_space=pltpu.VMEM)
    macs = 3 * SEQ * BIG * BLK * BLK
    return pl.pallas_call(
        functools.partial(block_body, loss_factor),
        out_shape=[
            jax.ShapeDtypeStruct((ACTS, BLK, BLK), bf16),
            jax.ShapeDtypeStruct((8 * LANES, 128), f32),
            jax.ShapeDtypeStruct((LANES, TOKEN_ROWS, 128), f32),
            jax.ShapeDtypeStruct((8, 128), f32),
        ],
        in_specs=[pl.BlockSpec(memory_space=pltpu.SMEM), pl.BlockSpec(memory_space=pl.ANY)] + [vmem] * 5,
        out_specs=[vmem] * 4,
        scratch_shapes=[
            pltpu.VMEM((BIG, BLK, BLK), bf16),
            pltpu.VMEM((NB, SEQ, BLK), f32),
            pltpu.VMEM((NB, SEQ, BLK), f32),
            pltpu.VMEM((NB, SEQ, BLK), f32),
            pltpu.VMEM((NB, SEQ, BLK), f32),
            pltpu.VMEM((NB, SEQ, BLK), f32),
            pltpu.VMEM((NB, SEQ, BLK), bf16),
            pltpu.VMEM((NB, SEQ, BLK), bf16),
            pltpu.VMEM((QB, SEQ, BLK), bf16),
            pltpu.VMEM((HB, SEQ, BLK), bf16),
            pltpu.VMEM((HB, SEQ, BLK), f32),
            pltpu.VMEM((HEADS, SEQ, SEQ), f32),
            pltpu.VMEM((NB, SEQ, BLK), f32),
            pltpu.VMEM((14, 8, D), f32),
            pltpu.VMEM((LANES, NEAR, 128), f32),
            pltpu.VMEM((B_DOWN + NB, 1, BLK), f32),
            pltpu.VMEM((8, D), f32),
            pltpu.VMEM((2 * NB + HB, 1, BLK), f32),
            pltpu.SemaphoreType.DMA((4,)),
        ],
        compiler_params=pltpu.CompilerParams(vmem_limit_bytes=54 << 20),
        cost_estimate=pl.CostEstimate(flops=2 * macs, bytes_accessed=BIG * BLK * BLK * 4, transcendentals=0),
        name="block_step",
    )(place, tiles, patches, noise, spots, near, mods)


def ada_front_body(row_ref, col_ref, cond_ref, tile_ref, out_ref):
    s = pl.program_id(0)

    @pl.when(s == 0)
    def _():
        out_ref[...] = jnp.zeros_like(out_ref)

    @pl.when(col_ref[s] >= 0)
    def _():
        c = col_ref[s]
        out_ref[c] = out_ref[c] + nn(cond_ref[row_ref[s]], tile_ref[0].astype(bf16))


def ada_front(row_of, col_of, cond_blocks, tile_master):
    per, images = tile_master.shape[0], cond_blocks.shape[1]
    return pl.pallas_call(
        ada_front_body,
        grid_spec=pltpu.PrefetchScalarGridSpec(
            num_scalar_prefetch=2,
            grid=(per,),
            in_specs=[
                pl.BlockSpec(cond_blocks.shape, lambda s, r, c: (0, 0, 0)),
                pl.BlockSpec((1, BLK, BLK), lambda s, r, c: (s, 0, 0)),
            ],
            out_specs=pl.BlockSpec((6 * NB, images, BLK), lambda s, r, c: (0, 0, 0)),
        ),
        out_shape=jax.ShapeDtypeStruct((6 * NB, images, BLK), f32),
        name="ada_front",
    )(row_of, col_of, cond_blocks, tile_master)


def ada_back_body(row_ref, col_ref, dmod_ref, tile_ref, out_ref):
    s = pl.program_id(0)

    @pl.when(s == 0)
    def _():
        out_ref[...] = jnp.zeros_like(out_ref)

    @pl.when(col_ref[s] >= 0)
    def _():
        r = row_ref[s]
        out_ref[r] = out_ref[r] + nt(dmod_ref[col_ref[s]], tile_ref[0].astype(bf16))


def ada_back(row_of, col_of, dmod_blocks, tile_master):
    per, images = tile_master.shape[0], dmod_blocks.shape[1]
    return pl.pallas_call(
        ada_back_body,
        grid_spec=pltpu.PrefetchScalarGridSpec(
            num_scalar_prefetch=2,
            grid=(per,),
            in_specs=[
                pl.BlockSpec(dmod_blocks.shape, lambda s, r, c: (0, 0, 0)),
                pl.BlockSpec((1, BLK, BLK), lambda s, r, c: (s, 0, 0)),
            ],
            out_specs=pl.BlockSpec((NB, images, BLK), lambda s, r, c: (0, 0, 0)),
        ),
        out_shape=jax.ShapeDtypeStruct((NB, images, BLK), f32),
        name="ada_back",
    )(row_of, col_of, dmod_blocks, tile_master)


def tile_grad_body(left_ref, right_ref, acts_ref, out_ref):
    s = pl.program_id(0)
    out_ref[0] = nn(acts_ref[left_ref[s]], acts_ref[right_ref[s]]).astype(bf16)


def tile_grads(left_of, right_of, acts):
    count = left_of.shape[0]
    return pl.pallas_call(
        tile_grad_body,
        grid_spec=pltpu.PrefetchScalarGridSpec(
            num_scalar_prefetch=2,
            grid=(count,),
            in_specs=[pl.BlockSpec(acts.shape, lambda s, a, b: (0, 0, 0))],
            out_specs=pl.BlockSpec((1, BLK, BLK), lambda s, a, b: (s, 0, 0)),
        ),
        out_shape=jax.ShapeDtypeStruct((count, BLK, BLK), bf16),
        compiler_params=pltpu.CompilerParams(vmem_limit_bytes=40 << 20),
        name="tile_grads",
    )(left_of, right_of, acts)


def adam_body(
    group, factors, where_ref, row_ref, col_ref,
    norm_ref, totals_ref, grads_ref, cond_ref, dmod_ref, bases_ref, moment_ref, second_ref, row_grad_ref, row_master_ref, row_moment_ref, row_second_ref,
    new_moment_ref, new_second_ref, update_ref, new_row_moment_ref, new_row_second_ref, row_update_ref,
    loss_ref, grad_norm_ref, act_rms_ref,
):
    step = pl.program_id(0)

    @pl.when(step == 0)
    def _():
        loss_ref[0] = totals_ref[0, 0] * factors[0]
        grad_norm_ref[0] = jnp.sqrt(norm_ref[...])[0, 0]
        roots = jnp.sqrt(totals_ref[...] * factors[1])
        for i in range(3):
            act_rms_ref[i] = roots[i + 1, 0]

    factor = clip_at / jnp.maximum(jnp.sqrt(norm_ref[0:1, 0:1]), clip_at)

    def moved(moment, second, grad):
        new_moment = beta_one * moment + (1.0 - beta_one) * grad
        new_second = beta_two * second + (1.0 - beta_two) * grad * grad
        return new_moment, new_second, new_moment / (jnp.sqrt(new_second) + adam_eps)

    for j in range(group):
        s = step * group + j
        r, c = row_ref[s], col_ref[s]
        cond = jnp.concatenate([cond_ref[2 * r], cond_ref[2 * r + 1]], axis=1)
        thin = tn(cond, dmod_ref[jnp.maximum(c, 0)]).astype(bf16)
        grad = jnp.where(c >= 0, thin, grads_ref[where_ref[s]])
        left, right = bases_ref[j, 0].astype(bf16), bases_ref[j, 1].astype(bf16)
        turned = factor * tn(left, nn(grad, right).astype(bf16))
        moment, second, direction = moved(moment_ref[j], second_ref[j], turned)
        new_moment_ref[j] = moment
        new_second_ref[j] = second
        update_ref[j] = -rate_step * nt(nn(left, direction.astype(bf16)).astype(bf16), right)

    moment, second, direction = moved(row_moment_ref[...], row_second_ref[...], factor * row_grad_ref[...])
    new_row_moment_ref[...] = moment
    new_row_second_ref[...] = second
    row_update_ref[...] = -rate_step * (direction + decay_rate * row_master_ref[...])


def adam(factors, where, row_of, col_of, norm, totals, grads, conds, dmod_blocks, bases, moment, second, row_grad, row_master, row_moment, row_second):
    per = moment.shape[0]
    group = next(g for g in (ADAM_GROUP, 3, 2, 1) if per % g == 0)
    steps = per // group
    tile = pl.BlockSpec((group, BLK, BLK), lambda s, *_: (s, 0, 0))
    row_count, columns = row_master.shape
    row = pl.BlockSpec((-(-row_count // (8 * steps)) * 8, columns), lambda s, *_: (s, 0))

    def whole(array):
        return pl.BlockSpec(array.shape, lambda s, *_: (0,) * array.ndim)

    shape = jax.ShapeDtypeStruct(moment.shape, f32)
    row_shape = jax.ShapeDtypeStruct(row_master.shape, f32)
    return pl.pallas_call(
        functools.partial(adam_body, group, factors),
        grid_spec=pltpu.PrefetchScalarGridSpec(
            num_scalar_prefetch=3,
            grid=(steps,),
            in_specs=[
                whole(norm),
                whole(totals),
                whole(grads),
                whole(conds),
                whole(dmod_blocks),
                pl.BlockSpec((group, 2, BLK, BLK), lambda s, *_: (s, 0, 0, 0)),
                tile,
                tile,
                row,
                row,
                row,
                row,
            ],
            out_specs=[tile] * 3 + [row] * 3 + [pl.BlockSpec(memory_space=pltpu.SMEM)] * 3,
        ),
        out_shape=[shape] * 3 + [row_shape] * 3 + [jax.ShapeDtypeStruct((n,), f32) for n in (1, 1, 3)],
        compiler_params=pltpu.CompilerParams(vmem_limit_bytes=61 << 20),
        name="adam",
    )(where, row_of, col_of, norm, totals, grads, conds, dmod_blocks, bases, moment, second, row_grad, row_master, row_moment, row_second)


def spread_body(
    cap, n_third,
    slot_ref, row_ref, col_ref, step_ref, name_ref, tiles_ref, bases_ref, rows_ref,
    out_ref, bases_low_ref, near_ref, mods_ref, freq_ref, label_ref, time_ref, cond_ref, pre_ref, own_cond_ref,
    tile, pack, ids, near, times, conds, near_wide, cond_group, product, part, part_out, part_in, basis, basis_low,
    basis_sem, basis_low_sem, load_sem, keep_sem, send_sem, recv_sem, small_send, small_recv,
):
    z, s = lax.axis_index("grp"), lax.axis_index("shard")
    per = tile.shape[0]
    images = GROUPS * SHARDS
    third = cap // 3
    both = cap - 2 * third
    x_at, y_at, c_at, z_at = (z, s ^ 2), (z, s ^ 4), (z, s ^ 1), (z ^ 1, s)
    far_z = [(lax.rem(z + i, GROUPS), s) for i in range(1, GROUPS)]
    near_s = [(z, s ^ i) for i in range(1, SHARDS)]

    barrier = pltpu.get_barrier_semaphore()
    for peer in far_z + near_s:
        pl.semaphore_signal(barrier, inc=1, device_id=peer, device_id_type=MESH_ID)
    load = pltpu.make_async_copy(tiles_ref, tile, load_sem)
    load.start()

    def block_rows(index, count):
        return pl.ds(pl.multiple_of(index * count, count), count)

    lane = lax.broadcasted_iota(jnp.int32, (8, 128), 1).astype(f32)
    angle = step_ref[0].astype(f32) * jnp.exp(-math.log(10000.0) * lane / (FREQ // 2))
    line = lax.broadcasted_iota(jnp.int32, (8, 128), 0)
    known = jnp.where(line == 0, jnp.cos(angle), jnp.where(line == 1, jnp.sin(angle), name_ref[0].astype(f32)))
    ids[block_rows(s * GROUPS + z, 8), :] = known
    near_wide[...] = jnp.zeros_like(near_wide)
    near_wide[: NEAR_REAL - 3, :] = rows_ref[NEAR_START : NEAR_START + NEAR_REAL - 3, :]
    near_wide[NEAR_REAL - 3 : NEAR_REAL, :] = rows_ref[NEAR_START + NEAR_REAL - 3 : NEAR_START + NEAR_REAL, :]
    near[s] = near_wide[...].astype(bf16)
    near_wide[...] = near_wide[...].astype(bf16).astype(f32)
    pl.semaphore_wait(barrier, len(far_z) + len(near_s))

    sent = []

    def push(src, dst, peer, index):
        copy = pltpu.make_async_remote_copy(
            src_ref=src, dst_ref=dst, send_sem=small_send.at[index], recv_sem=small_recv.at[index],
            device_id=peer, device_id_type=MESH_ID,
        )
        copy.start()
        sent.append(copy)
        return copy

    def to_group(stage, pairs):
        first = len(far_z) + stage * len(near_s)
        return [push(*pairs(peer[1]), peer, first + i) for i, peer in enumerate(near_s)]

    def got(copies):
        for copy in copies:
            copy.wait_recv()

    own_ids = ids.at[block_rows(s * GROUPS + z, 8)]
    id_far = [push(own_ids, own_ids, peer, i) for i, peer in enumerate(far_z)]
    near_copies = to_group(0, lambda p: (near.at[s], near.at[s]))

    parity = lax.rem(z, 2)
    starts = (both + parity * third, 0, both + third - parity * third)

    def chunk_of(index):
        kind, at = divmod(index, n_third)
        size = both if kind == 1 else third
        first, last = at * size // n_third, (at + 1) * size // n_third
        return starts[kind] + first, last - first

    def chunk(index):
        return pl.ds(*chunk_of(index))

    load.wait()
    big = []

    def send(kind, stream, index, peer, src, owner, arrives):
        copy = pltpu.make_async_remote_copy(
            src_ref=src, dst_ref=out_ref.at[owner, chunk(index)],
            send_sem=send_sem.at[kind, index], recv_sem=recv_sem.at[stream, arrives],
            device_id=peer, device_id_type=MESH_ID,
        )
        copy.start()
        big.append(copy)

    def wait_for(stream, index, owner):
        place = out_ref.at[owner, chunk(index)]
        pltpu.make_async_remote_copy(
            src_ref=place, dst_ref=place, send_sem=send_sem.at[0, index], recv_sem=recv_sem.at[stream, index],
            device_id=x_at, device_id_type=MESH_ID,
        ).wait_recv()

    def pack_chunk(index):
        start, count = chunk_of(index)

        def one(i, unused):
            p = start + i
            pack[p] = tile[slot_ref[p]].astype(bf16)
            return unused

        lax.fori_loop(0, count, one, 0)

    def send_mine(index):
        src = pack.at[chunk(index)]
        if index < 2 * n_third:
            send(0, 0, index, x_at, src, s, index)
            send(1, 1, index, y_at, src, s, index)
        send(2, 3, index, c_at, src, s, index)

    owners = (s ^ 2, s ^ 4, s ^ 6)

    def pass_on(which, index):
        owner = owners[which]
        wait_for(which, index, owner)
        here = out_ref.at[owner, chunk(index)]
        if index < 2 * n_third:
            if which == 0 and index % 2 == 0:
                send(6, 2, index, y_at, here, owner, index)
            if which == 1 and index % 2 == 1:
                send(7, 2, index, x_at, here, owner, index)
        if index < n_third:
            send(8 + which, which, index, z_at, here, owner, 2 * n_third + index)
        send(3 + which, 4 + which, index, c_at, here, owner, index)

    for j in range(n_third):
        pack_chunk(j)
        send_mine(j)
    got(id_far)
    span = block_rows(s, 8 * GROUPS)
    id_near = to_group(1, lambda p: (ids.at[span], ids.at[span]))
    for j in range(n_third, 3 * n_third):
        pack_chunk(j)
    keep = pltpu.make_async_copy(pack, out_ref.at[s, pl.ds(0, cap)], keep_sem)
    keep.start()
    stages = {}

    def silu_low(value):
        return (value * jax.nn.sigmoid(value)).astype(bf16)

    def row_slice(start, count):
        return rows_ref[start : start + count, :].astype(bf16)

    def time_stage():
        got(id_near)
        freq = jnp.concatenate([ids[pl.ds(i, images, stride=8), :] for i in range(2)], axis=1).astype(bf16)
        freq_ref[...] = freq
        label_ref[...] = ids[pl.ds(2, images, stride=8), :]
        pre = nn(freq, row_slice(NCLASS, FREQ)) + near_wide[N_TIME1 : N_TIME1 + 1, :]
        pre_ref[...] = pre
        times[s] = silu_low(pre)
        stages["time"] = to_group(2, lambda p: (times.at[s], times.at[s]))

    def cond_stage():
        got(stages["time"])
        total = jnp.zeros((images, 128), f32) + near_wide[N_TIME2 : N_TIME2 + 1, :]
        for o in range(SHARDS):
            total += nn(times[o], row_slice(NCLASS + FREQ + o * 128, 128))
        hot = label_ref[...].astype(jnp.int32)[:, :1] == lax.broadcasted_iota(jnp.int32, (images, D), 1)
        total += nn(hot.astype(bf16), row_slice(0, D))
        own_cond_ref[...] = total
        conds[s] = silu_low(total)
        stages["cond"] = to_group(3, lambda p: (conds.at[s], conds.at[s]))

    def group_stage():
        got(stages["cond"])
        at = lax.broadcasted_iota(jnp.int32, (SHARDS, images), 1)
        row = lax.broadcasted_iota(jnp.int32, (SHARDS, images), 0)
        pick = (at == row * GROUPS + z).astype(bf16)
        for o in range(SHARDS):
            half = o % 2
            cond_group[o // 2, :, half * 128 : (half + 1) * 128] = nn(pick, conds[o])

    def ada_stage(start, count):
        def one(j, unused):
            product[j] = nn(cond_group[row_ref[j]].astype(bf16), tile[j].astype(bf16))
            return unused

        lax.fori_loop(start, start + count, one, 0)

    def part_stage():
        part[...] = jnp.zeros_like(part)

        def column(c, unused):
            total = jnp.zeros((SHARDS, BLK), f32)
            for j in range(per):
                total += jnp.where(col_ref[j] == c, 1.0, 0.0) * product[j]
            for half in range(2):
                part[block_rows(2 * c + half, 8), :] = total[:, half * 128 : (half + 1) * 128]
            return unused

        lax.fori_loop(0, 6 * NB, column, 0)
        for i in range(6):
            place = block_rows(i * LANES + s, 8)
            part[place, :] = part[place, :] + near_wide[N_ADA + i : N_ADA + i + 1, :]
        for i in range(2):
            total = jnp.zeros((SHARDS, 128), f32) + near_wide[N_FINAL + i : N_FINAL + i + 1, :]
            for r in range(NB):
                weight = row_slice(NCLASS + FREQ + D + i * D + r * BLK, BLK)
                total += nn(cond_group[r].astype(bf16), weight)
            part[block_rows((6 + i) * LANES + s, 8), :] = total
        for o in range(SHARDS):
            part_out[o] = part[pl.ds(o, 8 * LANES, stride=8), :]
        part_in[s] = part_out[s]
        stages["part"] = to_group(4, lambda p: (part_out.at[p], part_in.at[s]))

    def mod_stage():
        got(stages["part"])
        total = part_in[0]
        for o in range(1, SHARDS):
            total += part_in[o]
        mods_ref[...] = total
        got(near_copies)
        near_ref[...] = near[...]
        time_ref[...] = times[...]
        cond_ref[...] = conds[...]

    pieces = per // basis.shape[1]

    def basis_load(k):
        span = pl.ds(k * basis.shape[1], basis.shape[1])
        return pltpu.make_async_copy(bases_ref.at[span], basis.at[k % 2], basis_sem.at[k % 2])

    def basis_store(k):
        span = pl.ds(k * basis.shape[1], basis.shape[1])
        return pltpu.make_async_copy(basis_low.at[k % 2], bases_low_ref.at[span], basis_low_sem.at[k % 2])

    taken = [0]

    def narrow():
        k = taken[0]
        if k == pieces:
            return
        taken[0] += 1
        basis_load(k).wait()
        if k >= 2:
            basis_store(k - 2).wait()
        def one(i, unused):
            for side in range(2):
                basis_low[k % 2, i, side] = basis[k % 2, i, side].astype(bf16)
            return unused

        lax.fori_loop(0, basis.shape[1], one, 0)
        basis_store(k).start()
        if k + 2 < pieces:
            basis_load(k + 2).start()

    basis_load(0).start()
    basis_load(1).start()

    cut = per // 3
    hooks = [
        (0.10, time_stage), (0.30, cond_stage), (0.50, group_stage), (0.55, lambda: ada_stage(0, cut)),
        (0.60, lambda: ada_stage(cut, cut)), (0.65, lambda: ada_stage(2 * cut, per - 2 * cut)), (0.70, part_stage), (2.0, mod_stage),
    ]
    seen = [0]
    steps = [0]

    def hook(last=False):
        steps[0] += 1
        narrow()
        while hooks and (last or steps[0] >= hooks[0][0] * 3 * n_third):
            hooks.pop(0)[1]()

    def z_next():
        order = [(w, 2 * n_third + j) for j in range(n_third) for w in (0, 1)]
        order += [(2, 2 * n_third + j) for j in range(n_third)]
        if seen[0] < len(order):
            pass_on(*order[seen[0]])
            seen[0] += 1

    for j in range(n_third):
        pass_on(0, j)
        pass_on(1, j)
        hook()
        if j:
            z_next()
    for j in range(n_third, 3 * n_third):
        send_mine(j)
    for j in range(n_third):
        pass_on(2, j)
        if j % 2:
            z_next()
            hook()
    for j in range(n_third, 2 * n_third):
        pass_on(0, j)
        pass_on(1, j)
        hook()
        z_next()
    for j in range(n_third, 2 * n_third):
        pass_on(2, j)
        if j % 2:
            z_next()
            hook()
    while seen[0] < 3 * n_third:
        z_next()
    hook(last=True)
    while taken[0] < pieces:
        narrow()
    for k in range(pieces - 2, pieces):
        basis_store(k).wait()
    for index in range(3 * n_third):
        wait_for(3, index, s ^ 1)
        for which in range(3):
            wait_for(4 + which, index, owners[which] ^ 1)
    keep.wait()
    for copy in big + sent:
        copy.wait_send()


def spread(cap, slot_of, row_of, col_of, timesteps, labels, tile_master, tile_bases, row_master):
    per = tile_master.shape[0]
    n_third = 5
    images = GROUPS * SHARDS
    vmem = pl.BlockSpec(memory_space=pltpu.VMEM)
    smem = pl.BlockSpec(memory_space=pltpu.SMEM)
    anywhere = pl.BlockSpec(memory_space=pl.ANY)
    small = (GROUPS - 1) + 5 * (SHARDS - 1)
    few = per // 12
    return pl.pallas_call(
        functools.partial(spread_body, cap, n_third),
        out_shape=[
            jax.ShapeDtypeStruct((SHARDS, per, BLK, BLK), bf16),
            jax.ShapeDtypeStruct(tile_bases.shape, bf16),
            jax.ShapeDtypeStruct((LANES, NEAR, 128), bf16),
            jax.ShapeDtypeStruct((8 * LANES, 128), f32),
            jax.ShapeDtypeStruct((images, FREQ), bf16),
            jax.ShapeDtypeStruct((images, 128), f32),
            jax.ShapeDtypeStruct((SHARDS, images, 128), bf16),
            jax.ShapeDtypeStruct((SHARDS, images, 128), bf16),
            jax.ShapeDtypeStruct((images, 128), f32),
            jax.ShapeDtypeStruct((images, 128), f32),
        ],
        in_specs=[smem] * 5 + [anywhere, anywhere, vmem],
        out_specs=[anywhere] * 2 + [vmem] * 8,
        scratch_shapes=[
            pltpu.VMEM((per, BLK, BLK), f32),
            pltpu.VMEM((cap, BLK, BLK), bf16),
            pltpu.VMEM((images * 8, 128), f32),
            pltpu.VMEM((LANES, NEAR, 128), bf16),
            pltpu.VMEM((SHARDS, images, 128), bf16),
            pltpu.VMEM((SHARDS, images, 128), bf16),
            pltpu.VMEM((NEAR, 128), f32),
            pltpu.VMEM((NB, SHARDS, BLK), f32),
            pltpu.VMEM((per, SHARDS, BLK), f32),
            pltpu.VMEM((8 * LANES * 8, 128), f32),
            pltpu.VMEM((SHARDS, 8 * LANES, 128), f32),
            pltpu.VMEM((SHARDS, 8 * LANES, 128), f32),
            pltpu.VMEM((2, few, 2, BLK, BLK), f32),
            pltpu.VMEM((2, few, 2, BLK, BLK), bf16),
            pltpu.SemaphoreType.DMA((2,)),
            pltpu.SemaphoreType.DMA((2,)),
            pltpu.SemaphoreType.DMA,
            pltpu.SemaphoreType.DMA,
            pltpu.SemaphoreType.DMA((11, 3 * n_third)),
            pltpu.SemaphoreType.DMA((7, 3 * n_third)),
            pltpu.SemaphoreType.DMA((small,)),
            pltpu.SemaphoreType.DMA((small,)),
        ],
        compiler_params=pltpu.CompilerParams(collective_id=cap, has_side_effects=True, vmem_limit_bytes=61 << 20),
        name="spread",
    )(slot_of, row_of, col_of, timesteps, labels, tile_master, tile_bases, row_master)

RING = 6
SUM_LAG = 2
Z_STEP = 1
Z_LAG = SUM_LAG + 4 * Z_STEP
ADA_PARTS = 6


def collect_body(
    cap, ch,
    left_ref, right_ref, row_ref, col_ref, count_ref,
    acts_ref, dmod_ref, ends_ref, stats_ref, time_ref, cond_ref, freq_ref, label_ref, pre_ref, own_cond_ref, rows_ref, tiles_ref,
    grads_ref, d_blocks_ref, own_rows_ref, norm_ref, stat_ref,
    out_c, in_c, out_d, out_x, out_y, in_dx, in_dy, in_x, in_y, total, low_in, high_in, final,
    tile, product, all_d, wide_d, all_stats, tok_out, tok_in, tok_z, tokens, part_out, part_in, pre_out, pre_in, own_dcond, own_dpre,
    vectors, squares, square_in,
    c_send, c_recv, d_send, dx_recv, dy_recv, x_send, x_recv, y_send, y_recv, up_send, low_recv, high_recv, final_recv, down_send,
    keep_sem, load_sem, small_send, small_recv,
):
    z, s = lax.axis_index("grp"), lax.axis_index("shard")
    per = product.shape[0]
    images = GROUPS * SHARDS
    chunks = cap // ch
    x_at, y_at, c_at = (z, s ^ 2), (z, s ^ 4), (z, s ^ 1)
    far_z = [(lax.rem(z + i, GROUPS), s) for i in range(1, GROUPS)]
    near_s = [(z, s ^ i) for i in range(1, SHARDS)]
    half = BLK // 2
    upper, lower = pl.ds(0, half), pl.ds(half, half)

    barrier = pltpu.get_barrier_semaphore()
    for peer in far_z + near_s:
        pl.semaphore_signal(barrier, inc=1, device_id=peer, device_id_type=MESH_ID)

    def remote(src, dst, sent, received, peer):
        return pltpu.make_async_remote_copy(
            src_ref=src, dst_ref=dst, send_sem=sent, recv_sem=received, device_id=peer, device_id_type=MESH_ID
        )

    def block_rows(index, count):
        return pl.ds(pl.multiple_of(index * count, count), count)

    def far(stage, src, dst):
        return [
            remote(src, dst, small_send.at[stage * 3 + i], small_recv.at[stage * 3 + i], peer) for i, peer in enumerate(far_z)
        ]

    def group(stage, src_of, dst):
        first = 9 + stage * 7
        return [
            remote(src_of(peer[1]), dst, small_send.at[first + i], small_recv.at[first + i], peer)
            for i, peer in enumerate(near_s)
        ]

    def direct(stage, ref):
        first = 9 + stage * 7
        return [
            remote(ref, ref, small_send.at[first + i], small_recv.at[first + i], peer)
            for i, peer in enumerate((x_at, y_at, (z, s ^ 6), c_at))
        ]

    def passed(stage, ref_of):
        first = 9 + stage * 7 + 4
        return [
            remote(ref_of(o), ref_of(o), small_send.at[first + i], small_recv.at[first + i], c_at)
            for i, o in enumerate((s ^ 2, s ^ 4, s ^ 6))
        ]

    own_d = all_d.at[block_rows(s * GROUPS + z, 8 * LANES)]
    own_stat = all_stats.at[block_rows(s * GROUPS + z, 8)]
    group_d = all_d.at[block_rows(s, 8 * LANES * GROUPS)]
    group_stat = all_stats.at[block_rows(s, 8 * GROUPS)]

    def small_copies(name):
        if name == "d_far":
            return far(0, own_d, own_d)
        if name == "stat_far":
            return far(1, own_stat, own_stat)
        if name == "tok_far":
            return far(2, tok_z.at[z], tok_z.at[z])
        if name == "tok":
            return group(0, lambda p: tok_out.at[p], tok_in.at[s])
        if name == "d":
            return direct(1, group_d)
        if name == "stat":
            return direct(2, group_stat)
        if name == "d_more":
            return passed(1, lambda o: all_d.at[block_rows(o, 8 * LANES * GROUPS)])
        if name == "stat_more":
            return passed(2, lambda o: all_stats.at[block_rows(o, 8 * GROUPS)])
        if name == "part":
            return group(3, lambda p: part_out.at[p], part_in.at[s])
        if name == "pre":
            return group(4, lambda p: pre_out.at[p], pre_in.at[s])
        return group(5, lambda p: square_in.at[s], square_in.at[s])

    def begin(*names):
        for name in names:
            for copy in small_copies(name):
                copy.start()

    def got(*names):
        for name in names:
            for copy in small_copies(name):
                copy.wait_recv()

    def load(part):
        count = tile.shape[0]
        return pltpu.make_async_copy(tiles_ref.at[pl.ds(part * count, count)], tile, load_sem)

    load(0).start()
    own_d[...] = dmod_ref[...].astype(bf16)
    own_stat[...] = stats_ref[...]
    tok_out[...] = ends_ref[...].astype(bf16)
    tok_in[s] = tok_out[s]
    squares[...] = jnp.zeros_like(squares)
    pl.semaphore_wait(barrier, len(far_z) + len(near_s))
    begin("d_far", "stat_far", "tok")

    def spread_stage():
        got("d_far", "stat_far")
        begin("d", "stat")
        got("tok")
        value = tok_in[0].astype(f32)
        for o in range(1, SHARDS):
            value += tok_in[o].astype(f32)
        tok_z[z] = value
        begin("tok_far")

    def pass_stage():
        got("d", "stat")
        begin("d_more", "stat_more")

    def order_stage():
        got("d_more", "stat_more", "tok_far")
        value = tok_z[0]
        for i in range(1, GROUPS):
            value += tok_z[i]
        tokens[...] = value
        value = all_stats[pl.ds(0, 8), :]
        for i in range(1, images):
            value += all_stats[pl.ds(8 * i, 8), :]
        stat_ref[...] = value

        def widen(i, unused):
            place = block_rows(i, 8 * LANES)
            wide_d[place, :] = all_d[place, :].astype(f32)
            return unused

        lax.fori_loop(0, images, widen, 0)
        for q in range(6 * LANES):
            d_blocks_ref[q // 2, :, (q % 2) * 128 : (q % 2 + 1) * 128] = wide_d[
                pl.ds(q, images, stride=8 * LANES), :
            ].astype(bf16)

    def own_columns(i):
        return wide_d[pl.ds(i * LANES + s, images, stride=8 * LANES), :]

    def ada_stage(part):
        count = tile.shape[0]
        load(part).wait()

        def one(j, unused):
            at = part * count + j
            product[at] = nt(d_blocks_ref[jnp.maximum(col_ref[at], 0)], tile[j].astype(bf16))
            return unused

        lax.fori_loop(0, count, one, 0)

        @pl.when(part < ADA_PARTS - 1)
        def _():
            load(part + 1).start()

    def row_slice(start, count):
        return rows_ref[start : start + count, :].astype(bf16)

    final_at = NCLASS + FREQ + D

    def part_stage():
        def add(j, values):
            chosen = [jnp.logical_and(col_ref[j] >= 0, row_ref[j] == r) for r in range(NB)]
            return tuple(value + jnp.where(one, 1.0, 0.0) * product[j] for one, value in zip(chosen, values))

        values = []
        for r in range(NB):
            value = jnp.zeros((images, BLK), f32)
            for i in range(2):
                value += nt(own_columns(6 + i).astype(bf16), row_slice(final_at + i * D + r * BLK, BLK))
            values.append(value)
        values = lax.fori_loop(0, per, add, tuple(values))
        for r in range(NB):
            for i in range(2):
                part_out[2 * r + i] = values[r][:, i * 128 : (i + 1) * 128].astype(bf16)
        part_in[s] = part_out[s]
        begin("part")

    def slope(value):
        gate = jax.nn.sigmoid(value)
        return gate * (1.0 + value * (1.0 - gate))

    def cond_stage():
        got("part")
        value = part_in[0].astype(f32)
        for o in range(1, SHARDS):
            value += part_in[o].astype(f32)
        value = value * slope(own_cond_ref[...])
        own_dcond[...] = value
        for o in range(SHARDS):
            pre_out[o] = nt(value.astype(bf16), row_slice(NCLASS + FREQ + o * 128, 128)).astype(bf16)
        pre_in[s] = pre_out[s]
        begin("pre")

    def row_stage():
        got("pre")
        value = pre_in[0].astype(f32)
        for o in range(1, SHARDS):
            value += pre_in[o].astype(f32)
        value = value * slope(pre_ref[...])
        own_dpre[...] = value
        dpre_low, dcond = value.astype(bf16), own_dcond[...]
        dcond_low = dcond.astype(bf16)
        gathered = []

        def keep(start, value):
            own_rows_ref[start : start + value.shape[0], :] = value
            gathered.append(fold(value * value))

        hot = label_ref[...].astype(jnp.int32)[:, :1] == lax.broadcasted_iota(jnp.int32, (images, NCLASS), 1)
        keep(
            0,
            lax.dot_general(
                hot.astype(f32), dcond, (((0,), (0,)), ((), ())), preferred_element_type=f32, precision=lax.Precision.HIGHEST
            ),
        )
        keep(NCLASS, tn(freq_ref[...], dpre_low))
        for o in range(SHARDS):
            keep(NCLASS + FREQ + o * 128, tn(time_ref[o], dcond_low))
            for i in range(2):
                keep(final_at + i * D + o * 128, tn(cond_ref[o], own_columns(6 + i).astype(bf16)))
        keep(NEAR_START, tokens[: 2 * PATCH_DIM, :])

        vectors[...] = jnp.zeros_like(vectors)

        def vector(row, value):
            vectors[row : row + 1, :] = value

        vector(0, tokens[T_PATCH : T_PATCH + 1, :])
        vector(1, jnp.sum(value, axis=0, keepdims=True))
        vector(2, jnp.sum(dcond, axis=0, keepdims=True))
        vector(3, tokens[T_QUERY : T_QUERY + 1, :])
        vector(4, tokens[T_VALUE : T_VALUE + 1, :])
        vector(5, tokens[T_OUT : T_OUT + 1, :])
        vector(6, tokens[T_DOWN : T_DOWN + 1, :])
        for i in range(8):
            vector(7 + i if i < 6 else 7 + i + FF // D, jnp.sum(own_columns(i), axis=0, keepdims=True))
        for i in range(FF // D):
            vector(13 + i, tokens[T_UP + i : T_UP + i + 1, :])
        start = NEAR_START + 2 * PATCH_DIM
        rest = own_rows_ref.shape[0] - start
        whole = rest // 8 * 8
        own_rows_ref[start : start + whole, :] = vectors[:whole, :]
        own_rows_ref[start + whole : start + rest, :] = vectors[whole:rest, :]
        value = fold(vectors[...] * vectors[...])
        for piece in gathered:
            value += piece
        squares[:, :128] = squares[:, :128] + value

    def slot_of(i):
        return lax.rem(i + 2 * RING, RING)

    def block(owner, p):
        at = owner * per + p
        return nn(acts_ref[left_ref[at]], acts_ref[right_ref[at]])

    targets = (s ^ 6, s ^ 2, s ^ 4, s)

    def c_copy(slot, item):
        return remote(out_c.at[slot, item], in_c.at[slot, item], c_send.at[slot, item], c_recv.at[slot, item], c_at)

    def dx_copy(slot):
        return remote(out_d.at[slot, :, upper], in_dx.at[slot], d_send.at[slot, 0], dx_recv.at[slot], x_at)

    def dy_copy(slot):
        return remote(out_d.at[slot, :, lower], in_dy.at[slot], d_send.at[slot, 1], dy_recv.at[slot], y_at)

    def x_copy(slot):
        return remote(out_x.at[slot], in_x.at[slot], x_send.at[slot], x_recv.at[slot], x_at)

    def y_copy(slot):
        return remote(out_y.at[slot], in_y.at[slot], y_send.at[slot], y_recv.at[slot], y_at)

    def inside(i):
        return jnp.logical_and(i >= 0, i < chunks)

    def each(body):
        if ch == 1:
            body(0)
            return

        def one(c, unused):
            body(c)
            return unused

        lax.fori_loop(0, ch, one, 0)

    def for_sibling(n):
        slot = slot_of(n)
        for items, at in (((0,), n + 1), ((1, 2, 3), n)):

            @pl.when(inside(at))
            def _():
                for item in items:
                    each(lambda c: out_c.__setitem__((slot, item, c), block(targets[item] ^ 1, at * ch + c).astype(bf16)))
                for item in items:
                    c_copy(slot, item).start()

    def for_owners(i):
        slot, before = slot_of(i), slot_of(i - 1)

        @pl.when(inside(i + 1))
        def _():
            c_copy(slot, 0).wait_recv()

            def one(c):
                value = block(targets[0], (i + 1) * ch + c) + in_c[slot, 0, c].astype(f32)
                out_d[slot, c] = value.astype(bf16)

            each(one)
            dx_copy(slot).start()
            dy_copy(slot).start()

        @pl.when(inside(i))
        def _():
            for item in (1, 2, 3):
                c_copy(slot, item).wait_recv()
            dy_copy(before).wait_recv()
            dx_copy(before).wait_recv()

            def one(c):
                value = block(targets[1], i * ch + c) + in_c[slot, 1, c].astype(f32)
                out_x[slot, c, upper] = value[:half].astype(bf16)
                out_x[slot, c, lower] = (value[half:] + in_dy[before, c].astype(f32)).astype(bf16)

            def two(c):
                value = block(targets[2], i * ch + c) + in_c[slot, 2, c].astype(f32)
                out_y[slot, c, upper] = (value[:half] + in_dx[before, c].astype(f32)).astype(bf16)
                out_y[slot, c, lower] = value[half:].astype(bf16)

            def three(c):
                value = block(targets[3], i * ch + c) + in_c[slot, 3, c].astype(f32)
                total[i * ch + c] = value.astype(bf16)

            each(one)
            each(two)
            x_copy(slot).start()
            y_copy(slot).start()
            each(three)

        old = slot_of(i - SUM_LAG)

        @pl.when(inside(i - SUM_LAG))
        def _():
            x_copy(old).wait_recv()
            y_copy(old).wait_recv()

            def one(c):
                at = (i - SUM_LAG) * ch + c
                value = total[at].astype(f32) + in_x[old, c].astype(f32) + in_y[old, c].astype(f32)
                total[at] = value.astype(bf16)

            each(one)

    def along(j):
        even = lax.rem(j, 2) == 0
        rank = jnp.where(even, z, GROUPS - 1 - z)
        down = jnp.where(even, lax.rem(z + GROUPS - 1, GROUPS), lax.rem(z + 1, GROUPS))
        up = jnp.where(even, lax.rem(z + 1, GROUPS), lax.rem(z + GROUPS - 1, GROUPS))
        return rank, (down, s), (up, s)

    def z_copy(name, j):
        _, down, up = along(j)
        span = pl.ds(j * ch, ch)
        if name == "rise":
            return remote(total.at[span], low_in.at[span], up_send.at[j], low_recv.at[j], up)
        if name == "sink":
            return remote(total.at[span], high_in.at[span], up_send.at[j], high_recv.at[j], down)
        if name == "final_down":
            return remote(final.at[span], final.at[span], down_send.at[0, j], final_recv.at[j], down)
        return remote(final.at[span], final.at[span], down_send.at[1, j], final_recv.at[j], up)

    def over_z(i):
        j = i - SUM_LAG

        @pl.when(inside(j))
        def _():
            rank, _, _ = along(j)

            @pl.when(rank == 0)
            def _():
                z_copy("rise", j).start()

            @pl.when(rank == 3)
            def _():
                z_copy("sink", j).start()

        j2 = j - Z_STEP

        @pl.when(jnp.logical_and(inside(j2), along(j2)[0] == 2))
        def _():
            z_copy("sink", j2).wait_recv()

            def one(c):
                at = j2 * ch + c
                total[at] = (total[at].astype(f32) + high_in[at].astype(f32)).astype(bf16)

            each(one)
            z_copy("sink", j2).start()

        j3 = j - 2 * Z_STEP

        @pl.when(jnp.logical_and(inside(j3), along(j3)[0] == 1))
        def _():
            z_copy("rise", j3).wait_recv()
            z_copy("sink", j3).wait_recv()

            def one(c):
                at = j3 * ch + c
                value = total[at].astype(f32) + low_in[at].astype(f32) + high_in[at].astype(f32)
                final[at] = value.astype(bf16)

            each(one)
            z_copy("final_down", j3).start()
            z_copy("final_up", j3).start()

        j4 = j - 3 * Z_STEP

        @pl.when(jnp.logical_and(inside(j4), along(j4)[0] == 2))
        def _():
            z_copy("final_up", j4).wait_recv()
            z_copy("final_up", j4).start()

        j5 = i - Z_LAG

        @pl.when(inside(j5))
        def _():
            rank = along(j5)[0]

            @pl.when(jnp.logical_or(rank == 0, rank == 3))
            def _():
                z_copy("final_up", j5).wait_recv()

            span = pl.ds(j5 * ch, ch)
            pltpu.make_async_copy(final.at[span], grads_ref.at[span], keep_sem.at[j5]).start()

            def one(c):
                at = j5 * ch + c
                value = final[at].astype(f32) * jnp.where(at < count_ref[0], 1.0, 0.0)
                squares[...] = squares[...] + fold(value * value)

            each(one)

    def settle(i):
        n = i - 2
        slot = slot_of(n)
        for item in range(4):

            @pl.when(inside(n + 1 if item == 0 else n))
            def _():
                c_copy(slot, item).wait_send()

        n2 = i - 3
        slot2 = slot_of(n2)

        @pl.when(inside(n2 + 1))
        def _():
            dx_copy(slot2).wait_send()
            dy_copy(slot2).wait_send()

        @pl.when(inside(n2))
        def _():
            x_copy(slot2).wait_send()
            y_copy(slot2).wait_send()

    hooks = {
        0: spread_stage, 3: pass_stage, 6: order_stage, 13: part_stage, 17: cond_stage, 21: row_stage,
    }

    for_sibling(-1)

    def iteration(step, unused):
        i = step - 1
        for_sibling(i + 1)
        for_owners(i)
        over_z(i)
        settle(i)
        pl.when(jnp.logical_and(i >= 7, i < 7 + ADA_PARTS))(lambda: ada_stage(i - 7))
        for at, stage in hooks.items():
            pl.when(i == at)(stage)
        return unused

    lax.fori_loop(0, chunks + 1 + Z_LAG, iteration, 0)

    square_in[s] = jnp.zeros((8, 128), f32) + jnp.sum(squares[...])
    begin("square")

    cond_gram = jnp.zeros((images, images), f32)
    for o in range(SHARDS):
        cond_gram += nt(cond_ref[o], cond_ref[o])

    def gram(c, value):
        return value + nt(d_blocks_ref[c], d_blocks_ref[c])

    d_gram = lax.fori_loop(0, 6 * NB, gram, jnp.zeros((images, images), f32))
    got("square")
    value = square_in[0]
    for o in range(1, SHARDS):
        value += square_in[o]
    norm_ref[...] = value + jnp.sum(cond_gram * d_gram)

    def finish(j, unused):
        span = pl.ds(j * ch, ch)
        pltpu.make_async_copy(final.at[span], grads_ref.at[span], keep_sem.at[j]).wait()
        rank = along(j)[0]

        @pl.when(rank == 0)
        def _():
            z_copy("rise", j).wait_send()

        @pl.when(rank >= 2)
        def _():
            z_copy("sink", j).wait_send()

        @pl.when(rank == 1)
        def _():
            z_copy("final_down", j).wait_send()

        @pl.when(jnp.logical_or(rank == 1, rank == 2))
        def _():
            z_copy("final_up", j).wait_send()

        return unused

    lax.fori_loop(0, chunks, finish, 0)
    for name in ("d_far", "stat_far", "tok_far", "tok", "d", "stat", "d_more", "stat_more", "part", "pre", "square"):
        for copy in small_copies(name):
            copy.wait_send()


def collect(cap, left_of, right_of, row_of, col_of, count, acts, dmod, ends, stats, times, conds, freq_low, label, own_pre, own_cond,
            row_master, tile_master):
    per = tile_master.shape[0]
    ch = 1
    chunks = cap // ch
    images = GROUPS * SHARDS
    vmem = pl.BlockSpec(memory_space=pltpu.VMEM)
    smem = pl.BlockSpec(memory_space=pltpu.SMEM)
    anywhere = pl.BlockSpec(memory_space=pl.ANY)
    small = 9 + 6 * (SHARDS - 1)
    dma = pltpu.SemaphoreType.DMA

    def blocks(*lead):
        return pltpu.VMEM(lead + (BLK, BLK), bf16)

    return pl.pallas_call(
        functools.partial(collect_body, cap, ch),
        out_shape=[
            jax.ShapeDtypeStruct((per, BLK, BLK), bf16),
            jax.ShapeDtypeStruct((6 * NB, images, BLK), bf16),
            jax.ShapeDtypeStruct(row_master.shape, f32),
            jax.ShapeDtypeStruct((8, 128), f32),
            jax.ShapeDtypeStruct((8, 128), f32),
        ],
        in_specs=[smem] * 5 + [vmem] * 11 + [anywhere],
        out_specs=[anywhere] + [vmem] * 4,
        scratch_shapes=[
            blocks(RING, 4, ch),
            blocks(RING, 4, ch),
            blocks(RING, ch),
            blocks(RING, ch),
            blocks(RING, ch),
            pltpu.VMEM((RING, ch, BLK // 2, BLK), bf16),
            pltpu.VMEM((RING, ch, BLK // 2, BLK), bf16),
            blocks(RING, ch),
            blocks(RING, ch),
            blocks(cap),
            blocks(cap),
            blocks(cap),
            blocks(cap),
            pltpu.VMEM((per // ADA_PARTS, BLK, BLK), f32),
            pltpu.VMEM((per, images, BLK), f32),
            pltpu.VMEM((images * 8 * LANES, 128), bf16),
            pltpu.VMEM((images * 8 * LANES, 128), f32),
            pltpu.VMEM((images * 8, 128), f32),
            pltpu.VMEM((SHARDS, TOKEN_ROWS, 128), bf16),
            pltpu.VMEM((SHARDS, TOKEN_ROWS, 128), bf16),
            pltpu.VMEM((GROUPS, TOKEN_ROWS, 128), f32),
            pltpu.VMEM((TOKEN_ROWS, 128), f32),
            pltpu.VMEM((SHARDS, images, 128), bf16),
            pltpu.VMEM((SHARDS, images, 128), bf16),
            pltpu.VMEM((SHARDS, images, 128), bf16),
            pltpu.VMEM((SHARDS, images, 128), bf16),
            pltpu.VMEM((images, 128), f32),
            pltpu.VMEM((images, 128), f32),
            pltpu.VMEM((24, 128), f32),
            pltpu.VMEM((8, BLK), f32),
            pltpu.VMEM((SHARDS, 8, 128), f32),
            dma((RING, 4)),
            dma((RING, 4)),
            dma((RING, 2)),
            dma((RING,)),
            dma((RING,)),
            dma((RING,)),
            dma((RING,)),
            dma((RING,)),
            dma((RING,)),
            dma((chunks,)),
            dma((chunks,)),
            dma((chunks,)),
            dma((chunks,)),
            dma((2, chunks)),
            dma((chunks,)),
            dma,
            dma((small,)),
            dma((small,)),
        ],
        compiler_params=pltpu.CompilerParams(
            collective_id=100 + cap, has_side_effects=True, vmem_limit_bytes=50 << 20
        ),
        name="collect",
    )(left_of, right_of, row_of, col_of, count, acts, dmod, ends, stats, times, conds, freq_low, label, own_pre, own_cond,
      row_master, tile_master)


def position_table(grid_side, model_width):
    quarter = model_width // 4
    omega = 1.0 / 10000.0 ** (jnp.arange(quarter, dtype=f32) / quarter)
    angle = jnp.arange(grid_side).astype(f32)[:, None] * omega[None, :]
    return jnp.stack([jnp.sin(angle), jnp.cos(angle)])


def time_freq(step_values, freq_width):
    half_width = freq_width // 2
    freqs = jnp.exp(-math.log(10000.0) * jnp.arange(half_width, dtype=f32) / half_width)
    angle_arg = step_values.astype(f32)[:, None] * freqs[None, :]
    return jnp.concatenate([jnp.cos(angle_arg), jnp.sin(angle_arg)], axis=1)


def silu_slope(value):
    gate = jax.nn.sigmoid(value)
    return gate * (1.0 + value * (1.0 - gate))


def blocked(array):
    count = array.shape[0]
    return array.reshape(count, -1, BLK).transpose(1, 0, 2)


def factors_of(block):
    n = jnp.maximum(block - ADA, 0)
    out, up, down = n - AT_OUT, n - AT_UP, n - AT_DOWN
    row = lax.div(n, jnp.int32(QB))
    left = jnp.where(n < AT_OUT, L_ATT + row, jnp.where(n < AT_UP, L_OUT + (out >> 2), jnp.where(n < AT_DOWN, L_MLP + (up >> 4), L_HID + (down >> 2))))
    right = jnp.where(
        n < AT_OUT,
        R_QKV + n - row * QB,
        jnp.where(n < AT_UP, R_OUT + (out & (NB - 1)), jnp.where(n < AT_DOWN, R_UP + (up & (HB - 1)), R_DOWN + (down & (NB - 1)))),
    )
    return left, right


def places_body(
    per, assign_ref, left_table, right_table, slot_ref, row_ref, col_ref, rank_ref, inverse_ref, left_ref, right_ref, count_ref, tier_ref
):
    me = lax.axis_index("shard")

    def place_in(block, s, before):
        return jnp.where(block < ADA, per - 1 - (s - before), before), before + jnp.where(block < ADA, 0, 1)

    def owner(o, most):
        def slot(s, before):
            block = assign_ref[o * per + s]
            p, after = place_in(block, s, before)
            place = o * per + p
            inverse_ref[block] = place
            left_ref[place] = left_table[block]
            right_ref[place] = right_table[block]
            return after

        return jnp.maximum(most, lax.fori_loop(0, per, slot, jnp.int32(0), unroll=True))

    most = lax.fori_loop(0, assign_ref.shape[0] // per, owner, jnp.int32(0))
    tier_ref[0] = sum(jnp.where(most > cap, 1, 0) for cap in CAPS)

    def own(s, before):
        block = assign_ref[me * per + s]
        p, after = place_in(block, s, before)
        slot_ref[p] = s
        rank_ref[s] = p
        row_ref[s] = jnp.where(block < ADA, block // (6 * NB), 0)
        col_ref[s] = jnp.where(block < ADA, block % (6 * NB), -1)
        return after

    count_ref[0] = lax.fori_loop(0, per, own, jnp.int32(0), unroll=True)


def find_places(assign, per):
    smem = pl.BlockSpec(memory_space=pltpu.SMEM)

    def ints(count):
        return jax.ShapeDtypeStruct((count,), jnp.int32)

    total = assign.shape[0]
    return pl.pallas_call(
        functools.partial(places_body, per),
        out_shape=[ints(per)] * 4 + [ints(total)] * 3 + [ints(1)] * 2,
        in_specs=[smem] * 3,
        out_specs=[smem] * 9,
        name="find_places",
    )(assign, *factors_of(jnp.arange(total, dtype=jnp.int32)))


def spread_plain(slot_of, row_of, col_of, tile_master, row_master, timesteps, labels):
    shard_count = lax.axis_size("shard")
    everyone = ("grp", "shard")
    me = lax.axis_index("shard")
    per, columns = tile_master.shape[0], row_master.shape[1]
    low_rows = row_master.astype(bf16)
    at = [0]

    def take(count):
        at[0] += count
        return low_rows[at[0] - count : at[0]]

    table, w_time1, w_time2 = take(NCLASS), take(FREQ), take(D)
    w_final = (take(D), take(D))
    take(2 * PATCH_DIM)
    take(1)
    b_time1, b_time2 = take(1), take(1)
    take(4)
    b_ada = take(6)
    take(FF // D)
    b_final = take(2)
    b_mod = jnp.concatenate([b_ada, b_final], axis=0)

    packed = pack_tiles(slot_of, tile_master)
    gathered = lax.all_gather(packed, "shard", axis=0, tiled=True)
    near = lax.all_gather(low_rows[NEAR_START:], "shard", axis=1, tiled=True)
    near = jnp.pad(near, ((0, NEAR - NEAR_REAL), (0, 0))).reshape(NEAR, LANES, 128).transpose(1, 0, 2)

    ids = lax.all_gather(jnp.concatenate([timesteps, labels]), everyone, axis=0)
    all_steps, all_labels = ids[:, 0], ids[:, 1]
    freq_low = time_freq(all_steps, FREQ).astype(bf16)
    own_pre = nn(freq_low, w_time1) + b_time1
    time_low = lax.all_gather(jax.nn.silu(own_pre).astype(bf16), "shard", axis=1, tiled=True)
    one_hot = (all_labels[:, None] == jnp.arange(NCLASS, dtype=jnp.int32)[None, :]).astype(bf16)
    own_cond = nn(time_low, w_time2) + b_time2 + nn(one_hot, table)
    cond_low = lax.all_gather(jax.nn.silu(own_cond).astype(bf16), "shard", axis=1, tiled=True)
    group_cond = lax.dynamic_slice(cond_low, (lax.axis_index("grp") * shard_count, 0), (shard_count, D))
    part_mod = ada_front(row_of, col_of, blocked(group_cond), tile_master)
    part_mod = part_mod.transpose(1, 0, 2).reshape(shard_count, 6, D)
    part_final = jnp.stack([nn(group_cond, w_final[0]), nn(group_cond, w_final[1])], axis=1)
    spread = jnp.zeros((shard_count, 8, D), f32)
    spread = lax.dynamic_update_slice(
        spread,
        jnp.concatenate([jnp.zeros((shard_count, 6, columns), f32), part_final], axis=1) + b_mod[None].astype(f32),
        (0, 0, me * columns),
    )
    spread = spread + jnp.concatenate([part_mod, jnp.zeros((shard_count, 2, D), f32)], axis=1)
    mods = lax.psum_scatter(spread, "shard", scatter_dimension=0, tiled=True)[0]
    label = jnp.broadcast_to(all_labels.astype(f32)[:, None], (all_labels.shape[0], 128))

    def lanes(array):
        return array.reshape(-1, LANES, 128).transpose(1, 0, 2)

    return (
        gathered, near, mods.reshape(8 * LANES, 128), freq_low, label, lanes(time_low), lanes(cond_low), own_pre, own_cond,
    )


def collect_plain(left_of, right_of, row_of, col_of, count, acts, dmod, ends, stats, times, conds, freq_low, label, own_pre, own_cond,
                  row_master, tile_master):
    everyone = ("grp", "shard")
    me = lax.axis_index("shard")
    columns = row_master.shape[1]
    low_rows = row_master.astype(bf16)
    w_time2 = low_rows[NCLASS + FREQ : NCLASS + FREQ + D]
    w_final = [low_rows[NCLASS + FREQ + (1 + i) * D : NCLASS + FREQ + (2 + i) * D] for i in range(2)]
    one_hot = (label[:, :1].astype(jnp.int32) == jnp.arange(NCLASS, dtype=jnp.int32)[None, :]).astype(bf16)
    time_low, cond_low = (array.transpose(1, 0, 2).reshape(-1, D) for array in (times, conds))
    partial = tile_grads(left_of, right_of, acts)
    own_tiles = lax.psum_scatter(partial, "shard", scatter_dimension=0, tiled=True)
    own_tiles = lax.psum(own_tiles, "grp")

    all_dmod = lax.all_gather(dmod.reshape(1, -1).astype(bf16), everyone, axis=0, tiled=True)
    dmod_blocks = blocked(all_dmod[:, : 6 * D])
    own_dmod = lax.dynamic_slice(all_dmod.reshape(-1, 8, D), (0, 0, me * columns), (all_dmod.shape[0], 8, columns))
    part_cond = ada_back(row_of, col_of, dmod_blocks, tile_master).transpose(1, 0, 2).reshape(-1, D)
    part_cond = part_cond + nt(own_dmod[:, 6], w_final[0]) + nt(own_dmod[:, 7], w_final[1])
    own_dcond = lax.psum_scatter(part_cond, "shard", scatter_dimension=1, tiled=True) * silu_slope(own_cond)
    dcond_low = own_dcond.astype(bf16)
    own_dpre = lax.psum_scatter(nt(dcond_low, w_time2), "shard", scatter_dimension=1, tiled=True)
    own_dpre = own_dpre * silu_slope(own_pre)
    wide_dmod = own_dmod.astype(f32)

    token_rows = ends.transpose(1, 0, 2).reshape(TOKEN_ROWS, D)
    token_rows = lax.psum_scatter(token_rows, "shard", scatter_dimension=1, tiled=True)
    token_rows = lax.psum(token_rows, "grp")
    own_rows = jnp.concatenate(
        [
            tn(one_hot.astype(f32), own_dcond),
            tn(freq_low, own_dpre.astype(bf16)),
            tn(time_low, dcond_low),
            tn(cond_low, own_dmod[:, 6]),
            tn(cond_low, own_dmod[:, 7]),
            token_rows[: T_PATCH + 1],
            jnp.sum(own_dpre, axis=0)[None],
            jnp.sum(own_dcond, axis=0)[None],
            token_rows[T_QUERY : T_VALUE + 1],
            token_rows[T_OUT : T_DOWN + 1],
            jnp.sum(wide_dmod[:, :6], axis=0),
            token_rows[T_UP:T_END],
            jnp.sum(wide_dmod[:, 6:], axis=0),
        ],
        axis=0,
    )
    totals = lax.psum(stats, everyone)
    cond_gram = nt(cond_low, cond_low)
    dmod_gram = nt(all_dmod[:, : 6 * D], all_dmod[:, : 6 * D])
    counted = jnp.arange(own_tiles.shape[0], dtype=jnp.int32) < count
    wide_tiles = jnp.where(counted[:, None, None], own_tiles.astype(f32), 0.0)
    square_part = jnp.sum(wide_tiles * wide_tiles) + jnp.sum(own_rows * own_rows)
    square_sum = lax.psum(square_part, "shard") + jnp.sum(cond_gram * dmod_gram)
    return own_tiles, dmod_blocks, own_rows, jnp.broadcast_to(square_sum, (8, 128)), totals


def pack_body(slot_ref, tile_ref, out_ref):
    out_ref[...] = tile_ref[...].astype(bf16)


def pack_tiles(slot_of, tile_master):
    per = tile_master.shape[0]
    return pl.pallas_call(
        pack_body,
        grid_spec=pltpu.PrefetchScalarGridSpec(
            num_scalar_prefetch=1,
            grid=(per,),
            in_specs=[pl.BlockSpec((1, BLK, BLK), lambda p, slots: (slots[p], 0, 0))],
            out_specs=pl.BlockSpec((1, BLK, BLK), lambda p, slots: (p, 0, 0)),
        ),
        out_shape=jax.ShapeDtypeStruct(tile_master.shape, bf16),
        name="pack_tiles",
    )(slot_of, tile_master)


def shards(
    patches, noise, timesteps, labels, assign, tile_master, tile_bases, tile_moment, tile_second,
    row_master, row_moment, row_second,
):
    group_count, shard_count = lax.axis_size("grp"), lax.axis_size("shard")
    everyone = ("grp", "shard")
    me = lax.axis_index("shard")
    per = tile_master.shape[0]
    columns = row_master.shape[1]
    token_total = patches.shape[0] * group_count * shard_count
    tile_total = assign.shape[0]

    slot_of, row_of, col_of, rank, inverse, left_of, right_of, count, tier = find_places(assign, per)
    fast = group_count == GROUPS and shard_count == SHARDS
    if fast:
        tier = tier[0]
        gathered, bases, near, mods, freq_low, label, times, conds, own_pre, own_cond = lax.switch(
            tier, [functools.partial(spread, cap) for cap in CAPS + (per,)], slot_of, row_of, col_of, timesteps, labels,
            tile_master, tile_bases, row_master,
        )
        gathered = gathered.reshape(tile_total, BLK, BLK)
    else:
        bases = tile_bases
        gathered, near, mods, freq_low, label, times, conds, own_pre, own_cond = spread_plain(
            slot_of, row_of, col_of, tile_master, row_master, timesteps, labels
        )

    loss_scale = 1.0 / (token_total * PATCH_DIM)
    acts, dmod, ends, stats = block_step(
        inverse, gathered, patches.T, noise.T, position_table(LAT // PATCH_SIDE, D), near, mods.reshape(8 * LANES, 128),
        2.0 * loss_scale,
    )

    if fast:
        own_tiles, dmod_blocks, own_rows, squares, totals = lax.switch(
            tier, [functools.partial(collect, cap) for cap in CAPS + (per,)], left_of, right_of, row_of, col_of, count, acts, dmod, ends, stats, times, conds, freq_low, label, own_pre,
            own_cond, row_master, tile_master,
        )
    else:
        own_tiles, dmod_blocks, own_rows, squares, totals = collect_plain(
            left_of, right_of, row_of, col_of, count, acts, dmod, ends, stats, times, conds, freq_low, label, own_pre,
            own_cond, row_master, tile_master,
        )
    new_tile_moment, new_tile_second, tile_update, new_row_moment, new_row_second, row_update, loss, grad_norm, act_rms = adam(
        (1.0 / (token_total * PATCH_DIM), 1.0 / (token_total * D)), rank, row_of, col_of, squares, totals, own_tiles, conds,
        dmod_blocks, bases, tile_moment, tile_second, own_rows, row_master, row_moment, row_second,
    )
    loss, grad_norm = loss.reshape(()), grad_norm.reshape(())
    return (
        loss, grad_norm, act_rms, new_tile_moment, new_tile_second, tile_update, new_row_moment, new_row_second, row_update,
    )


def solution(mesh):
    placed = (
        P(("grp", "shard"), None),
        P(("grp", "shard"), None),
        P(("grp", "shard")),
        P(("grp", "shard")),
        P(),
        P("shard", None, None),
        P("shard", None, None, None),
        P("shard", None, None),
        P("shard", None, None),
        P(None, "shard"),
        P(None, "shard"),
        P(None, "shard"),
    )
    return jax.shard_map(
        shards,
        mesh=mesh,
        in_specs=placed,
        out_specs=(
            P(), P(), P(),
            P("shard", None, None), P("shard", None, None), P("shard", None, None),
            P(None, "shard"), P(None, "shard"), P(None, "shard"),
        ),
        check_vma=False,
    )
```
